128 devices in a mesh: dom: 8 (over z, y_lo), band: 16 (over x, y_hi, core).
Axes of the slice: x: 4, y: 4 (y_hi: 2, y_lo: 2; y = y_hi * 2 + y_lo), z: 4, core: 2. Of those that a mesh axis runs over, the one named last changes fastest.
Arguments:
- states: float32 [1024, 147456], P('band', 'dom'), may hold values from -25 to 25
- cell_matrix: bfloat16 [343, 343], replicated, may hold values from -0.12 to 2, as said below
- potential: float32 [147456], P('dom'), may hold values from 0.2 to 2
- weights: float32 [147456], P('dom'), may hold values from 2.7126737e-06 to 2.7126736e-05
- connectivity: int32 [343, 1024], P(None, 'dom'), may hold values from 0 to 19967, as said below
- face_nodes: int32 [12288], P('dom'), may hold values from 0 to 18431, as said below
- cell_counts: int32 [8], P('dom'), may hold values from 32 to 128
Outputs:
- filtered: float32 [1024, 147456], P('band', 'dom')
- state_gram: float32 [1024, 1024], P('band')
The draws below stay inside these ranges and needn't reach their ends.
Inputs may be any that keep to these rules, and one draw needn't show every extreme that they name: `cell_matrix`: symmetric. `connectivity`: numbers from 18432 on name the shared nodes of the next partition. `face_nodes`: the 1536 numbers of one partition are distinct.
All inputs are finite; a program needn't handle non-finite values.
Results may differ from the reference program's by a relative error of at most 0.003.
Values may be sent and summed in bfloat16 or wider, within the bound.
No kernel may reach another device: no remote copies, remote signals or barrier semaphores. Data moves between devices by JAX's collectives and lax.ppermute only.
A program may use at most 192 MiB of HBM per device.

```python
import math
import jax
import jax.numpy as jnp
from jax import lax

CELL_NODES = 343
BLOCK = 64
NODES_DEV = 18432
CELLS = 128
FACE = 1536
PARTITIONS = 8
NODES = 147456
CELLS_ALL = 1024
STATES = 1024


def draw_states(key, part):
    key = jax.random.fold_in(key, 11)
    keys = jax.random.split(key, 4)
    scale_rows = jnp.exp(jax.random.uniform(keys[0], (STATES, 1), jnp.float32, -1.15, 1.15))
    shared_weight = jnp.clip(jax.random.normal(keys[1], (STATES, 1), jnp.float32), -2.0, 2.0)
    common = jnp.clip(jax.random.normal(keys[2], (1, NODES), jnp.float32), -3.0, 3.0)
    noise = jnp.clip(jax.random.normal(keys[3], (STATES, NODES), jnp.float32), -3.0, 3.0)
    return scale_rows * (0.8 * shared_weight * common + noise)


def draw_cell_matrix(key, part):
    key = jax.random.fold_in(key, 12)
    keys = jax.random.split(key, 2)
    raw = jnp.clip(0.02 * jax.random.normal(keys[0], (CELL_NODES, CELL_NODES), jnp.float32), -0.08, 0.08)
    symmetric = (raw + raw.T) * 0.7071
    diagonal = jax.random.uniform(keys[1], (CELL_NODES,), jnp.float32, 1.0, 2.0)
    identity = jnp.eye(CELL_NODES, dtype=jnp.float32)
    return (symmetric * (1.0 - identity) + identity * diagonal[None, :]).astype(jnp.bfloat16)


def draw_connectivity(key, part):
    key = jax.random.fold_in(key, 13)
    top_value = NODES_DEV + FACE
    raw = jax.random.randint(key, (CELL_NODES, CELLS_ALL), 0, top_value)
    row_ids = jnp.arange(CELL_NODES)[:, None]
    col_ids = jnp.arange(CELLS_ALL)[None, :]
    raw = jnp.where((row_ids == 0) & (col_ids == 0), top_value - 1, raw)
    raw = jnp.where((row_ids == 1) & (col_ids == 0), 0, raw)
    return raw.astype(jnp.int32)


def draw_face_nodes(key, part):
    key = jax.random.fold_in(key, 14)
    keys = jax.random.split(key, PARTITIONS)

    def one_list(subkey):
        order = jax.random.permutation(subkey, NODES_DEV)
        order = jnp.where(order == NODES_DEV - 1, order[0], order).at[0].set(NODES_DEV - 1)
        order = jnp.where(order == 0, order[1], order).at[1].set(0)
        return order[:FACE]
    return jax.vmap(one_list)(keys).reshape(-1).astype(jnp.int32)


def draw_cell_counts(key, part):
    key = jax.random.fold_in(key, 15)
    keys = jax.random.split(key, 3)
    raw = jax.random.randint(keys[0], (PARTITIONS,), CELLS // 4, CELLS + 1)
    busiest = jax.random.randint(keys[1], (), 0, PARTITIONS)
    lightest = (busiest + 1 + jax.random.randint(keys[2], (), 0, PARTITIONS - 1)) % PARTITIONS
    position = jnp.arange(PARTITIONS)
    raw = jnp.where(position == busiest, CELLS, raw)
    raw = jnp.where(position == lightest, CELLS // 4, raw)
    return raw.astype(jnp.int32)


def shard_levels(own_key, extent, cuts, least, largest):
    factor_of, own = 1.0, jax.random.fold_in(own_key, 6)
    for dim, shards_of in cuts:
        draws = jnp.exp(jax.random.uniform(jax.random.fold_in(own, dim), (shards_of,), jnp.float32, least / len(cuts), largest / len(cuts)))
        factor_of = factor_of * jnp.repeat(draws, extent[dim] // shards_of).reshape([-1 if axis == dim else 1 for axis in range(len(extent))])
    return factor_of


def setup_inputs(seed: int = 0) -> dict:
    key_list = jax.random.split(jax.random.key(seed), 8)
    return {
        "states": draw_states(jax.random.fold_in(key_list[7], 71), 0),
        "cell_matrix": draw_cell_matrix(jax.random.fold_in(key_list[7], 71), 0),
        "potential": jnp.clip(jnp.exp(math.log(2.0) - 2.3025851 * jax.random.uniform(key_list[2], (NODES,), jnp.float32) ** shard_levels(key_list[2], (NODES,), ((0, 8),), -0.2, 0.2)), 0.2, 2.0),
        "weights": jnp.clip(jnp.exp(math.log(2.7126736313221045e-05) - 2.3025851 * jax.random.uniform(key_list[3], (NODES,), jnp.float32) ** shard_levels(key_list[3], (NODES,), ((0, 8),), -0.2, 0.2)), 2.7126736767968396e-06, 2.7126736313221045e-05),
        "connectivity": draw_connectivity(jax.random.fold_in(key_list[7], 71), 0),
        "face_nodes": draw_face_nodes(jax.random.fold_in(key_list[7], 71), 0),
        "cell_counts": draw_cell_counts(jax.random.fold_in(key_list[7], 71), 0),
    }


filter_centre = 6.0
filter_half = 4.0


def reference(states, cell_matrix, potential, weights, connectivity, face_nodes, cell_counts):
    node_total = NODES_DEV * PARTITIONS
    owner = (jnp.arange(CELLS_ALL) // CELLS).astype(jnp.int32)[None, :]
    following = owner + 1
    face_table = face_nodes.reshape(PARTITIONS, FACE)
    ghost_slot = jnp.clip(connectivity - NODES_DEV, 0, FACE - 1).astype(jnp.int32)
    following_row = jnp.minimum(following, PARTITIONS - 1).astype(jnp.int32)
    ghost_global = jnp.where(following < PARTITIONS, following * NODES_DEV + face_table[following_row, ghost_slot], node_total)
    node_index = jnp.where(connectivity < NODES_DEV, owner * NODES_DEV + connectivity, ghost_global).astype(jnp.int32)
    flat_index = node_index.reshape(-1)
    cell_live = (jnp.arange(CELLS)[None, :] < cell_counts[:, None]).reshape(-1).astype(jnp.float32)
    matrix_wide = cell_matrix.astype(jnp.float32)

    def apply_hamiltonian(field_now):
        rows_here = field_now.shape[0]
        rounded = field_now.astype(jnp.bfloat16)
        padded = jnp.concatenate([rounded, jnp.zeros((rows_here, 1), jnp.bfloat16)], axis=1)
        gathered = padded[:, node_index].astype(jnp.float32)
        products = jnp.einsum("ab,sbc->sac", matrix_wide, gathered) * cell_live
        assembled = jnp.zeros((rows_here, node_total + 1), jnp.float32).at[:, flat_index].add(products.reshape(rows_here, -1))
        return assembled[:, :node_total] + potential * field_now

    def filter_block(block_states):
        first_term = (apply_hamiltonian(block_states) - filter_centre * block_states) / filter_half
        return 2.0 * (apply_hamiltonian(first_term) - filter_centre * first_term) / filter_half - block_states

    blocks = states.reshape(STATES // BLOCK, BLOCK, node_total)
    filtered = lax.map(filter_block, blocks).reshape(STATES, node_total)
    rounded_wide = filtered.astype(jnp.bfloat16).astype(jnp.float32)
    scaled_wide = (weights * rounded_wide).astype(jnp.bfloat16).astype(jnp.float32)

    def gram_rows(scaled_block):
        return jnp.dot(scaled_block, rounded_wide.T, precision=lax.Precision.HIGHEST, preferred_element_type=jnp.float32)

    state_gram = lax.map(gram_rows, scaled_wide.reshape(STATES // BLOCK, BLOCK, node_total)).reshape(STATES, STATES)
    return filtered, state_gram
```

```python
import functools

import jax
import jax.numpy as jnp
from jax import lax
from jax.experimental import pallas as pl
from jax.experimental.pallas import tpu as pltpu
from jax.sharding import PartitionSpec as P

NODES = 18432
HALF = 9216
FACE = 1536
HFACE = 768
EXT = NODES + FACE
CELL_NODES = 343
CELLS = 64
ROW = 344
MAT = 352
LANES = 128
ACCS = 4
SPARE = 8
BLOCK = 1024
PIECE = 2304
VMEM = pl.BlockSpec(memory_space=pltpu.VMEM)
SMEM = pl.BlockSpec(memory_space=pltpu.SMEM)
ANY = pl.BlockSpec(memory_space=pl.ANY)
f32 = jnp.float32
bf16 = jnp.bfloat16


def to_mate(block):
    return lax.ppermute(block, "band", [(i, i ^ 1) for i in range(16)])


def along_dom(block, shift):
    return lax.ppermute(block, "dom", [(i, i + shift) for i in range(8) if 0 <= i + shift < 8])


def params(mib):
    return pltpu.CompilerParams(vmem_limit_bytes=mib * 2**20)


def turn_kernel(core, face, own, other, field, half, faces, whole, picked):
    step = pl.program_id(0)
    first = core[0] == 0
    low = jnp.where(first, own[...], other[...])
    high = jnp.where(first, other[...], own[...])
    rows = jnp.concatenate([low, high], axis=0).T
    field[...] = rows.astype(bf16)
    whole[pl.ds(pl.multiple_of(step * BLOCK, BLOCK), BLOCK), :] = rows

    @pl.when(step // 9 == core[0])
    def _():
        half[...] = rows

    @pl.when(step == 17)
    def _():
        def pick(i, _):
            for k in range(16):
                at = i * 16 + k
                picked[pl.ds(at, 1), :] = whole[pl.ds(face[at], 1), :]
            return 0

        lax.fori_loop(0, FACE // 16, pick, 0)
        faces[...] = picked[...].astype(bf16)


def turn(core, face, own, other):
    return pl.pallas_call(
        turn_kernel,
        grid_spec=pltpu.PrefetchScalarGridSpec(
            num_scalar_prefetch=2,
            grid=(18,),
            in_specs=[pl.BlockSpec((64, BLOCK), lambda i, c, f: (0, i))] * 2,
            out_specs=[
                pl.BlockSpec((BLOCK, LANES), lambda i, c, f: (i, 0)),
                pl.BlockSpec((BLOCK, LANES), lambda i, c, f: (jnp.clip(i - 9 * c[0], 0, 8), 0)),
                pl.BlockSpec((FACE, LANES), lambda i, c, f: (0, 0)),
            ],
            scratch_shapes=[pltpu.VMEM((NODES, LANES), f32), pltpu.VMEM((FACE, LANES), f32)],
        ),
        out_shape=[
            jax.ShapeDtypeStruct((NODES, LANES), bf16),
            jax.ShapeDtypeStruct((HALF, LANES), f32),
            jax.ShapeDtypeStruct((FACE, LANES), bf16),
        ],
        compiler_params=params(40),
        name="turn",
    )(core, face, own, other)


def spread_kernel(values, out):
    for j in range(8):
        row = jnp.broadcast_to(values[pl.ds(j, 1), :], (LANES, LANES))
        out[pl.ds(j * LANES, LANES), :] = row.T


def spread(values):
    count = values.shape[0]
    return pl.pallas_call(
        spread_kernel,
        grid=(count // BLOCK,),
        in_specs=[pl.BlockSpec((8, LANES), lambda i: (i, 0))],
        out_specs=pl.BlockSpec((BLOCK, LANES), lambda i: (i, 0)),
        out_shape=jax.ShapeDtypeStruct((count, LANES), f32),
        name="spread",
    )(values.reshape(count // LANES, LANES))


def apply_kernel(
    second, core, cells, index, face, potential,
    low, high, ghosts, start, matrix, faces, back,
    kept, sent, edge_kept, edge_sent,
    x, g0, g1, p0, p1, stage, picked, *rest,
):
    accs = rest[:ACCS]
    sems = rest[ACCS]
    h = core[0]
    mine = pl.multiple_of(h * HALF, HALF)
    theirs = pl.multiple_of((1 - h) * HALF, HALF)
    load = pltpu.make_async_copy(start, accs[0].at[pl.ds(mine, HALF)], sems.at[2])
    load.start()

    pieces = []
    for ref in (low, high):
        pieces += [(ref, at, PIECE) for at in range(0, ref.shape[0], PIECE)]
    pieces.append((ghosts, 0, FACE))
    copies = []
    for k, (ref, at, size) in enumerate(pieces):
        copies.append(
            pltpu.make_async_copy(
                ref.at[pl.ds(at, size)], stage.at[k % 2, pl.ds(0, size)], sems.at[k % 2]
            )
        )
    copies[0].start()

    def clear(i, _):
        for a in accs[1:]:
            a[pl.ds(pl.multiple_of(i * 256, 256), 256), :] = jnp.zeros((256, LANES), f32)
        return 0

    lax.fori_loop(0, EXT // 256, clear, 0)

    def clear_first(i, _):
        at = pl.multiple_of(theirs + i * 256, 256)
        accs[0][pl.ds(at, 256), :] = jnp.zeros((256, LANES), f32)
        return 0

    lax.fori_loop(0, HALF // 256, clear_first, 0)
    accs[0][pl.ds(NODES, FACE), :] = jnp.zeros((FACE, LANES), f32)
    for ref in (x, *accs):
        ref[pl.ds(EXT, SPARE), :] = jnp.zeros((SPARE, LANES), f32)
    for ref in (g0, g1, p0, p1):
        ref[...] = jnp.zeros_like(ref)

    done = 0
    for k, (ref, at, size) in enumerate(pieces):
        if k + 1 < len(pieces):
            copies[k + 1].start()
        copies[k].wait()

        def widen(i, _, k=k, done=done):
            at = pl.multiple_of(i * 256, 256)
            to = pl.multiple_of(done + i * 256, 256)
            x[pl.ds(to, 256), :] = stage[k % 2, pl.ds(at, 256), :].astype(f32)
            return 0

        lax.fori_loop(0, size // 256, widen, 0)
        done += size
    load.wait()

    if second:
        picked[...] = faces[...].astype(f32)

        def put(i, _):
            for k in range(16):
                at = i * 16 + k
                x[pl.ds(face[at], 1), :] = picked[pl.ds(at, 1), :]
            return 0

        lax.fori_loop(0, FACE // 16, put, 0)

        def shift(i, _):
            for k in range(8):
                at = i * 8 + k
                node = face[h * HFACE + at]
                gain = (potential[node] - 6.0) * 0.25
                accs[0][pl.ds(node, 1), :] += back[pl.ds(at, 1), :] * gain
            return 0

        lax.fori_loop(0, HFACE // 8, shift, 0)

    def gather(g, cell, lo, hi):
        for a in range(lo, min(hi, CELL_NODES)):
            g[pl.ds(a, 1), :] = x[pl.ds(index[(cell + 1) * ROW + a], 1), :]

    def scatter(p, cell, lo, hi):
        hi = min(hi, CELL_NODES)
        for a in range(lo, hi, ACCS):
            count = min(ACCS, hi - a)
            nodes = [index[(cell + 1) * ROW + a + k] for k in range(count)]
            sums = [accs[k][pl.ds(nodes[k], 1), :] + p[pl.ds(a + k, 1), :] for k in range(count)]
            for k in range(count):
                accs[k][pl.ds(nodes[k], 1), :] = sums[k]

    def step(g_next, next_cell, p_last, last_cell, g_now, p_now):
        p_now[...] = jnp.dot(matrix[...], g_now[...].astype(bf16), preferred_element_type=f32)
        for lo in range(0, CELL_NODES, 8):
            scatter(p_last, last_cell, lo, lo + 8)
            gather(g_next, next_cell, lo, lo + 8)

    gather(g0, 0, 0, CELL_NODES)

    def pair(i, _):
        cell = 2 * i
        step(g1, cell + 1, p1, cell - 1, g0, p0)
        step(g0, cell + 2, p0, cell, g1, p1)
        return 0

    pairs = (cells[0] + 1) // 2
    lax.fori_loop(0, pairs, pair, 0)
    scatter(p1, 2 * pairs - 1, 0, CELL_NODES)

    def total(i, _):
        rows = pl.ds(pl.multiple_of(i * 256, 256), 256)
        accs[0][rows, :] = (accs[0][rows, :] + accs[1][rows, :]) + (accs[2][rows, :] + accs[3][rows, :])
        return 0

    lax.fori_loop(0, EXT // 256, total, 0)
    out = [
        (accs[0].at[pl.ds(theirs, HALF)], sent),
        (accs[0].at[pl.ds(mine, HALF)], kept),
        (accs[0].at[pl.ds(pl.multiple_of(NODES + h * HFACE, HFACE), HFACE)], edge_kept.at[pl.ds(0, HFACE)]),
        (accs[0].at[pl.ds(pl.multiple_of(NODES + (1 - h) * HFACE, HFACE), HFACE)], edge_sent.at[pl.ds(0, HFACE)]),
    ]
    if not second:

        def pick(i, _):
            for k in range(16):
                at = i * 16 + k
                picked[pl.ds(at, 1), :] = accs[0][pl.ds(face[at], 1), :]
            return 0

        lax.fori_loop(0, FACE // 16, pick, 0)
        out += [
            (picked.at[pl.ds(pl.multiple_of(h * HFACE, HFACE), HFACE)], edge_kept.at[pl.ds(HFACE, HFACE)]),
            (picked.at[pl.ds(pl.multiple_of((1 - h) * HFACE, HFACE), HFACE)], edge_sent.at[pl.ds(HFACE, HFACE)]),
        ]
    writes = [pltpu.make_async_copy(a, b, sems.at[k]) for k, (a, b) in enumerate(out)]
    for w in writes:
        w.start()
    for w in writes:
        w.wait()


def apply(second, core, cells, index, face, potential, low, high, ghosts, start, matrix, faces, back):
    edge = jax.ShapeDtypeStruct((HFACE if second else FACE, LANES), f32)
    half = jax.ShapeDtypeStruct((HALF, LANES), f32)
    return pl.pallas_call(
        functools.partial(apply_kernel, second),
        in_specs=[SMEM] * 5 + [ANY] * 4 + [VMEM] * 3,
        out_specs=[ANY] * 4,
        scratch_shapes=[pltpu.VMEM((EXT + SPARE, LANES), f32)]
        + [pltpu.VMEM((MAT, LANES), f32)] * 4
        + [pltpu.VMEM((2, PIECE, LANES), bf16), pltpu.VMEM((FACE, LANES), f32)]
        + [pltpu.VMEM((EXT + SPARE, LANES), f32)] * ACCS
        + [pltpu.SemaphoreType.DMA((6,))],
        out_shape=[half, half, edge, edge],
        compiler_params=params(61),
        name="apply_second" if second else "apply_first",
    )(core, cells, index, face, potential, low, high, ghosts, start, matrix, faces, back)


def finish_kernel(core, face, kept, came, back, turned, rounded, sums):
    def add(i, _):
        rows = pl.ds(pl.multiple_of(i * 256, 256), 256)
        sums[rows, :] = (kept[rows, :] + came[rows, :]) * 0.5
        return 0

    lax.fori_loop(0, HALF // 256, add, 0)
    sums[pl.ds(HALF, SPARE), :] = jnp.zeros((SPARE, LANES), f32)
    base = core[0] * HALF

    def put(i, _):
        for k in range(8):
            at = i * 8 + k
            node = face[at] - base
            node = jnp.where((node >= 0) & (node < HALF), node, HALF)
            sums[pl.ds(node, 1), :] += back[pl.ds(at, 1), :] * 0.5
        return 0

    lax.fori_loop(0, FACE // 8, put, 0)

    def out(i, _):
        rows = pl.ds(pl.multiple_of(i * 256, 256), 256)
        block = sums[rows, :]
        rounded[rows, :] = block.astype(bf16)
        turned[:, rows] = block.T
        return 0

    lax.fori_loop(0, HALF // 256, out, 0)


def finish(core, face, kept, came, back):
    return pl.pallas_call(
        finish_kernel,
        in_specs=[SMEM] * 2 + [VMEM] * 3,
        out_specs=[VMEM] * 2,
        scratch_shapes=[pltpu.VMEM((HALF + SPARE, LANES), f32)],
        out_shape=[
            jax.ShapeDtypeStruct((LANES, HALF), f32),
            jax.ShapeDtypeStruct((HALF, LANES), bf16),
        ],
        compiler_params=params(40),
        name="finish",
    )(core, face, kept, came, back)


def across_chips(block):
    groups = [list(range(0, 16, 2)), list(range(1, 16, 2))]
    return lax.all_to_all(block, "band", 0, 0, axis_index_groups=groups, tiled=True)


def sum_over_dom(rows):
    p = lax.axis_index("dom")
    parts = rows.reshape(8, 8, 1024)
    part = lax.dynamic_index_in_dim(parts, p, 0, keepdims=False)
    for k in range(1, 8):
        route = [(i, i ^ k) for i in range(8)]
        part = part + lax.ppermute(
            lax.dynamic_index_in_dim(parts, p ^ k, 0, keepdims=False), "dom", route
        )
    whole = jnp.zeros((8, 8, 1024), f32)
    whole = lax.dynamic_update_index_in_dim(whole, part, p, 0)
    for k in range(1, 8):
        route = [(i, i ^ k) for i in range(8)]
        whole = lax.dynamic_update_index_in_dim(
            whole, lax.ppermute(part, "dom", route), p ^ k, 0
        )
    return whole.reshape(64, 1024)


def body(states, cell_matrix, potential, weights, connectivity, face_nodes, cell_counts):
    band = lax.axis_index("band")
    chip = band // 2
    h = band % 2
    core = h.astype(jnp.int32).reshape(1)

    other = to_mate(states)
    own_cells = lax.dynamic_index_in_dim(
        connectivity.reshape(CELL_NODES, CELLS, 2), h, 2, keepdims=False
    )
    cells = (cell_counts - h + 1) // 2
    live = jnp.arange(CELLS) < cells[0]
    index = jnp.where(live[:, None], own_cells.T, EXT)
    index = jnp.pad(index, ((1, 1), (0, ROW - CELL_NODES)), constant_values=EXT).reshape(-1)
    matrix = jnp.pad(cell_matrix, ((0, MAT - CELL_NODES),) * 2)
    raised = spread(lax.dynamic_slice(potential, (h * HALF,), (HALF,)) - 6.0)

    field, half, faces = turn(core, face_nodes, states, other)
    ghosts = along_dom(faces, -1)
    nothing = jnp.zeros((HFACE, LANES), f32)
    kept, sent, edge_kept, edge_sent = apply(
        False, core, cells, index, face_nodes, potential,
        field[:HALF], field[HALF:], ghosts, raised * half, matrix, faces, nothing,
    )
    came = to_mate(sent)
    edge = edge_kept + to_mate(edge_sent)
    back = along_dom(edge[:HFACE], 1)
    ahead = along_dom(edge[HFACE:], -1)
    inner = (lax.axis_index("dom") < 7).astype(f32)
    edge_mine = jnp.concatenate([(edge[:HFACE] + ahead) * inner, edge[HFACE:] + back])
    edge_mine = (edge_mine * 0.25).astype(bf16)
    edge_other = to_mate(edge_mine)

    def in_order(mine, theirs):
        return jnp.where(h == 0, mine, theirs), jnp.where(h == 0, theirs, mine)

    ghosts = jnp.concatenate(in_order(edge_mine[:HFACE], edge_other[:HFACE]))
    faces = jnp.concatenate(in_order(edge_mine[HFACE:], edge_other[HFACE:]))

    first_term = (kept + came) * 0.25
    rounded = first_term.astype(bf16)
    low, high = in_order(rounded, to_mate(rounded))
    kept, sent, edge_kept, edge_sent = apply(
        True, core, cells, index, face_nodes, potential,
        low, high, ghosts, raised * first_term - 2.0 * half, matrix, faces, back,
    )
    came = to_mate(sent)
    edge = edge_kept + to_mate(edge_sent)
    back = along_dom(edge, 1)
    back = jnp.concatenate(in_order(back, to_mate(back)))
    turned, rounded = finish(core, face_nodes, kept, came, back)

    everyone = across_chips(rounded.reshape(8, HALF // 8, LANES))
    pairs = turned.reshape(2, 64, HALF)
    mine = lax.dynamic_index_in_dim(pairs, h, 0, keepdims=False)
    theirs = to_mate(lax.dynamic_index_in_dim(pairs, 1 - h, 0, keepdims=False))
    filtered = jnp.concatenate(in_order(mine, theirs), axis=1)

    weight = lax.dynamic_slice(weights, (h * HALF + chip * (HALF // 8),), (HALF // 8,))
    scaled = (weight[None, :, None] * everyone.astype(f32)).astype(bf16)
    gram = jnp.einsum("qns,pnt->qspt", scaled, everyone, preferred_element_type=f32)
    gram = gram.reshape(8, 2, 64, 1024)
    mine = lax.dynamic_index_in_dim(gram, h, 1, keepdims=False)
    theirs = to_mate(lax.dynamic_index_in_dim(gram, 1 - h, 1, keepdims=False))
    rows = across_chips(mine + theirs).sum(0)
    return filtered, sum_over_dom(rows)


def solution(mesh):
    in_specs = (P("band", "dom"), P(), P("dom"), P("dom"), P(None, "dom"), P("dom"), P("dom"))
    out_specs = (P("band", "dom"), P("band", None))
    return jax.shard_map(body, mesh=mesh, in_specs=in_specs, out_specs=out_specs, check_vma=False)
```

```python
import functools

import jax
import jax.numpy as jnp
from jax import lax
from jax.experimental import pallas as pl
from jax.experimental.pallas import tpu as pltpu
from jax.sharding import PartitionSpec as P

NODES = 18432
HALF = 9216
FACE = 1536
HFACE = 768
EXT = NODES + FACE
CELL_NODES = 343
CELLS = 64
ROW = 344
MAT = 352
LANES = 128
ACCS = 4
SPARE = 8
SHARE = HALF // 8
FSHARE = HFACE // 8
BLOCK = 1024
PIECE = 2304
VMEM = pl.BlockSpec(memory_space=pltpu.VMEM)
SMEM = pl.BlockSpec(memory_space=pltpu.SMEM)
ANY = pl.BlockSpec(memory_space=pl.ANY)
f32 = jnp.float32
bf16 = jnp.bfloat16


def to_mate(block):
    return lax.ppermute(block, "band", [(i, i ^ 1) for i in range(16)])


def along_dom(block, shift):
    return lax.ppermute(block, "dom", [(i, i + shift) for i in range(8) if 0 <= i + shift < 8])


def params(mib):
    return pltpu.CompilerParams(vmem_limit_bytes=mib * 2**20)


def turn_kernel(core, face, own, other, field, half, faces, whole, picked):
    step = pl.program_id(0)
    first = core[0] == 0
    low = jnp.where(first, own[...], other[...])
    high = jnp.where(first, other[...], own[...])
    rows = jnp.concatenate([low, high], axis=0).T
    field[...] = rows.astype(bf16)
    whole[pl.ds(pl.multiple_of(step * BLOCK, BLOCK), BLOCK), :] = rows

    @pl.when(step // 9 == core[0])
    def _():
        half[...] = rows

    @pl.when(step == 17)
    def _():
        def pick(i, _):
            for k in range(16):
                at = i * 16 + k
                picked[pl.ds(at, 1), :] = whole[pl.ds(face[at], 1), :]
            return 0

        lax.fori_loop(0, FACE // 16, pick, 0)
        faces[...] = picked[...].astype(bf16)


def turn(core, face, own, other):
    return pl.pallas_call(
        turn_kernel,
        grid_spec=pltpu.PrefetchScalarGridSpec(
            num_scalar_prefetch=2,
            grid=(18,),
            in_specs=[pl.BlockSpec((64, BLOCK), lambda i, c, f: (0, i))] * 2,
            out_specs=[
                pl.BlockSpec((BLOCK, LANES), lambda i, c, f: (i, 0)),
                pl.BlockSpec((BLOCK, LANES), lambda i, c, f: (jnp.clip(i - 9 * c[0], 0, 8), 0)),
                pl.BlockSpec((FACE, LANES), lambda i, c, f: (0, 0)),
            ],
            scratch_shapes=[pltpu.VMEM((NODES, LANES), f32), pltpu.VMEM((FACE, LANES), f32)],
        ),
        out_shape=[
            jax.ShapeDtypeStruct((NODES, LANES), bf16),
            jax.ShapeDtypeStruct((HALF, LANES), f32),
            jax.ShapeDtypeStruct((FACE, LANES), bf16),
        ],
        compiler_params=params(40),
        name="turn",
    )(core, face, own, other)


def spread_kernel(values, out):
    for j in range(8):
        row = jnp.broadcast_to(values[pl.ds(j, 1), :], (LANES, LANES))
        out[pl.ds(j * LANES, LANES), :] = row.T


def spread(values):
    count = values.shape[0]
    return pl.pallas_call(
        spread_kernel,
        grid=(count // BLOCK,),
        in_specs=[pl.BlockSpec((8, LANES), lambda i: (i, 0))],
        out_specs=pl.BlockSpec((BLOCK, LANES), lambda i: (i, 0)),
        out_shape=jax.ShapeDtypeStruct((count, LANES), f32),
        name="spread",
    )(values.reshape(count // LANES, LANES))


def apply_kernel(
    second, core, cells, index, face, potential,
    field, ghosts, start, matrix, edge_mine, edge_other, back,
    kept, sent, edge_kept, edge_sent,
    x, g0, g1, p0, p1, stage, picked, *rest,
):
    accs = rest[:ACCS]
    sems = rest[ACCS]
    h = core[0]
    mine = pl.multiple_of(h * HALF, HALF)
    theirs = pl.multiple_of((1 - h) * HALF, HALF)
    load = pltpu.make_async_copy(start, accs[0].at[pl.ds(mine, HALF)], sems.at[2])
    load.start()

    if second:
        mine_first = [(field[0], at, PIECE, mine + at) for at in range(0, HALF, PIECE)]
        pieces = mine_first + [(field[1], at, PIECE, theirs + at) for at in range(0, HALF, PIECE)]
    else:
        pieces = [(field[0], at, PIECE, at) for at in range(0, NODES, PIECE)]
        pieces.append((ghosts[0], 0, FACE, NODES))
    copies = []
    for k, (ref, at, size, _) in enumerate(pieces):
        copies.append(
            pltpu.make_async_copy(
                ref.at[pl.ds(at, size)], stage.at[k % 2, pl.ds(0, size)], sems.at[k % 2]
            )
        )
    copies[0].start()

    def clear(i, _):
        for a in accs[1:]:
            a[pl.ds(pl.multiple_of(i * 256, 256), 256), :] = jnp.zeros((256, LANES), f32)
        return 0

    lax.fori_loop(0, EXT // 256, clear, 0)

    def clear_first(i, _):
        at = pl.multiple_of(theirs + i * 256, 256)
        accs[0][pl.ds(at, 256), :] = jnp.zeros((256, LANES), f32)
        return 0

    lax.fori_loop(0, HALF // 256, clear_first, 0)
    accs[0][pl.ds(NODES, FACE), :] = jnp.zeros((FACE, LANES), f32)
    for ref in (x, *accs):
        ref[pl.ds(EXT, SPARE), :] = jnp.zeros((SPARE, LANES), f32)
    for ref in (g0, g1, p0, p1):
        ref[...] = jnp.zeros_like(ref)

    for k, (_, _, size, to) in enumerate(pieces):
        if k + 1 < len(pieces):
            copies[k + 1].start()
        copies[k].wait()

        def widen(i, _, k=k, to=to):
            at = pl.multiple_of(i * 256, 256)
            rows = pl.ds(pl.multiple_of(to + i * 256, 256), 256)
            x[rows, :] = stage[k % 2, pl.ds(at, 256), :].astype(f32)
            return 0

        lax.fori_loop(0, size // 256, widen, 0)
    load.wait()

    if second:
        for edge, part in ((edge_mine, h), (edge_other, 1 - h)):
            to = pl.multiple_of(NODES + part * HFACE, HFACE)
            x[pl.ds(to, HFACE), :] = edge[pl.ds(0, HFACE), :].astype(f32)
            picked[pl.ds(pl.multiple_of(part * HFACE, HFACE), HFACE), :] = edge[
                pl.ds(HFACE, HFACE), :
            ].astype(f32)

        def put(i, _):
            for k in range(16):
                at = i * 16 + k
                x[pl.ds(face[at], 1), :] = picked[pl.ds(at, 1), :]
            return 0

        lax.fori_loop(0, FACE // 16, put, 0)

        def shift(i, _):
            for k in range(8):
                at = i * 8 + k
                node = face[h * HFACE + at]
                gain = (potential[node] - 6.0) * 0.25
                accs[0][pl.ds(node, 1), :] += back[pl.ds(at, 1), :] * gain
            return 0

        lax.fori_loop(0, HFACE // 8, shift, 0)

    def gather(g, cell, lo, hi):
        for a in range(lo, min(hi, CELL_NODES)):
            g[pl.ds(a, 1), :] = x[pl.ds(index[(cell + 1) * ROW + a], 1), :]

    def scatter(p, cell, lo, hi):
        hi = min(hi, CELL_NODES)
        for a in range(lo, hi, ACCS):
            count = min(ACCS, hi - a)
            nodes = [index[(cell + 1) * ROW + a + k] for k in range(count)]
            sums = [accs[k][pl.ds(nodes[k], 1), :] + p[pl.ds(a + k, 1), :] for k in range(count)]
            for k in range(count):
                accs[k][pl.ds(nodes[k], 1), :] = sums[k]

    def step(g_next, next_cell, p_last, last_cell, g_now, p_now):
        p_now[...] = jnp.dot(matrix[...], g_now[...].astype(bf16), preferred_element_type=f32)
        for lo in range(0, CELL_NODES, 8):
            scatter(p_last, last_cell, lo, lo + 8)
            gather(g_next, next_cell, lo, lo + 8)

    gather(g0, 0, 0, CELL_NODES)

    def pair(i, _):
        cell = 2 * i
        step(g1, cell + 1, p1, cell - 1, g0, p0)
        step(g0, cell + 2, p0, cell, g1, p1)
        return 0

    pairs = (cells[0] + 1) // 2
    lax.fori_loop(0, pairs, pair, 0)
    scatter(p1, 2 * pairs - 1, 0, CELL_NODES)

    def total(i, _):
        rows = pl.ds(pl.multiple_of(i * 256, 256), 256)
        accs[0][rows, :] = (accs[0][rows, :] + accs[1][rows, :]) + (accs[2][rows, :] + accs[3][rows, :])
        return 0

    lax.fori_loop(0, EXT // 256, total, 0)
    out = [
        (accs[0].at[pl.ds(theirs, HALF)], sent),
        (accs[0].at[pl.ds(mine, HALF)], kept),
        (accs[0].at[pl.ds(pl.multiple_of(NODES + h * HFACE, HFACE), HFACE)], edge_kept.at[pl.ds(0, HFACE)]),
        (accs[0].at[pl.ds(pl.multiple_of(NODES + (1 - h) * HFACE, HFACE), HFACE)], edge_sent.at[pl.ds(0, HFACE)]),
    ]

    def pick(i, _):
        for k in range(16):
            at = i * 16 + k
            picked[pl.ds(at, 1), :] = accs[0][pl.ds(face[at], 1), :]
        return 0

    lax.fori_loop(0, FACE // 16, pick, 0)
    out += [
        (picked.at[pl.ds(pl.multiple_of(h * HFACE, HFACE), HFACE)], edge_kept.at[pl.ds(HFACE, HFACE)]),
        (picked.at[pl.ds(pl.multiple_of((1 - h) * HFACE, HFACE), HFACE)], edge_sent.at[pl.ds(HFACE, HFACE)]),
    ]
    writes = [pltpu.make_async_copy(a, b, sems.at[k]) for k, (a, b) in enumerate(out)]
    for w in writes:
        w.start()
    for w in writes:
        w.wait()


def first_kernel(core, cells, index, face, potential, field, ghosts, start, matrix, *rest):
    apply_kernel(
        False, core, cells, index, face, potential,
        (field,), (ghosts,), start, matrix, None, None, None, *rest,
    )


def second_kernel(
    core, cells, index, face, potential, mine, theirs, start, matrix,
    edge_mine, edge_other, back, *rest,
):
    apply_kernel(
        True, core, cells, index, face, potential,
        (mine, theirs), (), start, matrix, edge_mine, edge_other, back, *rest,
    )


def apply(kernel, extra, *operands):
    edge = jax.ShapeDtypeStruct((FACE, LANES), f32)
    half = jax.ShapeDtypeStruct((HALF, LANES), f32)
    return pl.pallas_call(
        kernel,
        in_specs=[SMEM] * 5 + [ANY] * 3 + [VMEM] * (1 + extra),
        out_specs=[ANY] * 4,
        scratch_shapes=[pltpu.VMEM((EXT + SPARE, LANES), f32)]
        + [pltpu.VMEM((MAT, LANES), f32)] * 4
        + [pltpu.VMEM((2, PIECE, LANES), bf16), pltpu.VMEM((FACE, LANES), f32)]
        + [pltpu.VMEM((EXT + SPARE, LANES), f32)] * ACCS
        + [pltpu.SemaphoreType.DMA((6,))],
        out_shape=[half, half, edge, edge],
        compiler_params=params(61),
        name="apply",
    )(*operands)


def finish_kernel(core, face, kept, came, back_mine, back_other, turned, sums):
    def add(i, _):
        rows = pl.ds(pl.multiple_of(i * 256, 256), 256)
        sums[rows, :] = (kept[rows, :] + came[rows, :]) * 0.5
        return 0

    lax.fori_loop(0, HALF // 256, add, 0)
    sums[pl.ds(HALF, SPARE), :] = jnp.zeros((SPARE, LANES), f32)
    base = core[0] * HALF
    for back, part in ((back_mine, core[0]), (back_other, 1 - core[0])):

        def put(i, _, back=back, part=part):
            for k in range(8):
                at = i * 8 + k
                node = face[part * HFACE + at] - base
                node = jnp.where((node >= 0) & (node < HALF), node, HALF)
                sums[pl.ds(node, 1), :] += back[pl.ds(at, 1), :] * 0.5
            return 0

        lax.fori_loop(0, HFACE // 8, put, 0)

    def out(i, _):
        rows = pl.ds(pl.multiple_of(i * 256, 256), 256)
        turned[:, rows] = sums[rows, :].T
        return 0

    lax.fori_loop(0, HALF // 256, out, 0)


def finish(core, face, kept, came, back_mine, back_other):
    return pl.pallas_call(
        finish_kernel,
        in_specs=[SMEM] * 2 + [VMEM] * 4,
        out_specs=VMEM,
        scratch_shapes=[pltpu.VMEM((HALF + SPARE, LANES), f32)],
        out_shape=jax.ShapeDtypeStruct((LANES, HALF), f32),
        compiler_params=params(40),
        name="finish",
    )(core, face, kept, came, back_mine, back_other)


def weigh_kernel(place, face, weights, own, out, rows):
    for j in range(SHARE // LANES):
        row = jnp.broadcast_to(own[pl.ds(j, 1), :], (LANES, LANES))
        rows[pl.ds(j * LANES, LANES), :] = row.T
    zero = jnp.zeros((1, LANES), f32)

    def drop(i, _):
        for k in range(8):
            node = face[i * 8 + k] - place[0]
            node = jnp.where((node >= 0) & (node < SHARE), node, SHARE)
            rows[pl.ds(node, 1), :] = zero
        return 0

    lax.fori_loop(0, FACE // 8, drop, 0)
    out[pl.ds(0, SHARE), :] = rows[pl.ds(0, SHARE), :]

    def add(i, _):
        for k in range(8):
            at = i * 8 + k
            out[pl.ds(SHARE + at, 1), :] = jnp.full((1, LANES), weights[face[place[1] + at]], f32)
        return 0

    lax.fori_loop(0, FSHARE // 8, add, 0)


def weigh(place, face, weights, own):
    return pl.pallas_call(
        weigh_kernel,
        in_specs=[SMEM] * 3 + [VMEM],
        out_specs=VMEM,
        scratch_shapes=[pltpu.VMEM((SHARE + SPARE, LANES), f32)],
        out_shape=jax.ShapeDtypeStruct((SHARE + FSHARE, LANES), f32),
        compiler_params=params(16),
        name="weigh",
    )(place, face, weights, own.reshape(SHARE // LANES, LANES))


def gram_kernel(nodes, faces, weights, out, everyone):
    for q in range(8):
        lanes = pl.ds(q * LANES, LANES)
        everyone[pl.ds(0, SHARE), lanes] = nodes[q]
        everyone[pl.ds(SHARE, FSHARE), lanes] = faces[q]

    def rows(q, _):
        at = pl.multiple_of(q * LANES, LANES)
        block = everyone[:, pl.ds(at, LANES)].astype(f32)
        scaled = (weights[...] * block).T.astype(bf16)
        product = jnp.dot(scaled, everyone[...], preferred_element_type=f32)
        out[pl.ds(at, LANES), :] = product.astype(bf16)
        return 0

    lax.fori_loop(0, 8, rows, 0)


def gram_rows(nodes, faces, weights):
    return pl.pallas_call(
        gram_kernel,
        in_specs=[VMEM] * 3,
        out_specs=VMEM,
        scratch_shapes=[pltpu.VMEM((SHARE + FSHARE, 1024), bf16)],
        out_shape=jax.ShapeDtypeStruct((1024, 1024), bf16),
        compiler_params=params(40),
        name="gram",
    )(nodes, faces, weights)


def across_chips(block):
    groups = [list(range(0, 16, 2)), list(range(1, 16, 2))]
    return lax.all_to_all(block, "band", 0, 0, axis_index_groups=groups, tiled=True)


def sum_everywhere(partial):
    parts = lax.all_to_all(partial.reshape(128, 8, 1024), ("band", "dom"), 0, 0, tiled=True)
    part = jnp.sum(parts.astype(f32), axis=0)
    copies = jnp.broadcast_to(part[None], (8, 8, 1024))
    return lax.all_to_all(copies, "dom", 0, 0, tiled=True).reshape(64, 1024)


def body(states, cell_matrix, potential, weights, connectivity, face_nodes, cell_counts):
    band = lax.axis_index("band")
    chip = band // 2
    h = band % 2
    core = h.astype(jnp.int32).reshape(1)

    other = to_mate(states)
    own_cells = lax.dynamic_index_in_dim(
        connectivity.reshape(CELL_NODES, CELLS, 2), h, 2, keepdims=False
    )
    cells = (cell_counts - h + 1) // 2
    live = jnp.arange(CELLS) < cells[0]
    index = jnp.where(live[:, None], own_cells.T, EXT)
    index = jnp.pad(index, ((1, 1), (0, ROW - CELL_NODES)), constant_values=EXT).reshape(-1)
    matrix = jnp.pad(cell_matrix, ((0, MAT - CELL_NODES),) * 2)
    raised = spread(lax.dynamic_slice(potential, (h * HALF,), (HALF,)) - 6.0)

    field, half, faces = turn(core, face_nodes, states, other)
    ghosts = along_dom(faces, -1)
    scalars = (core, cells, index, face_nodes, potential)
    kept, sent, edge_kept, edge_sent = apply(
        first_kernel, 0, *scalars, field, ghosts, raised * half, matrix
    )
    came = to_mate(sent)
    edge = edge_kept + to_mate(edge_sent)
    back = along_dom(edge[:HFACE], 1)
    ahead = along_dom(edge[HFACE:], -1)
    inner = (lax.axis_index("dom") < 7).astype(f32)
    edge_mine = jnp.concatenate([(edge[:HFACE] + ahead) * inner, edge[HFACE:] + back])
    edge_mine = (edge_mine * 0.25).astype(bf16)
    edge_other = to_mate(edge_mine)

    rounded = ((kept + came) * 0.25).astype(bf16)
    theirs = to_mate(rounded)
    kept, came = lax.optimization_barrier((kept, came))
    start = raised * ((kept + came) * 0.25) - 2.0 * half
    kept, sent, edge_kept, edge_sent = apply(
        second_kernel, 3, *scalars, rounded, theirs, start, matrix, edge_mine, edge_other, back
    )
    came = to_mate(sent)
    edge = edge_kept + to_mate(edge_sent)
    back = along_dom(edge[:HFACE], 1)
    rounded = ((kept + came) * 0.5).astype(bf16)
    nodes = across_chips(rounded.reshape(8, SHARE, LANES))
    edge_rounded = ((edge[HFACE:] + back) * 0.5).astype(bf16)
    faces = across_chips(edge_rounded.reshape(8, FSHARE, LANES))

    turned = finish(core, face_nodes, kept, came, back, to_mate(back))
    pairs = turned.reshape(2, 64, HALF)
    mine = lax.dynamic_index_in_dim(pairs, h, 0, keepdims=False)
    theirs = to_mate(lax.dynamic_index_in_dim(pairs, 1 - h, 0, keepdims=False))
    low = jnp.where(h == 0, mine, theirs)
    high = jnp.where(h == 0, theirs, mine)
    filtered = jnp.concatenate([low, high], axis=1)

    begin = h * HALF + chip * SHARE
    place = jnp.stack([begin, h * HFACE + chip * FSHARE]).astype(jnp.int32)
    own = lax.dynamic_slice(weights, (begin,), (SHARE,))
    partial = gram_rows(nodes, faces, weigh(place, face_nodes, weights, own))
    return filtered, sum_everywhere(partial)


def solution(mesh):
    in_specs = (P("band", "dom"), P(), P("dom"), P("dom"), P(None, "dom"), P("dom"), P("dom"))
    out_specs = (P("band", "dom"), P("band", None))
    return jax.shard_map(body, mesh=mesh, in_specs=in_specs, out_specs=out_specs, check_vma=False)
```

```python
import functools

import jax
import jax.numpy as jnp
from jax import lax
from jax.experimental import pallas as pl
from jax.experimental.pallas import tpu as pltpu
from jax.sharding import PartitionSpec as P

NODES = 18432
HALF = 9216
FACE = 1536
HFACE = 768
EXT = NODES + FACE
CELL_NODES = 343
CELLS = 64
ROWS = 70
MAT = 352
LANES = 128
ACCS = 4
SPARE = 8
SHARE = HALF // 8
FSHARE = HFACE // 8
BLOCK = 1024
PIECE = 4608
VMEM = pl.BlockSpec(memory_space=pltpu.VMEM)
SMEM = pl.BlockSpec(memory_space=pltpu.SMEM)
ANY = pl.BlockSpec(memory_space=pl.ANY)
f32 = jnp.float32
bf16 = jnp.bfloat16


def to_mate(block):
    return lax.ppermute(block, "band", [(i, i ^ 1) for i in range(16)])


def along_dom(block, shift):
    return lax.ppermute(block, "dom", [(i, i + shift) for i in range(8) if 0 <= i + shift < 8])


def along_dom_crossed(block, shift):
    pairs = [(i, i + shift, j) for i in range(8) for j in range(16) if 0 <= i + shift < 8]
    route = [(i * 16 + (j ^ 1), to * 16 + j) for i, to, j in pairs]
    return lax.ppermute(block, ("dom", "band"), route)


def params(mib):
    return pltpu.CompilerParams(vmem_limit_bytes=mib * 2**20)


def eye():
    rows = lax.broadcasted_iota(jnp.int32, (LANES, LANES), 0)
    return jnp.where(rows == lax.broadcasted_iota(jnp.int32, (LANES, LANES), 1), 1.0, 0.0).astype(bf16)


def turned_by(unit, block):
    return lax.dot_general(unit, block, (((1,), (1,)), ((), ())), preferred_element_type=f32)


def faces_kernel(face, own, out, whole, picked):
    step = pl.program_id(0)
    unit = eye()
    block = own[...].astype(bf16)
    for j in range(BLOCK // LANES):
        rows = pl.ds(pl.multiple_of(step * BLOCK + j * LANES, LANES), LANES)
        whole[rows, pl.ds(0, 64)] = turned_by(unit, block[:, j * LANES : (j + 1) * LANES])

    @pl.when(step == NODES // BLOCK - 1)
    def _():
        def pick(i, _):
            for k in range(16):
                at = i * 16 + k
                picked[pl.ds(at, 1), :] = whole[pl.ds(face[at], 1), :]
            return 0

        lax.fori_loop(0, FACE // 16, pick, 0)
        left = lax.broadcasted_iota(jnp.int32, (HFACE, LANES), 1) < 64
        right = pltpu.roll(picked[pl.ds(HFACE, HFACE), :], 64, 1)
        out[...] = jnp.where(left, picked[pl.ds(0, HFACE), :], right).astype(bf16)


def own_faces(face, own):
    return pl.pallas_call(
        faces_kernel,
        grid_spec=pltpu.PrefetchScalarGridSpec(
            num_scalar_prefetch=1,
            grid=(NODES // BLOCK,),
            in_specs=[pl.BlockSpec((64, BLOCK), lambda i, f: (0, i))],
            out_specs=pl.BlockSpec((HFACE, LANES), lambda i, f: (0, 0)),
            scratch_shapes=[pltpu.VMEM((NODES, LANES), f32), pltpu.VMEM((FACE, LANES), f32)],
        ),
        out_shape=jax.ShapeDtypeStruct((HFACE, LANES), bf16),
        compiler_params=params(48),
        name="faces",
    )(face, own)


def turn_kernel(core, own, other, potential, field, half, raised, start):
    step = pl.program_id(0)
    first = core[0] == 0
    low = jnp.where(first, own[...], other[...])
    high = jnp.where(first, other[...], own[...])
    block = jnp.concatenate([low, high], axis=0)
    unit = eye()
    rounded = block.astype(bf16)
    for j in range(BLOCK // LANES):
        rows = pl.ds(j * LANES, LANES)
        field[rows, :] = turned_by(unit, rounded[:, j * LANES : (j + 1) * LANES]).astype(bf16)

    @pl.when(step // 9 == core[0])
    def _():
        half[...] = block.T
        for j in range(BLOCK // LANES):
            rows = pl.ds(j * LANES, LANES)
            rest = jnp.broadcast_to(potential[0, pl.ds(j, 1), :] - 6.0, (LANES, LANES))
            column = jnp.zeros((LANES, LANES), f32)
            for _ in range(3):
                part = rest.astype(bf16)
                column = column + turned_by(unit, part)
                rest = rest - part.astype(f32)
            raised[rows, :] = column
            start[rows, :] = column * half[rows, :]


def turn(core, own, other, potential):
    half = pl.BlockSpec((BLOCK, LANES), lambda i, c: (jnp.clip(i - 9 * c[0], 0, 8), 0))
    return pl.pallas_call(
        turn_kernel,
        grid_spec=pltpu.PrefetchScalarGridSpec(
            num_scalar_prefetch=1,
            grid=(NODES // BLOCK,),
            in_specs=[pl.BlockSpec((64, BLOCK), lambda i, c: (0, i))] * 2
            + [pl.BlockSpec((1, 8, LANES), lambda i, c: (i, 0, 0))],
            out_specs=[pl.BlockSpec((BLOCK, LANES), lambda i, c: (i, 0)), half, half, half],
        ),
        out_shape=[jax.ShapeDtypeStruct((NODES, LANES), bf16)]
        + [jax.ShapeDtypeStruct((HALF, LANES), f32)] * 3,
        compiler_params=params(60),
        name="turn",
    )(core, own, other, potential.reshape(NODES // BLOCK, 8, LANES))


def apply_kernel(
    second, core, cells, face, potential,
    index, field, start, matrix, ghosts, edge_mine, edge_other, back,
    kept, sent, edge_kept, edge_sent,
    x, g0, g1, p0, p1, stage, picked, *rest,
):
    accs = rest[:ACCS]
    ahead, behind, sems, slots = rest[ACCS : ACCS + 4], rest[ACCS + 4 : ACCS + 8], rest[-2], rest[-1]
    h = core[0]
    mine = pl.multiple_of(h * HALF, HALF)
    theirs = pl.multiple_of((1 - h) * HALF, HALF)
    load = pltpu.make_async_copy(start, accs[0].at[pl.ds(mine, HALF)], sems.at[0])
    copies = []
    for k in range(NODES // PIECE):
        ref, at = (field[0], k * PIECE) if len(field) == 1 else (field[k // 2], k % 2 * PIECE)
        copies.append(
            pltpu.make_async_copy(
                ref.at[pl.ds(at, PIECE)], stage.at[pl.ds(k * PIECE, PIECE)], sems.at[k + 1]
            )
        )
    for copy in copies:
        copy.start()
    load.start()

    def fetch(stage_number, cell):
        row = cell + 1
        a = pltpu.make_async_copy(index.at[row + 1], ahead[stage_number], slots.at[stage_number])
        b = pltpu.make_async_copy(index.at[row - 1], behind[stage_number], slots.at[4 + stage_number])
        return a, b

    for k in range(4):
        for copy in fetch(k, k):
            copy.start()

    zeros = jnp.zeros((256, LANES), f32)

    def clear(i, _):
        for a in accs[1:]:
            a[pl.ds(pl.multiple_of(i * 256, 256), 256), :] = zeros
        return 0

    lax.fori_loop(0, EXT // 256, clear, 0)

    def clear_first(i, _):
        accs[0][pl.ds(pl.multiple_of(theirs + i * 256, 256), 256), :] = zeros
        return 0

    lax.fori_loop(0, HALF // 256, clear_first, 0)
    accs[0][pl.ds(NODES, FACE), :] = jnp.zeros((FACE, LANES), f32)
    for ref in (x, *accs):
        ref[pl.ds(EXT, SPARE), :] = jnp.zeros((SPARE, LANES), f32)
    for ref in (g0, g1, p0, p1):
        ref[...] = jnp.zeros_like(ref)

    if second:
        for edge, part in ((edge_mine, h), (edge_other, 1 - h)):
            to = pl.multiple_of(NODES + part * HFACE, HFACE)
            x[pl.ds(to, HFACE), :] = edge[pl.ds(0, HFACE), :].astype(f32)
            picked[pl.ds(pl.multiple_of(part * HFACE, HFACE), HFACE), :] = edge[
                pl.ds(HFACE, HFACE), :
            ].astype(f32)
    else:
        first = core[0] == 0
        own, other = ghosts[0][...].astype(f32), ghosts[1][...].astype(f32)
        low, high = jnp.where(first, own, other), jnp.where(first, other, own)
        left = lax.broadcasted_iota(jnp.int32, (HFACE, LANES), 1) < 64
        x[pl.ds(NODES, HFACE), :] = jnp.where(left, low, pltpu.roll(high, 64, 1))
        x[pl.ds(NODES + HFACE, HFACE), :] = jnp.where(left, pltpu.roll(low, 64, 1), high)

    for k, copy in enumerate(copies):
        copy.wait()
        if second:
            base = (mine if k < 2 else theirs) + k % 2 * PIECE
        else:
            base = k * PIECE

        def widen(i, _, k=k, base=base):
            at = pl.multiple_of(k * PIECE + i * 256, 256)
            rows = pl.ds(pl.multiple_of(base + i * 256, 256), 256)
            x[rows, :] = stage[pl.ds(at, 256), :].astype(f32)
            return 0

        lax.fori_loop(0, PIECE // 256, widen, 0)
    load.wait()

    if second:

        def put(i, _):
            for k in range(16):
                at = i * 16 + k
                x[pl.ds(face[at], 1), :] = picked[pl.ds(at, 1), :]
            return 0

        lax.fori_loop(0, FACE // 16, put, 0)

        def shift(i, _):
            for j in range(0, 16, ACCS):
                at = [i * 16 + j + k for k in range(ACCS)]
                node = [face[h * HFACE + a] for a in at]
                gain = [(potential[n] - 6.0) * 0.25 for n in node]
                sums = [
                    accs[k][pl.ds(node[k], 1), :] + back[pl.ds(at[k], 1), :] * gain[k]
                    for k in range(ACCS)
                ]
                for k in range(ACCS):
                    accs[k][pl.ds(node[k], 1), :] = sums[k]
            return 0

        lax.fori_loop(0, HFACE // 16, shift, 0)

    def gather(g, nodes, lo, hi):
        for a in range(lo, min(hi, CELL_NODES)):
            g[pl.ds(a, 1), :] = x[pl.ds(nodes[a // LANES, a % LANES], 1), :]

    def scatter(p, nodes, lo, hi):
        for a in range(lo, min(hi, CELL_NODES), 2 * ACCS):
            count = min(2 * ACCS, CELL_NODES - a)
            at = [nodes[(a + k) // LANES, (a + k) % LANES] for k in range(count)]
            held = [accs[k % ACCS][pl.ds(at[k], 1), :] for k in range(count)]
            sums = []
            for k in range(count):
                if k >= ACCS:
                    held[k] = jnp.where(at[k] == at[k - ACCS], sums[k - ACCS], held[k])
                sums.append(held[k] + p[pl.ds(a + k, 1), :])
            for k in range(count):
                accs[k % ACCS][pl.ds(at[k], 1), :] = sums[k]

    def step(k, cell):
        g_now, g_next, p_now, p_last = (g0, g1, p0, p1) if k % 2 == 0 else (g1, g0, p1, p0)
        for copy in fetch(k, cell + k):
            copy.wait()
        p_now[...] = jnp.dot(matrix[...], g_now[...].astype(bf16), preferred_element_type=f32)
        for lo in range(0, CELL_NODES, 8):
            scatter(p_last, behind[k], lo, lo + 8)
            gather(g_next, ahead[k], lo, lo + 8)
        for copy in fetch(k, cell + 4 + k):
            copy.start()

    first = pltpu.make_async_copy(index.at[1], rest[ACCS + 8], slots.at[8])
    first.start()
    first.wait()
    gather(g0, rest[ACCS + 8], 0, CELL_NODES)

    def four(i, _):
        for k in range(4):
            step(k, 4 * i)
        return 0

    fours = (cells[0] + 3) // 4
    lax.fori_loop(0, fours, four, 0)
    for k in range(4):
        for copy in fetch(k, 4 * fours + k):
            copy.wait()
    scatter(p1, behind[0], 0, CELL_NODES)

    def total(begin, count):
        def add(i, _):
            rows = pl.ds(pl.multiple_of(begin + i * 256, 256), 256)
            accs[0][rows, :] = (accs[0][rows, :] + accs[1][rows, :]) + (
                accs[2][rows, :] + accs[3][rows, :]
            )
            return 0

        lax.fori_loop(0, count // 256, add, 0)

    writes = []

    def write(source, target):
        writes.append(pltpu.make_async_copy(source, target, sems.at[len(writes)]))
        writes[-1].start()

    for begin, target in ((theirs, sent), (mine, kept)):
        for at in range(0, HALF, PIECE):
            total(begin + at, PIECE)
            write(
                accs[0].at[pl.ds(pl.multiple_of(begin + at, PIECE), PIECE)],
                target.at[pl.ds(at, PIECE)],
            )
    total(NODES, FACE)

    def pick(i, _):
        for k in range(16):
            at = i * 16 + k
            picked[pl.ds(at, 1), :] = accs[0][pl.ds(face[at], 1), :]
        return 0

    lax.fori_loop(0, FACE // 16, pick, 0)
    for part, target in ((1 - h, edge_sent), (h, edge_kept)):
        ghost = pl.multiple_of(NODES + part * HFACE, HFACE)
        write(accs[0].at[pl.ds(ghost, HFACE)], target.at[pl.ds(0, HFACE)])
        own = pl.multiple_of(part * HFACE, HFACE)
        write(picked.at[pl.ds(own, HFACE)], target.at[pl.ds(HFACE, HFACE)])
    for w in writes:
        w.wait()


def first_kernel(core, cells, face, potential, index, field, start, matrix, own, other, *rest):
    apply_kernel(
        False, core, cells, face, potential, index,
        (field,), start, matrix, (own, other), None, None, None, *rest,
    )


def second_kernel(
    core, cells, face, potential, index, mine, theirs, start, matrix,
    edge_mine, edge_other, back, *rest,
):
    apply_kernel(
        True, core, cells, face, potential, index,
        (mine, theirs), start, matrix, None, edge_mine, edge_other, back, *rest,
    )


def apply(kernel, fields, edges, *operands):
    edge = jax.ShapeDtypeStruct((FACE, LANES), f32)
    half = jax.ShapeDtypeStruct((HALF, LANES), f32)
    return pl.pallas_call(
        kernel,
        in_specs=[SMEM] * 4 + [ANY] * (2 + fields) + [VMEM] * (1 + edges),
        out_specs=[ANY] * 4,
        scratch_shapes=[pltpu.VMEM((EXT + SPARE, LANES), f32)]
        + [pltpu.VMEM((MAT, LANES), f32)] * 4
        + [pltpu.VMEM((NODES, LANES), bf16), pltpu.VMEM((FACE, LANES), f32)]
        + [pltpu.VMEM((EXT + SPARE, LANES), f32)] * ACCS
        + [pltpu.SMEM((8, LANES), jnp.int32)] * 9
        + [pltpu.SemaphoreType.DMA((8,)), pltpu.SemaphoreType.DMA((9,))],
        out_shape=[half, half, edge, edge],
        compiler_params=params(61),
        name="apply",
    )(*operands)


def finish_kernel(core, face, kept, came, back_mine, back_other, turned, sums):
    def add(i, _):
        rows = pl.ds(pl.multiple_of(i * 256, 256), 256)
        sums[rows, :] = (kept[rows, :] + came[rows, :]) * 0.5
        return 0

    lax.fori_loop(0, HALF // 256, add, 0)
    sums[pl.ds(HALF, SPARE), :] = jnp.zeros((SPARE, LANES), f32)
    base = core[0] * HALF
    for back, part in ((back_mine, core[0]), (back_other, 1 - core[0])):

        def put(i, _, back=back, part=part):
            for k in range(8):
                at = i * 8 + k
                node = face[part * HFACE + at] - base
                node = jnp.where((node >= 0) & (node < HALF), node, HALF)
                sums[pl.ds(node, 1), :] += back[pl.ds(at, 1), :] * 0.5
            return 0

        lax.fori_loop(0, HFACE // 8, put, 0)

    def out(i, _):
        rows = pl.ds(pl.multiple_of(i * 256, 256), 256)
        turned[:, rows] = sums[rows, :].T
        return 0

    lax.fori_loop(0, HALF // 256, out, 0)


def finish(core, face, kept, came, back_mine, back_other):
    return pl.pallas_call(
        finish_kernel,
        in_specs=[SMEM] * 2 + [VMEM] * 4,
        out_specs=VMEM,
        scratch_shapes=[pltpu.VMEM((HALF + SPARE, LANES), f32)],
        out_shape=jax.ShapeDtypeStruct((LANES, HALF), f32),
        compiler_params=params(60),
        name="finish",
    )(core, face, kept, came, back_mine, back_other)


def weigh_kernel(place, face, weights, own, out, rows):
    for j in range(SHARE // LANES):
        row = jnp.broadcast_to(own[pl.ds(j, 1), :], (LANES, LANES))
        rows[pl.ds(j * LANES, LANES), :] = row.T
    zero = jnp.zeros((1, LANES), f32)

    def drop(i, _):
        for k in range(8):
            node = face[i * 8 + k] - place[0]
            node = jnp.where((node >= 0) & (node < SHARE), node, SHARE)
            rows[pl.ds(node, 1), :] = zero
        return 0

    lax.fori_loop(0, FACE // 8, drop, 0)
    out[pl.ds(0, SHARE), :] = rows[pl.ds(0, SHARE), :]

    def add(i, _):
        for k in range(8):
            at = i * 8 + k
            out[pl.ds(SHARE + at, 1), :] = jnp.full((1, LANES), weights[face[place[1] + at]], f32)
        return 0

    lax.fori_loop(0, FSHARE // 8, add, 0)


def weigh(place, face, weights, own):
    return pl.pallas_call(
        weigh_kernel,
        in_specs=[SMEM] * 3 + [VMEM],
        out_specs=VMEM,
        scratch_shapes=[pltpu.VMEM((SHARE + SPARE, LANES), f32)],
        out_shape=jax.ShapeDtypeStruct((SHARE + FSHARE, LANES), f32),
        compiler_params=params(60),
        name="weigh",
    )(place, face, weights, own.reshape(SHARE // LANES, LANES))


def gram_kernel(nodes, faces, weights, out, everyone):
    for q in range(8):
        lanes = pl.ds(q * LANES, LANES)
        everyone[pl.ds(0, SHARE), lanes] = nodes[q]
        everyone[pl.ds(SHARE, FSHARE), lanes] = faces[q]

    def rows(q, _):
        at = pl.multiple_of(q * LANES, LANES)
        block = everyone[:, pl.ds(at, LANES)].astype(f32)
        scaled = (weights[...] * block).T.astype(bf16)
        product = jnp.dot(scaled, everyone[...], preferred_element_type=f32)
        out[pl.ds(at, LANES), :] = product.astype(bf16)
        return 0

    lax.fori_loop(0, 8, rows, 0)


def gram_rows(nodes, faces, weights):
    return pl.pallas_call(
        gram_kernel,
        in_specs=[VMEM] * 3,
        out_specs=VMEM,
        scratch_shapes=[pltpu.VMEM((SHARE + FSHARE, 1024), bf16)],
        out_shape=jax.ShapeDtypeStruct((1024, 1024), bf16),
        compiler_params=params(60),
        name="gram",
    )(nodes, faces, weights)


def across_chips(block):
    groups = [list(range(0, 16, 2)), list(range(1, 16, 2))]
    return lax.all_to_all(block, "band", 0, 0, axis_index_groups=groups, tiled=True)


def sum_everywhere(partial):
    parts = lax.all_to_all(partial.reshape(128, 8, 1024), ("band", "dom"), 0, 0, tiled=True)
    part = jnp.sum(parts.astype(f32), axis=0)
    copies = jnp.broadcast_to(part[None], (8, 8, 1024))
    return lax.all_to_all(copies, "dom", 0, 0, tiled=True).reshape(64, 1024)


def body(states, cell_matrix, potential, weights, connectivity, face_nodes, cell_counts):
    band = lax.axis_index("band")
    chip = band // 2
    h = band % 2
    core = h.astype(jnp.int32).reshape(1)

    other = to_mate(states)
    own_cells = lax.dynamic_index_in_dim(
        connectivity.reshape(CELL_NODES, CELLS, 2), h, 2, keepdims=False
    )
    cells = (cell_counts - h + 1) // 2
    live = jnp.arange(CELLS) < cells[0]
    index = jnp.where(live[:, None], own_cells.T, EXT)
    index = jnp.pad(index, ((1, ROWS - 1 - CELLS), (0, 1024 - CELL_NODES)), constant_values=EXT)
    index = index.reshape(ROWS, 8, LANES)
    matrix = jnp.pad(cell_matrix, ((0, MAT - CELL_NODES),) * 2)
    faces = own_faces(face_nodes, states)
    ghosts = along_dom(faces, -1)
    ghosts_other = along_dom_crossed(faces, -1)
    field, half, raised, start = turn(core, states, other, potential)
    scalars = (core, cells, face_nodes, potential, index)
    kept, sent, edge_kept, edge_sent = apply(
        first_kernel, 1, 2, *scalars, field, start, matrix, ghosts, ghosts_other
    )
    edge = edge_kept + to_mate(edge_sent)
    came = to_mate(sent)
    rounded = ((kept + came) * 0.25).astype(bf16)
    edge, _ = lax.optimization_barrier((edge, rounded))
    back = along_dom(edge[:HFACE], 1)
    ahead = along_dom(edge[HFACE:], -1)
    theirs = to_mate(rounded)
    kept, came, _ = lax.optimization_barrier((kept, came, rounded))
    start = raised * ((kept + came) * 0.25) - 2.0 * half
    inner = (lax.axis_index("dom") < 7).astype(f32)
    edge_mine = jnp.concatenate([(edge[:HFACE] + ahead) * inner, edge[HFACE:] + back])
    edge_mine = (edge_mine * 0.25).astype(bf16)
    edge_other = to_mate(edge_mine)
    kept, sent, edge_kept, edge_sent = apply(
        second_kernel, 2, 3, *scalars, rounded, theirs, start, matrix, edge_mine, edge_other, back
    )
    edge = edge_kept + to_mate(edge_sent)
    came = to_mate(sent)
    rounded = ((kept + came) * 0.5).astype(bf16)
    edge, kept, came, _ = lax.optimization_barrier((edge, kept, came, rounded))
    back = along_dom(edge[:HFACE], 1)
    nodes = across_chips(rounded.reshape(8, SHARE, LANES))
    edge_rounded = ((edge[HFACE:] + back) * 0.5).astype(bf16)
    faces = across_chips(edge_rounded.reshape(8, FSHARE, LANES))

    turned = finish(core, face_nodes, kept, came, back, to_mate(back))
    pairs = turned.reshape(2, 64, HALF)
    mine = lax.dynamic_index_in_dim(pairs, h, 0, keepdims=False)
    theirs = to_mate(lax.dynamic_index_in_dim(pairs, 1 - h, 0, keepdims=False))
    low = jnp.where(h == 0, mine, theirs)
    high = jnp.where(h == 0, theirs, mine)
    filtered = jnp.concatenate([low, high], axis=1)

    begin = h * HALF + chip * SHARE
    place = jnp.stack([begin, h * HFACE + chip * FSHARE]).astype(jnp.int32)
    own = lax.dynamic_slice(weights, (begin,), (SHARE,))
    partial = gram_rows(nodes, faces, weigh(place, face_nodes, weights, own))
    return filtered, sum_everywhere(partial)


def solution(mesh):
    in_specs = (P("band", "dom"), P(), P("dom"), P("dom"), P(None, "dom"), P("dom"), P("dom"))
    out_specs = (P("band", "dom"), P("band", None))
    return jax.shard_map(body, mesh=mesh, in_specs=in_specs, out_specs=out_specs, check_vma=False)
```

```python
import functools

import jax
import jax.numpy as jnp
from jax import lax
from jax.experimental import pallas as pl
from jax.experimental.pallas import tpu as pltpu
from jax.sharding import PartitionSpec as P

NODES = 18432
HALF = 9216
FACE = 1536
HFACE = 768
EXT = NODES + FACE
CELL_NODES = 343
CELLS = 64
ROWS = 70
MAT = 352
LANES = 128
ACCS = 4
SPARE = 8
SHARE = HALF // 8
FSHARE = HFACE // 8
BLOCK = 3072
PIECE = 4608
VMEM = pl.BlockSpec(memory_space=pltpu.VMEM)
SMEM = pl.BlockSpec(memory_space=pltpu.SMEM)
ANY = pl.BlockSpec(memory_space=pl.ANY)
f32 = jnp.float32
bf16 = jnp.bfloat16


def to_mate(block):
    return lax.ppermute(block, "band", [(i, i ^ 1) for i in range(16)])


def along_dom(block, shift):
    return lax.ppermute(block, "dom", [(i, i + shift) for i in range(8) if 0 <= i + shift < 8])


def along_dom_crossed(block, shift):
    pairs = [(i, i + shift, j) for i in range(8) for j in range(16) if 0 <= i + shift < 8]
    route = [(i * 16 + (j ^ 1), to * 16 + j) for i, to, j in pairs]
    return lax.ppermute(block, ("dom", "band"), route)


FREE = pl.CostEstimate(flops=0, bytes_accessed=0, transcendentals=0)


def params(mib):
    return pltpu.CompilerParams(vmem_limit_bytes=mib * 2**20)


def eye():
    rows = lax.broadcasted_iota(jnp.int32, (LANES, LANES), 0)
    return jnp.where(rows == lax.broadcasted_iota(jnp.int32, (LANES, LANES), 1), 1.0, 0.0).astype(bf16)


def turned_by(unit, block):
    return lax.dot_general(unit, block, (((1,), (1,)), ((), ())), preferred_element_type=f32)


def faces_kernel(face, own, out, whole, picked):
    step = pl.program_id(0)
    unit = eye()
    block = own[...].astype(bf16)
    for j in range(BLOCK // LANES):
        rows = pl.ds(pl.multiple_of(step * BLOCK + j * LANES, LANES), LANES)
        whole[rows, pl.ds(0, 64)] = turned_by(unit, block[:, j * LANES : (j + 1) * LANES])

    @pl.when(step == NODES // BLOCK - 1)
    def _():
        def pick(i, _):
            for k in range(16):
                at = i * 16 + k
                picked[pl.ds(at, 1), :] = whole[pl.ds(face[at], 1), :]
            return 0

        lax.fori_loop(0, FACE // 16, pick, 0)
        left = lax.broadcasted_iota(jnp.int32, (HFACE, LANES), 1) < 64
        right = pltpu.roll(picked[pl.ds(HFACE, HFACE), :], 64, 1)
        out[...] = jnp.where(left, picked[pl.ds(0, HFACE), :], right).astype(bf16)


def own_faces(face, own):
    return pl.pallas_call(
        faces_kernel,
        grid_spec=pltpu.PrefetchScalarGridSpec(
            num_scalar_prefetch=1,
            grid=(NODES // BLOCK,),
            in_specs=[pl.BlockSpec((64, BLOCK), lambda i, f: (0, i))],
            out_specs=pl.BlockSpec((HFACE, LANES), lambda i, f: (0, 0)),
            scratch_shapes=[pltpu.VMEM((NODES, LANES), f32), pltpu.VMEM((FACE, LANES), f32)],
        ),
        out_shape=jax.ShapeDtypeStruct((HFACE, LANES), bf16),
        compiler_params=params(48),
        name="faces",
        cost_estimate=FREE,
    )(face, own)


def turn_kernel(core, own, other, potential, field, half, raised, start):
    step = pl.program_id(0)
    first = core[0] == 0
    low = jnp.where(first, own[...], other[...])
    high = jnp.where(first, other[...], own[...])
    block = jnp.concatenate([low, high], axis=0)
    field[...] = block.astype(bf16).T

    @pl.when(step // (HALF // BLOCK) == core[0])
    def _():
        half[...] = block.T
        for j in range(BLOCK // LANES):
            rows = pl.ds(j * LANES, LANES)
            row = potential[0, pl.ds(j, 1), :] - 6.0
            column = jnp.broadcast_to(row, (LANES, LANES)).T
            raised[rows, :] = column
            start[rows, :] = column * half[rows, :]


def turn(core, own, other, potential):
    half = pl.BlockSpec((BLOCK, LANES), lambda i, c: (jnp.clip(i - HALF // BLOCK * c[0], 0, HALF // BLOCK - 1), 0))
    return pl.pallas_call(
        turn_kernel,
        grid_spec=pltpu.PrefetchScalarGridSpec(
            num_scalar_prefetch=1,
            grid=(NODES // BLOCK,),
            in_specs=[pl.BlockSpec((64, BLOCK), lambda i, c: (0, i))] * 2
            + [pl.BlockSpec((1, BLOCK // LANES, LANES), lambda i, c: (i, 0, 0))],
            out_specs=[pl.BlockSpec((BLOCK, LANES), lambda i, c: (i, 0)), half, half, half],
        ),
        out_shape=[jax.ShapeDtypeStruct((NODES, LANES), bf16)]
        + [jax.ShapeDtypeStruct((HALF, LANES), f32)] * 3,
        compiler_params=params(60),
        name="turn",
        cost_estimate=FREE,
    )(core, own, other, potential.reshape(NODES // BLOCK, BLOCK // LANES, LANES))


def apply_kernel(
    second, core, cells, face, potential,
    index, field, start, matrix, ghosts, edge_mine, edge_other, back,
    kept, sent, edge_kept, edge_sent,
    x, g0, g1, p0, p1, stage, picked, *rest,
):
    accs = rest[:ACCS]
    ahead, behind, sems, slots = rest[ACCS : ACCS + 4], rest[ACCS + 4 : ACCS + 8], rest[-2], rest[-1]
    h = core[0]
    mine = pl.multiple_of(h * HALF, HALF)
    theirs = pl.multiple_of((1 - h) * HALF, HALF)
    load = pltpu.make_async_copy(start, accs[0].at[pl.ds(mine, HALF)], sems.at[0])
    copies = []
    for k in range(NODES // PIECE):
        ref, at = (field[0], k * PIECE) if len(field) == 1 else (field[k // 2], k % 2 * PIECE)
        copies.append(
            pltpu.make_async_copy(
                ref.at[pl.ds(at, PIECE)], stage.at[pl.ds(k * PIECE, PIECE)], sems.at[k + 1]
            )
        )
    for copy in copies:
        copy.start()
    load.start()

    def fetch(stage_number, cell):
        row = cell + 1
        a = pltpu.make_async_copy(index.at[row + 1], ahead[stage_number], slots.at[stage_number])
        b = pltpu.make_async_copy(index.at[row - 1], behind[stage_number], slots.at[4 + stage_number])
        return a, b

    for k in range(4):
        for copy in fetch(k, k):
            copy.start()

    zeros = jnp.zeros((256, LANES), f32)

    def clear(i, _):
        for a in accs[1:]:
            a[pl.ds(pl.multiple_of(i * 256, 256), 256), :] = zeros
        return 0

    lax.fori_loop(0, EXT // 256, clear, 0)

    def clear_first(i, _):
        accs[0][pl.ds(pl.multiple_of(theirs + i * 256, 256), 256), :] = zeros
        return 0

    lax.fori_loop(0, HALF // 256, clear_first, 0)
    accs[0][pl.ds(NODES, FACE), :] = jnp.zeros((FACE, LANES), f32)
    for ref in (x, *accs):
        ref[pl.ds(EXT, SPARE), :] = jnp.zeros((SPARE, LANES), f32)
    for ref in (g0, g1, p0, p1):
        ref[...] = jnp.zeros_like(ref)

    if second:
        for edge, part in ((edge_mine, h), (edge_other, 1 - h)):
            to = pl.multiple_of(NODES + part * HFACE, HFACE)
            x[pl.ds(to, HFACE), :] = edge[pl.ds(0, HFACE), :].astype(f32)
            picked[pl.ds(pl.multiple_of(part * HFACE, HFACE), HFACE), :] = edge[
                pl.ds(HFACE, HFACE), :
            ].astype(f32)
    else:
        first = core[0] == 0
        own, other = ghosts[0][...].astype(f32), ghosts[1][...].astype(f32)
        low, high = jnp.where(first, own, other), jnp.where(first, other, own)
        left = lax.broadcasted_iota(jnp.int32, (HFACE, LANES), 1) < 64
        x[pl.ds(NODES, HFACE), :] = jnp.where(left, low, pltpu.roll(high, 64, 1))
        x[pl.ds(NODES + HFACE, HFACE), :] = jnp.where(left, pltpu.roll(low, 64, 1), high)

    for k, copy in enumerate(copies):
        copy.wait()
        if second:
            base = (mine if k < 2 else theirs) + k % 2 * PIECE
        else:
            base = k * PIECE

        def widen(i, _, k=k, base=base):
            at = pl.multiple_of(k * PIECE + i * 256, 256)
            rows = pl.ds(pl.multiple_of(base + i * 256, 256), 256)
            x[rows, :] = stage[pl.ds(at, 256), :].astype(f32)
            return 0

        lax.fori_loop(0, PIECE // 256, widen, 0)
    load.wait()

    if second:

        def put(i, _):
            for k in range(16):
                at = i * 16 + k
                x[pl.ds(face[at], 1), :] = picked[pl.ds(at, 1), :]
            return 0

        lax.fori_loop(0, FACE // 16, put, 0)

        def shift(i, _):
            for j in range(0, 16, ACCS):
                at = [i * 16 + j + k for k in range(ACCS)]
                node = [face[h * HFACE + a] for a in at]
                gain = [(potential[n] - 6.0) * 0.25 for n in node]
                sums = [
                    accs[k][pl.ds(node[k], 1), :] + back[pl.ds(at[k], 1), :] * gain[k]
                    for k in range(ACCS)
                ]
                for k in range(ACCS):
                    accs[k][pl.ds(node[k], 1), :] = sums[k]
            return 0

        lax.fori_loop(0, HFACE // 16, shift, 0)

    def gather(g, nodes, lo, hi):
        for a in range(lo, min(hi, CELL_NODES)):
            g[pl.ds(a, 1), :] = x[pl.ds(nodes[a // LANES, a % LANES], 1), :]

    def scatter(p, nodes, lo, hi):
        for a in range(lo, min(hi, CELL_NODES), 2 * ACCS):
            count = min(2 * ACCS, CELL_NODES - a)
            at = [nodes[(a + k) // LANES, (a + k) % LANES] for k in range(count)]
            held = [accs[k % ACCS][pl.ds(at[k], 1), :] for k in range(count)]
            sums = []
            for k in range(count):
                if k >= ACCS:
                    held[k] = jnp.where(at[k] == at[k - ACCS], sums[k - ACCS], held[k])
                sums.append(held[k] + p[pl.ds(a + k, 1), :])
            for k in range(count):
                accs[k % ACCS][pl.ds(at[k], 1), :] = sums[k]

    def step(k, cell):
        g_now, g_next, p_now, p_last = (g0, g1, p0, p1) if k % 2 == 0 else (g1, g0, p1, p0)
        for copy in fetch(k, cell + k):
            copy.wait()
        p_now[...] = jnp.dot(matrix[...], g_now[...].astype(bf16), preferred_element_type=f32)
        for lo in range(0, CELL_NODES, 8):
            scatter(p_last, behind[k], lo, lo + 8)
            gather(g_next, ahead[k], lo, lo + 8)
        for copy in fetch(k, cell + 4 + k):
            copy.start()

    first = pltpu.make_async_copy(index.at[1], rest[ACCS + 8], slots.at[8])
    first.start()
    first.wait()
    gather(g0, rest[ACCS + 8], 0, CELL_NODES)

    def four(i, _):
        for k in range(4):
            step(k, 4 * i)
        return 0

    fours = (cells[0] + 3) // 4
    lax.fori_loop(0, fours, four, 0)
    for k in range(4):
        for copy in fetch(k, 4 * fours + k):
            copy.wait()
    scatter(p1, behind[0], 0, CELL_NODES)

    def total(begin, count):
        def add(i, _):
            rows = pl.ds(pl.multiple_of(begin + i * 256, 256), 256)
            accs[0][rows, :] = (accs[0][rows, :] + accs[1][rows, :]) + (
                accs[2][rows, :] + accs[3][rows, :]
            )
            return 0

        lax.fori_loop(0, count // 256, add, 0)

    writes = []

    def write(source, target):
        writes.append(pltpu.make_async_copy(source, target, sems.at[len(writes)]))
        writes[-1].start()

    for begin, target in ((theirs, sent), (mine, kept)):
        for at in range(0, HALF, PIECE):
            total(begin + at, PIECE)
            write(
                accs[0].at[pl.ds(pl.multiple_of(begin + at, PIECE), PIECE)],
                target.at[pl.ds(at, PIECE)],
            )
    total(NODES, FACE)

    def pick(i, _):
        for k in range(16):
            at = i * 16 + k
            picked[pl.ds(at, 1), :] = accs[0][pl.ds(face[at], 1), :]
        return 0

    lax.fori_loop(0, FACE // 16, pick, 0)
    for part, target in ((1 - h, edge_sent), (h, edge_kept)):
        ghost = pl.multiple_of(NODES + part * HFACE, HFACE)
        write(accs[0].at[pl.ds(ghost, HFACE)], target.at[pl.ds(0, HFACE)])
        own = pl.multiple_of(part * HFACE, HFACE)
        write(picked.at[pl.ds(own, HFACE)], target.at[pl.ds(HFACE, HFACE)])
    for w in writes:
        w.wait()


def first_kernel(core, cells, face, potential, index, field, start, matrix, own, other, *rest):
    apply_kernel(
        False, core, cells, face, potential, index,
        (field,), start, matrix, (own, other), None, None, None, *rest,
    )


def second_kernel(
    core, cells, face, potential, index, mine, theirs, start, matrix,
    edge_mine, edge_other, back, *rest,
):
    apply_kernel(
        True, core, cells, face, potential, index,
        (mine, theirs), start, matrix, None, edge_mine, edge_other, back, *rest,
    )


def apply(kernel, fields, edges, *operands):
    edge = jax.ShapeDtypeStruct((FACE, LANES), f32)
    half = jax.ShapeDtypeStruct((HALF, LANES), f32)
    return pl.pallas_call(
        kernel,
        in_specs=[SMEM] * 4 + [ANY] * (2 + fields) + [VMEM] * (1 + edges),
        out_specs=[ANY] * 4,
        scratch_shapes=[pltpu.VMEM((EXT + SPARE, LANES), f32)]
        + [pltpu.VMEM((MAT, LANES), f32)] * 4
        + [pltpu.VMEM((NODES, LANES), bf16), pltpu.VMEM((FACE, LANES), f32)]
        + [pltpu.VMEM((EXT + SPARE, LANES), f32)] * ACCS
        + [pltpu.SMEM((8, LANES), jnp.int32)] * 9
        + [pltpu.SemaphoreType.DMA((8,)), pltpu.SemaphoreType.DMA((9,))],
        out_shape=[half, half, edge, edge],
        compiler_params=params(61),
        name="apply",
    )(*operands)


def finish_kernel(core, face, kept, came, back_mine, back_other, mine, theirs, sums):
    def add(i, _):
        rows = pl.ds(pl.multiple_of(i * 256, 256), 256)
        sums[rows, :] = (kept[rows, :] + came[rows, :]) * 0.5
        return 0

    lax.fori_loop(0, HALF // 256, add, 0)
    sums[pl.ds(HALF, SPARE), :] = jnp.zeros((SPARE, LANES), f32)
    base = core[0] * HALF
    for back, part in ((back_mine, core[0]), (back_other, 1 - core[0])):

        def put(i, _, back=back, part=part):
            for k in range(8):
                at = i * 8 + k
                node = face[part * HFACE + at] - base
                node = jnp.where((node >= 0) & (node < HALF), node, HALF)
                sums[pl.ds(node, 1), :] += back[pl.ds(at, 1), :] * 0.5
            return 0

        lax.fori_loop(0, HFACE // 8, put, 0)

    def out(i, _):
        rows = pl.ds(pl.multiple_of(i * 256, 256), 256)
        block = sums[rows, :].T
        mine[:, rows] = jnp.where(core[0] == 0, block[:64], block[64:])
        theirs[:, rows] = jnp.where(core[0] == 0, block[64:], block[:64])
        return 0

    lax.fori_loop(0, HALF // 256, out, 0)


def finish(core, face, kept, came, back_mine, back_other):
    return pl.pallas_call(
        finish_kernel,
        in_specs=[SMEM] * 2 + [VMEM] * 4,
        out_specs=[VMEM] * 2,
        scratch_shapes=[pltpu.VMEM((HALF + SPARE, LANES), f32)],
        out_shape=[jax.ShapeDtypeStruct((64, HALF), f32)] * 2,
        compiler_params=params(60),
        name="finish",
        cost_estimate=FREE,
    )(core, face, kept, came, back_mine, back_other)


def place_kernel(core, mine, theirs, out):
    out[...] = jnp.where(pl.program_id(0) // (HALF // BLOCK) == core[0], mine[...], theirs[...])


def assemble(core, mine, theirs):
    last = HALF // BLOCK - 1
    return pl.pallas_call(
        place_kernel,
        grid_spec=pltpu.PrefetchScalarGridSpec(
            num_scalar_prefetch=1,
            grid=(NODES // BLOCK,),
            in_specs=[
                pl.BlockSpec((64, BLOCK), lambda i, c: (0, jnp.clip(i - (last + 1) * c[0], 0, last))),
                pl.BlockSpec((64, BLOCK), lambda i, c: (0, jnp.clip(i - (last + 1) * (1 - c[0]), 0, last))),
            ],
            out_specs=pl.BlockSpec((64, BLOCK), lambda i, c: (0, i)),
        ),
        out_shape=jax.ShapeDtypeStruct((64, NODES), f32),
        compiler_params=params(40),
        name="place",
        cost_estimate=FREE,
    )(core, mine, theirs)


def weigh_kernel(place, face, weights, own, out, rows):
    for j in range(SHARE // LANES):
        row = jnp.broadcast_to(own[pl.ds(j, 1), :], (LANES, LANES))
        rows[pl.ds(j * LANES, LANES), :] = row.T
    zero = jnp.zeros((1, LANES), f32)

    def drop(i, _):
        for k in range(8):
            node = face[i * 8 + k] - place[0]
            node = jnp.where((node >= 0) & (node < SHARE), node, SHARE)
            rows[pl.ds(node, 1), :] = zero
        return 0

    lax.fori_loop(0, FACE // 8, drop, 0)
    out[pl.ds(0, SHARE), :] = rows[pl.ds(0, SHARE), :]

    def add(i, _):
        for k in range(8):
            at = i * 8 + k
            out[pl.ds(SHARE + at, 1), :] = jnp.full((1, LANES), weights[face[place[1] + at]], f32)
        return 0

    lax.fori_loop(0, FSHARE // 8, add, 0)


def weigh(place, face, weights, own):
    return pl.pallas_call(
        weigh_kernel,
        in_specs=[SMEM] * 3 + [VMEM],
        out_specs=VMEM,
        scratch_shapes=[pltpu.VMEM((SHARE + SPARE, LANES), f32)],
        out_shape=jax.ShapeDtypeStruct((SHARE + FSHARE, LANES), f32),
        compiler_params=params(60),
        name="weigh",
        cost_estimate=FREE,
    )(place, face, weights, own.reshape(SHARE // LANES, LANES))


def outgoing_kernel(kept, came, edge, back, out):
    out[0, pl.ds(0, SHARE), :] = ((kept[...] + came[...]) * 0.5).astype(bf16)
    out[0, pl.ds(SHARE, FSHARE), :] = ((edge[...] + back[...]) * 0.5).astype(bf16)


def outgoing(kept, came, edge, back):
    nodes = pl.BlockSpec((SHARE, LANES), lambda i: (i, 0))
    faces = pl.BlockSpec((FSHARE, LANES), lambda i: (i, 0))
    return pl.pallas_call(
        outgoing_kernel,
        grid=(8,),
        in_specs=[nodes, nodes, faces, faces],
        out_specs=pl.BlockSpec((1, SHARE + FSHARE, LANES), lambda i: (i, 0, 0)),
        out_shape=jax.ShapeDtypeStruct((8, SHARE + FSHARE, LANES), bf16),
        compiler_params=params(40),
        name="outgoing",
        cost_estimate=FREE,
    )(kept, came, edge, back)


def gram_kernel(nodes, weights, out, everyone):
    for q in range(8):
        lanes = pl.ds(q * LANES, LANES)
        everyone[:, lanes] = nodes[q]

    def rows(q, _):
        at = pl.multiple_of(q * LANES, LANES)
        block = everyone[:, pl.ds(at, LANES)].astype(f32)
        scaled = (weights[...] * block).T.astype(bf16)
        product = jnp.dot(scaled, everyone[...], preferred_element_type=f32)
        out[pl.ds(at, LANES), :] = product.astype(bf16)
        return 0

    lax.fori_loop(0, 8, rows, 0)


def gram_rows(nodes, weights):
    return pl.pallas_call(
        gram_kernel,
        in_specs=[VMEM] * 2,
        out_specs=VMEM,
        scratch_shapes=[pltpu.VMEM((SHARE + FSHARE, 1024), bf16)],
        out_shape=jax.ShapeDtypeStruct((1024, 1024), bf16),
        compiler_params=params(40),
        name="gram",
    )(nodes, weights)


def across_chips(block):
    groups = [list(range(0, 16, 2)), list(range(1, 16, 2))]
    return lax.all_to_all(block, "band", 0, 0, axis_index_groups=groups, tiled=True)


def sum_everywhere(partial):
    parts = lax.all_to_all(partial.reshape(128, 8, 1024), ("band", "dom"), 0, 0, tiled=True)
    part = jnp.sum(parts.astype(f32), axis=0)
    copies = jnp.broadcast_to(part[None], (8, 8, 1024))
    return lax.all_to_all(copies, "dom", 0, 0, tiled=True).reshape(64, 1024)


def body(states, cell_matrix, potential, weights, connectivity, face_nodes, cell_counts):
    band = lax.axis_index("band")
    chip = band // 2
    h = band % 2
    core = h.astype(jnp.int32).reshape(1)

    other = to_mate(states)
    own_cells = lax.dynamic_index_in_dim(
        connectivity.reshape(CELL_NODES, CELLS, 2), h, 2, keepdims=False
    )
    cells = (cell_counts - h + 1) // 2
    live = jnp.arange(CELLS) < cells[0]
    index = jnp.where(live[:, None], own_cells.T, EXT)
    index = jnp.pad(index, ((1, ROWS - 1 - CELLS), (0, 1024 - CELL_NODES)), constant_values=EXT)
    index = index.reshape(ROWS, 8, LANES)
    matrix = jnp.pad(cell_matrix, ((0, MAT - CELL_NODES),) * 2)
    faces = own_faces(face_nodes, states)
    ghosts = along_dom(faces, -1)
    ghosts_other = along_dom_crossed(faces, -1)
    field, half, raised, start = turn(core, states, other, potential)
    scalars = (core, cells, face_nodes, potential, index)
    kept, sent, edge_kept, edge_sent = apply(
        first_kernel, 1, 2, *scalars, field, start, matrix, ghosts, ghosts_other
    )
    edge = edge_kept + to_mate(edge_sent)
    came = to_mate(sent)
    rounded = ((kept + came) * 0.25).astype(bf16)
    back = along_dom(edge_kept[:HFACE], 1) + along_dom_crossed(edge_sent[:HFACE], 1)
    ahead = along_dom(edge_kept[HFACE:], -1) + along_dom_crossed(edge_sent[HFACE:], -1)
    theirs = to_mate(rounded)
    kept, came, _ = lax.optimization_barrier((kept, came, rounded))
    start = raised * ((kept + came) * 0.25) - 2.0 * half
    back, ahead, start = lax.optimization_barrier((back, ahead, start))
    inner = (lax.axis_index("dom") < 7).astype(f32)
    edge_mine = jnp.concatenate([(edge[:HFACE] + ahead) * inner, edge[HFACE:] + back])
    edge_mine = (edge_mine * 0.25).astype(bf16)
    edge_other = to_mate(edge_mine)
    kept, sent, edge_kept, edge_sent = apply(
        second_kernel, 2, 3, *scalars, rounded, theirs, start, matrix, edge_mine, edge_other, back
    )
    edge = edge_kept + to_mate(edge_sent)
    came = to_mate(sent)
    back = along_dom(edge_kept[:HFACE], 1) + along_dom_crossed(edge_sent[:HFACE], 1)
    everyone = across_chips(outgoing(kept, came, edge[HFACE:], back))

    begin = h * HALF + chip * SHARE
    place = jnp.stack([begin, h * HFACE + chip * FSHARE]).astype(jnp.int32)
    own = lax.dynamic_slice(weights, (begin,), (SHARE,))
    partial = gram_rows(everyone, weigh(place, face_nodes, weights, own))
    kept, came, back, back_other, partial = lax.optimization_barrier(
        (kept, came, back, to_mate(back), partial)
    )
    mine, theirs = finish(core, face_nodes, kept, came, back, back_other)
    filtered = assemble(core, mine, to_mate(theirs))
    return filtered, sum_everywhere(partial)


def solution(mesh):
    in_specs = (P("band", "dom"), P(), P("dom"), P("dom"), P(None, "dom"), P("dom"), P("dom"))
    out_specs = (P("band", "dom"), P("band", None))
    return jax.shard_map(body, mesh=mesh, in_specs=in_specs, out_specs=out_specs, check_vma=False)
```

```python
import functools

import jax
import jax.numpy as jnp
from jax import lax
from jax.experimental import pallas as pl
from jax.experimental.pallas import tpu as pltpu
from jax.sharding import PartitionSpec as P

NODES = 18432
HALF = 9216
FACE = 1536
HFACE = 768
EXT = NODES + FACE
CELL_NODES = 343
CELLS = 64
ROWS = 70
MAT = 352
LANES = 128
ACCS = 4
SPARE = 8
SHARE = HALF // 8
FSHARE = HFACE // 8
BLOCK = 3072
PIECE = 4608
VMEM = pl.BlockSpec(memory_space=pltpu.VMEM)
SMEM = pl.BlockSpec(memory_space=pltpu.SMEM)
ANY = pl.BlockSpec(memory_space=pl.ANY)
f32 = jnp.float32
bf16 = jnp.bfloat16


def to_mate(block):
    return lax.ppermute(block, "band", [(i, i ^ 1) for i in range(16)])


def along_dom(block, shift):
    return lax.ppermute(block, "dom", [(i, i + shift) for i in range(8) if 0 <= i + shift < 8])


def along_dom_crossed(block, shift):
    pairs = [(i, i + shift, j) for i in range(8) for j in range(16) if 0 <= i + shift < 8]
    route = [(i * 16 + (j ^ 1), to * 16 + j) for i, to, j in pairs]
    return lax.ppermute(block, ("dom", "band"), route)


FREE = pl.CostEstimate(flops=0, bytes_accessed=0, transcendentals=0)


def params(mib):
    return pltpu.CompilerParams(vmem_limit_bytes=mib * 2**20)


def eye():
    rows = lax.broadcasted_iota(jnp.int32, (LANES, LANES), 0)
    return jnp.where(rows == lax.broadcasted_iota(jnp.int32, (LANES, LANES), 1), 1.0, 0.0).astype(bf16)


def turned_by(unit, block):
    return lax.dot_general(unit, block, (((1,), (1,)), ((), ())), preferred_element_type=f32)


def faces_kernel(face, own, out, whole, picked):
    step = pl.program_id(0)
    unit = eye()
    block = own[...].astype(bf16)
    for j in range(BLOCK // LANES):
        rows = pl.ds(pl.multiple_of(step * BLOCK + j * LANES, LANES), LANES)
        whole[rows, pl.ds(0, 64)] = turned_by(unit, block[:, j * LANES : (j + 1) * LANES])

    @pl.when(step == NODES // BLOCK - 1)
    def _():
        def pick(i, _):
            for k in range(16):
                at = i * 16 + k
                picked[pl.ds(at, 1), :] = whole[pl.ds(face[at], 1), :]
            return 0

        lax.fori_loop(0, FACE // 16, pick, 0)
        left = lax.broadcasted_iota(jnp.int32, (HFACE, LANES), 1) < 64
        right = pltpu.roll(picked[pl.ds(HFACE, HFACE), :], 64, 1)
        out[...] = jnp.where(left, picked[pl.ds(0, HFACE), :], right).astype(bf16)


def own_faces(face, own):
    return pl.pallas_call(
        faces_kernel,
        grid_spec=pltpu.PrefetchScalarGridSpec(
            num_scalar_prefetch=1,
            grid=(NODES // BLOCK,),
            in_specs=[pl.BlockSpec((64, BLOCK), lambda i, f: (0, i))],
            out_specs=pl.BlockSpec((HFACE, LANES), lambda i, f: (0, 0)),
            scratch_shapes=[pltpu.VMEM((NODES, LANES), f32), pltpu.VMEM((FACE, LANES), f32)],
        ),
        out_shape=jax.ShapeDtypeStruct((HFACE, LANES), bf16),
        compiler_params=params(48),
        name="faces",
        cost_estimate=FREE,
    )(face, own)


def turn_kernel(core, own, other, potential, field, half, raised, start):
    step = pl.program_id(0)
    first = core[0] == 0
    low = jnp.where(first, own[...], other[...])
    high = jnp.where(first, other[...], own[...])
    block = jnp.concatenate([low, high], axis=0)
    field[...] = block.astype(bf16).T

    @pl.when(step // (HALF // BLOCK) == core[0])
    def _():
        half[...] = block.T
        for j in range(BLOCK // LANES):
            rows = pl.ds(j * LANES, LANES)
            row = potential[0, pl.ds(j, 1), :] - 6.0
            column = jnp.broadcast_to(row, (LANES, LANES)).T
            raised[rows, :] = column
            start[rows, :] = column * half[rows, :]


def turn(core, own, other, potential):
    half = pl.BlockSpec((BLOCK, LANES), lambda i, c: (jnp.clip(i - HALF // BLOCK * c[0], 0, HALF // BLOCK - 1), 0))
    return pl.pallas_call(
        turn_kernel,
        grid_spec=pltpu.PrefetchScalarGridSpec(
            num_scalar_prefetch=1,
            grid=(NODES // BLOCK,),
            in_specs=[pl.BlockSpec((64, BLOCK), lambda i, c: (0, i))] * 2
            + [pl.BlockSpec((1, BLOCK // LANES, LANES), lambda i, c: (i, 0, 0))],
            out_specs=[pl.BlockSpec((BLOCK, LANES), lambda i, c: (i, 0)), half, half, half],
        ),
        out_shape=[jax.ShapeDtypeStruct((NODES, LANES), bf16)]
        + [jax.ShapeDtypeStruct((HALF, LANES), f32)] * 3,
        compiler_params=params(60),
        name="turn",
        cost_estimate=FREE,
    )(core, own, other, potential.reshape(NODES // BLOCK, BLOCK // LANES, LANES))


def apply_kernel(
    second, core, cells, face, potential,
    index, field, start, matrix, ghosts, edge_mine, edge_other, back,
    kept, sent, edge_kept, edge_sent,
    x, g0, g1, p0, p1, stage, picked, *rest,
):
    accs = rest[:ACCS]
    ahead, behind, sems, slots = rest[ACCS : ACCS + 4], rest[ACCS + 4 : ACCS + 8], rest[-2], rest[-1]
    h = core[0]
    mine = pl.multiple_of(h * HALF, HALF)
    theirs = pl.multiple_of((1 - h) * HALF, HALF)
    load = pltpu.make_async_copy(start, accs[0].at[pl.ds(mine, HALF)], sems.at[0])
    copies = []
    for k in range(NODES // PIECE):
        ref, at = (field[0], k * PIECE) if len(field) == 1 else (field[k // 2], k % 2 * PIECE)
        copies.append(
            pltpu.make_async_copy(
                ref.at[pl.ds(at, PIECE)], stage.at[pl.ds(k * PIECE, PIECE)], sems.at[k + 1]
            )
        )
    for copy in copies:
        copy.start()
    load.start()

    def fetch(stage_number, cell):
        row = cell + 1
        a = pltpu.make_async_copy(index.at[row + 1], ahead[stage_number], slots.at[stage_number])
        b = pltpu.make_async_copy(index.at[row - 1], behind[stage_number], slots.at[4 + stage_number])
        return a, b

    for k in range(4):
        for copy in fetch(k, k):
            copy.start()

    zeros = jnp.zeros((256, LANES), f32)

    def clear(i, _):
        for a in accs[1:]:
            a[pl.ds(pl.multiple_of(i * 256, 256), 256), :] = zeros
        return 0

    lax.fori_loop(0, EXT // 256, clear, 0)

    def clear_first(i, _):
        accs[0][pl.ds(pl.multiple_of(theirs + i * 256, 256), 256), :] = zeros
        return 0

    lax.fori_loop(0, HALF // 256, clear_first, 0)
    accs[0][pl.ds(NODES, FACE), :] = jnp.zeros((FACE, LANES), f32)
    for ref in (x, *accs):
        ref[pl.ds(EXT, SPARE), :] = jnp.zeros((SPARE, LANES), f32)
    for ref in (g0, g1, p0, p1):
        ref[...] = jnp.zeros_like(ref)

    if second:
        for edge, part in ((edge_mine, h), (edge_other, 1 - h)):
            to = pl.multiple_of(NODES + part * HFACE, HFACE)
            x[pl.ds(to, HFACE), :] = edge[pl.ds(0, HFACE), :].astype(f32)
            picked[pl.ds(pl.multiple_of(part * HFACE, HFACE), HFACE), :] = edge[
                pl.ds(HFACE, HFACE), :
            ].astype(f32)
    else:
        first = core[0] == 0
        own, other = ghosts[0][...].astype(f32), ghosts[1][...].astype(f32)
        low, high = jnp.where(first, own, other), jnp.where(first, other, own)
        left = lax.broadcasted_iota(jnp.int32, (HFACE, LANES), 1) < 64
        x[pl.ds(NODES, HFACE), :] = jnp.where(left, low, pltpu.roll(high, 64, 1))
        x[pl.ds(NODES + HFACE, HFACE), :] = jnp.where(left, pltpu.roll(low, 64, 1), high)

    for k, copy in enumerate(copies):
        copy.wait()
        if second:
            base = (mine if k < 2 else theirs) + k % 2 * PIECE
        else:
            base = k * PIECE

        def widen(i, _, k=k, base=base):
            at = pl.multiple_of(k * PIECE + i * 256, 256)
            rows = pl.ds(pl.multiple_of(base + i * 256, 256), 256)
            x[rows, :] = stage[pl.ds(at, 256), :].astype(f32)
            return 0

        lax.fori_loop(0, PIECE // 256, widen, 0)
    load.wait()

    if second:

        def put(i, _):
            for k in range(16):
                at = i * 16 + k
                x[pl.ds(face[at], 1), :] = picked[pl.ds(at, 1), :]
            return 0

        lax.fori_loop(0, FACE // 16, put, 0)

        picked[pl.ds(0, HFACE), :] = back[...].astype(f32)

        def shift(i, _):
            for j in range(0, 16, ACCS):
                at = [i * 16 + j + k for k in range(ACCS)]
                node = [face[h * HFACE + a] for a in at]
                gain = [(potential[n] - 6.0) * 0.25 for n in node]
                sums = [
                    accs[k][pl.ds(node[k], 1), :] + picked[pl.ds(at[k], 1), :] * gain[k]
                    for k in range(ACCS)
                ]
                for k in range(ACCS):
                    accs[k][pl.ds(node[k], 1), :] = sums[k]
            return 0

        lax.fori_loop(0, HFACE // 16, shift, 0)

    def gather(g, nodes, lo, hi):
        for a in range(lo, min(hi, CELL_NODES)):
            g[pl.ds(a, 1), :] = x[pl.ds(nodes[a // LANES, a % LANES], 1), :]

    def scatter(p, nodes, lo, hi):
        for a in range(lo, min(hi, CELL_NODES), 2 * ACCS):
            count = min(2 * ACCS, CELL_NODES - a)
            at = [nodes[(a + k) // LANES, (a + k) % LANES] for k in range(count)]
            held = [accs[k % ACCS][pl.ds(at[k], 1), :] for k in range(count)]
            sums = []
            for k in range(count):
                if k >= ACCS:
                    held[k] = jnp.where(at[k] == at[k - ACCS], sums[k - ACCS], held[k])
                sums.append(held[k] + p[pl.ds(a + k, 1), :])
            for k in range(count):
                accs[k % ACCS][pl.ds(at[k], 1), :] = sums[k]

    def step(k, cell):
        g_now, g_next, p_now, p_last = (g0, g1, p0, p1) if k % 2 == 0 else (g1, g0, p1, p0)
        for copy in fetch(k, cell + k):
            copy.wait()
        p_now[...] = jnp.dot(matrix[...], g_now[...].astype(bf16), preferred_element_type=f32)
        for lo in range(0, CELL_NODES, 8):
            scatter(p_last, behind[k], lo, lo + 8)
            gather(g_next, ahead[k], lo, lo + 8)
        for copy in fetch(k, cell + 4 + k):
            copy.start()

    first = pltpu.make_async_copy(index.at[1], rest[ACCS + 8], slots.at[8])
    first.start()
    first.wait()
    gather(g0, rest[ACCS + 8], 0, CELL_NODES)

    def four(i, _):
        for k in range(4):
            step(k, 4 * i)
        return 0

    fours = (cells[0] + 3) // 4
    lax.fori_loop(0, fours, four, 0)
    for k in range(4):
        for copy in fetch(k, 4 * fours + k):
            copy.wait()
    scatter(p1, behind[0], 0, CELL_NODES)

    def total(begin, count):
        def add(i, _):
            rows = pl.ds(pl.multiple_of(begin + i * 256, 256), 256)
            accs[0][rows, :] = (accs[0][rows, :] + accs[1][rows, :]) + (
                accs[2][rows, :] + accs[3][rows, :]
            )
            return 0

        lax.fori_loop(0, count // 256, add, 0)

    writes = []

    def write(source, target):
        writes.append(pltpu.make_async_copy(source, target, sems.at[len(writes)]))
        writes[-1].start()

    for begin, target in ((theirs, sent), (mine, kept)):
        for at in range(0, HALF, PIECE):
            total(begin + at, PIECE)
            write(
                accs[0].at[pl.ds(pl.multiple_of(begin + at, PIECE), PIECE)],
                target.at[pl.ds(at, PIECE)],
            )
    total(NODES, FACE)

    def pick(i, _):
        for k in range(16):
            at = i * 16 + k
            picked[pl.ds(at, 1), :] = accs[0][pl.ds(face[at], 1), :]
        return 0

    lax.fori_loop(0, FACE // 16, pick, 0)
    for part, target in ((1 - h, edge_sent), (h, edge_kept)):
        ghost = pl.multiple_of(NODES + part * HFACE, HFACE)
        write(accs[0].at[pl.ds(ghost, HFACE)], target.at[pl.ds(0, HFACE)])
        own = pl.multiple_of(part * HFACE, HFACE)
        write(picked.at[pl.ds(own, HFACE)], target.at[pl.ds(HFACE, HFACE)])
    for w in writes:
        w.wait()


def first_kernel(core, cells, face, potential, index, field, start, matrix, own, other, *rest):
    apply_kernel(
        False, core, cells, face, potential, index,
        (field,), start, matrix, (own, other), None, None, None, *rest,
    )


def second_kernel(
    core, cells, face, potential, index, mine, theirs, start, matrix,
    edge_mine, edge_other, back, *rest,
):
    apply_kernel(
        True, core, cells, face, potential, index,
        (mine, theirs), start, matrix, None, edge_mine, edge_other, back, *rest,
    )


def apply(kernel, fields, edges, *operands):
    edge = jax.ShapeDtypeStruct((FACE, LANES), f32)
    half = jax.ShapeDtypeStruct((HALF, LANES), f32)
    return pl.pallas_call(
        kernel,
        in_specs=[SMEM] * 4 + [ANY] * (2 + fields) + [VMEM] * (1 + edges),
        out_specs=[ANY] * 4,
        scratch_shapes=[pltpu.VMEM((EXT + SPARE, LANES), f32)]
        + [pltpu.VMEM((MAT, LANES), f32)] * 4
        + [pltpu.VMEM((NODES, LANES), bf16), pltpu.VMEM((FACE, LANES), f32)]
        + [pltpu.VMEM((EXT + SPARE, LANES), f32)] * ACCS
        + [pltpu.SMEM((8, LANES), jnp.int32)] * 9
        + [pltpu.SemaphoreType.DMA((8,)), pltpu.SemaphoreType.DMA((9,))],
        out_shape=[half, half, edge, edge],
        compiler_params=params(61),
        name="apply",
    )(*operands)


def finish_kernel(core, face, kept, came, back_mine, back_other, mine, theirs, sums, wide):
    def add(i, _):
        rows = pl.ds(pl.multiple_of(i * 256, 256), 256)
        sums[rows, :] = (kept[rows, :] + came[rows, :]) * 0.5
        return 0

    lax.fori_loop(0, HALF // 256, add, 0)
    sums[pl.ds(HALF, SPARE), :] = jnp.zeros((SPARE, LANES), f32)
    base = core[0] * HALF
    for back, part in ((back_mine, core[0]), (back_other, 1 - core[0])):
        wide[...] = back[...].astype(f32)

        def put(i, _, part=part):
            for k in range(8):
                at = i * 8 + k
                node = face[part * HFACE + at] - base
                node = jnp.where((node >= 0) & (node < HALF), node, HALF)
                sums[pl.ds(node, 1), :] += wide[pl.ds(at, 1), :] * 0.5
            return 0

        lax.fori_loop(0, HFACE // 8, put, 0)

    def out(i, _):
        rows = pl.ds(pl.multiple_of(i * 256, 256), 256)
        block = sums[rows, :].T
        mine[:, rows] = jnp.where(core[0] == 0, block[:64], block[64:])
        theirs[:, rows] = jnp.where(core[0] == 0, block[64:], block[:64])
        return 0

    lax.fori_loop(0, HALF // 256, out, 0)


def finish(core, face, kept, came, back_mine, back_other):
    return pl.pallas_call(
        finish_kernel,
        in_specs=[SMEM] * 2 + [VMEM] * 4,
        out_specs=[VMEM] * 2,
        scratch_shapes=[pltpu.VMEM((HALF + SPARE, LANES), f32), pltpu.VMEM((HFACE, LANES), f32)],
        out_shape=[jax.ShapeDtypeStruct((64, HALF), f32)] * 2,
        compiler_params=params(60),
        name="finish",
        cost_estimate=FREE,
    )(core, face, kept, came, back_mine, back_other)


def place_kernel(core, mine, theirs, out):
    out[...] = jnp.where(pl.program_id(0) // (HALF // BLOCK) == core[0], mine[...], theirs[...])


def assemble(core, mine, theirs):
    last = HALF // BLOCK - 1
    return pl.pallas_call(
        place_kernel,
        grid_spec=pltpu.PrefetchScalarGridSpec(
            num_scalar_prefetch=1,
            grid=(NODES // BLOCK,),
            in_specs=[
                pl.BlockSpec((64, BLOCK), lambda i, c: (0, jnp.clip(i - (last + 1) * c[0], 0, last))),
                pl.BlockSpec((64, BLOCK), lambda i, c: (0, jnp.clip(i - (last + 1) * (1 - c[0]), 0, last))),
            ],
            out_specs=pl.BlockSpec((64, BLOCK), lambda i, c: (0, i)),
        ),
        out_shape=jax.ShapeDtypeStruct((64, NODES), f32),
        compiler_params=params(40),
        name="place",
        cost_estimate=FREE,
    )(core, mine, theirs)


def weigh_kernel(place, face, weights, own, out, rows):
    for j in range(SHARE // LANES):
        row = jnp.broadcast_to(own[pl.ds(j, 1), :], (LANES, LANES))
        rows[pl.ds(j * LANES, LANES), :] = row.T
    zero = jnp.zeros((1, LANES), f32)

    def drop(i, _):
        for k in range(8):
            node = face[i * 8 + k] - place[0]
            node = jnp.where((node >= 0) & (node < SHARE), node, SHARE)
            rows[pl.ds(node, 1), :] = zero
        return 0

    lax.fori_loop(0, FACE // 8, drop, 0)
    out[pl.ds(0, SHARE), :] = rows[pl.ds(0, SHARE), :]

    def add(i, _):
        for k in range(8):
            at = i * 8 + k
            out[pl.ds(SHARE + at, 1), :] = jnp.full((1, LANES), weights[face[place[1] + at]], f32)
        return 0

    lax.fori_loop(0, FSHARE // 8, add, 0)


def weigh(place, face, weights, own):
    return pl.pallas_call(
        weigh_kernel,
        in_specs=[SMEM] * 3 + [VMEM],
        out_specs=VMEM,
        scratch_shapes=[pltpu.VMEM((SHARE + SPARE, LANES), f32)],
        out_shape=jax.ShapeDtypeStruct((SHARE + FSHARE, LANES), f32),
        compiler_params=params(60),
        name="weigh",
        cost_estimate=FREE,
    )(place, face, weights, own.reshape(SHARE // LANES, LANES))


def outgoing_kernel(kept, came, edge, back, out):
    out[0, pl.ds(0, SHARE), :] = ((kept[...] + came[...]) * 0.5).astype(bf16)
    out[0, pl.ds(SHARE, FSHARE), :] = ((edge[...] + back[...].astype(f32)) * 0.5).astype(bf16)


def outgoing(kept, came, edge, back):
    nodes = pl.BlockSpec((SHARE, LANES), lambda i: (i, 0))
    faces = pl.BlockSpec((FSHARE, LANES), lambda i: (i, 0))
    return pl.pallas_call(
        outgoing_kernel,
        grid=(8,),
        in_specs=[nodes, nodes, faces, faces],
        out_specs=pl.BlockSpec((1, SHARE + FSHARE, LANES), lambda i: (i, 0, 0)),
        out_shape=jax.ShapeDtypeStruct((8, SHARE + FSHARE, LANES), bf16),
        compiler_params=params(40),
        name="outgoing",
        cost_estimate=FREE,
    )(kept, came, edge, back)


def gram_kernel(nodes, weights, out, everyone):
    for q in range(8):
        lanes = pl.ds(q * LANES, LANES)
        everyone[:, lanes] = nodes[q]

    def rows(q, _):
        at = pl.multiple_of(q * LANES, LANES)
        block = everyone[:, pl.ds(at, LANES)].astype(f32)
        scaled = (weights[...] * block).T.astype(bf16)
        product = jnp.dot(scaled, everyone[...], preferred_element_type=f32)
        out[pl.ds(at, LANES), :] = product.astype(bf16)
        return 0

    lax.fori_loop(0, 8, rows, 0)


def gram_rows(nodes, weights):
    return pl.pallas_call(
        gram_kernel,
        in_specs=[VMEM] * 2,
        out_specs=VMEM,
        scratch_shapes=[pltpu.VMEM((SHARE + FSHARE, 1024), bf16)],
        out_shape=jax.ShapeDtypeStruct((1024, 1024), bf16),
        compiler_params=params(40),
        name="gram",
    )(nodes, weights)


def across_chips(block):
    groups = [list(range(0, 16, 2)), list(range(1, 16, 2))]
    return lax.all_to_all(block, "band", 0, 0, axis_index_groups=groups, tiled=True)


def sum_everywhere(partial, filtered):
    parts = lax.all_to_all(partial.reshape(128, 8, 1024), ("band", "dom"), 0, 0, tiled=True)
    parts, filtered = lax.optimization_barrier((parts, filtered))
    part = jnp.sum(parts.astype(f32), axis=0)
    copies = jnp.broadcast_to(part[None], (8, 8, 1024))
    return filtered, lax.all_to_all(copies, "dom", 0, 0, tiled=True).reshape(64, 1024)


def body(states, cell_matrix, potential, weights, connectivity, face_nodes, cell_counts):
    band = lax.axis_index("band")
    chip = band // 2
    h = band % 2
    core = h.astype(jnp.int32).reshape(1)

    other = to_mate(states)
    own_cells = lax.dynamic_index_in_dim(
        connectivity.reshape(CELL_NODES, CELLS, 2), h, 2, keepdims=False
    )
    cells = (cell_counts - h + 1) // 2
    live = jnp.arange(CELLS) < cells[0]
    index = jnp.where(live[:, None], own_cells.T, EXT)
    index = jnp.pad(index, ((1, ROWS - 1 - CELLS), (0, 1024 - CELL_NODES)), constant_values=EXT)
    index = index.reshape(ROWS, 8, LANES)
    matrix = jnp.pad(cell_matrix, ((0, MAT - CELL_NODES),) * 2)
    faces = own_faces(face_nodes, states)
    ghosts = along_dom(faces, -1)
    ghosts_other = along_dom_crossed(faces, -1)
    field, half, raised, start = turn(core, states, other, potential)
    scalars = (core, cells, face_nodes, potential, index)
    kept, sent, edge_kept, edge_sent = apply(
        first_kernel, 1, 2, *scalars, field, start, matrix, ghosts, ghosts_other
    )
    edge = edge_kept + to_mate(edge_sent)
    sent, edge = lax.optimization_barrier((sent, edge))
    came = to_mate(sent)
    rounded = ((kept + came) * 0.25).astype(bf16)
    back = along_dom(edge[:HFACE].astype(bf16), 1)
    ahead = along_dom(edge[HFACE:].astype(bf16), -1)
    theirs = to_mate(rounded)
    kept, came, _ = lax.optimization_barrier((kept, came, rounded))
    start = raised * ((kept + came) * 0.25) - 2.0 * half
    back, ahead, start = lax.optimization_barrier((back, ahead, start))
    inner = (lax.axis_index("dom") < 7).astype(f32)
    edge_mine = jnp.concatenate(
        [(edge[:HFACE] + ahead.astype(f32)) * inner, edge[HFACE:] + back.astype(f32)]
    )
    edge_mine = (edge_mine * 0.25).astype(bf16)
    edge_other = to_mate(edge_mine)
    kept, sent, edge_kept, edge_sent = apply(
        second_kernel, 2, 3, *scalars, rounded, theirs, start, matrix, edge_mine, edge_other, back
    )
    edge = edge_kept + to_mate(edge_sent)
    sent, edge = lax.optimization_barrier((sent, edge))
    came = to_mate(sent)
    back = along_dom(edge[:HFACE].astype(bf16), 1)
    everyone = across_chips(outgoing(kept, came, edge[HFACE:], back))

    begin = h * HALF + chip * SHARE
    place = jnp.stack([begin, h * HFACE + chip * FSHARE]).astype(jnp.int32)
    own = lax.dynamic_slice(weights, (begin,), (SHARE,))
    partial = gram_rows(everyone, weigh(place, face_nodes, weights, own))
    kept, came, back, back_other, partial = lax.optimization_barrier(
        (kept, came, back, to_mate(back), partial)
    )
    mine, theirs = finish(core, face_nodes, kept, came, back, back_other)
    filtered = assemble(core, mine, to_mate(theirs))
    return sum_everywhere(partial, filtered)


def solution(mesh):
    in_specs = (P("band", "dom"), P(), P("dom"), P("dom"), P(None, "dom"), P("dom"), P("dom"))
    out_specs = (P("band", "dom"), P("band", None))
    return jax.shard_map(body, mesh=mesh, in_specs=in_specs, out_specs=out_specs, check_vma=False)
```

```python
import functools

import jax
import jax.numpy as jnp
from jax import lax
from jax.experimental import pallas as pl
from jax.experimental.pallas import tpu as pltpu
from jax.sharding import PartitionSpec as P

NODES = 18432
HALF = 9216
FACE = 1536
HFACE = 768
EXT = NODES + FACE
CELL_NODES = 343
CELLS = 64
ROWS = 70
MAT = 352
LANES = 128
ACCS = 4
SPARE = 8
SHARE = HALF // 8
FSHARE = HFACE // 8
BLOCK = 3072
PIECE = 4608
VMEM = pl.BlockSpec(memory_space=pltpu.VMEM)
SMEM = pl.BlockSpec(memory_space=pltpu.SMEM)
ANY = pl.BlockSpec(memory_space=pl.ANY)
f32 = jnp.float32
bf16 = jnp.bfloat16


def to_mate(block):
    return lax.ppermute(block, "band", [(i, i ^ 1) for i in range(16)])


def along_dom(block, shift):
    return lax.ppermute(block, "dom", [(i, i + shift) for i in range(8) if 0 <= i + shift < 8])


def along_dom_crossed(block, shift):
    pairs = [(i, i + shift, j) for i in range(8) for j in range(16) if 0 <= i + shift < 8]
    route = [(i * 16 + (j ^ 1), to * 16 + j) for i, to, j in pairs]
    return lax.ppermute(block, ("dom", "band"), route)


FREE = pl.CostEstimate(flops=0, bytes_accessed=0, transcendentals=0)


def params(mib):
    return pltpu.CompilerParams(vmem_limit_bytes=mib * 2**20)


def eye():
    rows = lax.broadcasted_iota(jnp.int32, (LANES, LANES), 0)
    return jnp.where(rows == lax.broadcasted_iota(jnp.int32, (LANES, LANES), 1), 1.0, 0.0).astype(bf16)


def turned_by(unit, block):
    return lax.dot_general(unit, block, (((1,), (1,)), ((), ())), preferred_element_type=f32)


def faces_kernel(face, own, out, whole, picked):
    step = pl.program_id(0)
    unit = eye()
    block = own[...].astype(bf16)
    for j in range(BLOCK // LANES):
        rows = pl.ds(pl.multiple_of(step * BLOCK + j * LANES, LANES), LANES)
        whole[rows, pl.ds(0, 64)] = turned_by(unit, block[:, j * LANES : (j + 1) * LANES])

    @pl.when(step == NODES // BLOCK - 1)
    def _():
        def pick(i, _):
            for k in range(16):
                at = i * 16 + k
                picked[pl.ds(at, 1), :] = whole[pl.ds(face[at], 1), :]
            return 0

        lax.fori_loop(0, FACE // 16, pick, 0)
        left = lax.broadcasted_iota(jnp.int32, (HFACE, LANES), 1) < 64
        right = pltpu.roll(picked[pl.ds(HFACE, HFACE), :], 64, 1)
        out[...] = jnp.where(left, picked[pl.ds(0, HFACE), :], right).astype(bf16)


def own_faces(face, own):
    return pl.pallas_call(
        faces_kernel,
        grid_spec=pltpu.PrefetchScalarGridSpec(
            num_scalar_prefetch=1,
            grid=(NODES // BLOCK,),
            in_specs=[pl.BlockSpec((64, BLOCK), lambda i, f: (0, i))],
            out_specs=pl.BlockSpec((HFACE, LANES), lambda i, f: (0, 0)),
            scratch_shapes=[pltpu.VMEM((NODES, LANES), f32), pltpu.VMEM((FACE, LANES), f32)],
        ),
        out_shape=jax.ShapeDtypeStruct((HFACE, LANES), bf16),
        compiler_params=params(48),
        name="faces",
        cost_estimate=FREE,
    )(face, own)


def turn_kernel(core, own, other, potential, field, half, raised, start):
    step = pl.program_id(0)
    first = core[0] == 0
    low = jnp.where(first, own[...], other[...])
    high = jnp.where(first, other[...], own[...])
    block = jnp.concatenate([low, high], axis=0)
    field[...] = block.astype(bf16).T

    @pl.when(step // (HALF // BLOCK) == core[0])
    def _():
        half[...] = block.T
        for j in range(BLOCK // LANES):
            rows = pl.ds(j * LANES, LANES)
            row = potential[0, pl.ds(j, 1), :] - 6.0
            column = jnp.broadcast_to(row, (LANES, LANES)).T
            raised[rows, :] = column
            start[rows, :] = column * half[rows, :]


def turn(core, own, other, potential):
    half = pl.BlockSpec((BLOCK, LANES), lambda i, c: (jnp.clip(i - HALF // BLOCK * c[0], 0, HALF // BLOCK - 1), 0))
    return pl.pallas_call(
        turn_kernel,
        grid_spec=pltpu.PrefetchScalarGridSpec(
            num_scalar_prefetch=1,
            grid=(NODES // BLOCK,),
            in_specs=[pl.BlockSpec((64, BLOCK), lambda i, c: (0, i))] * 2
            + [pl.BlockSpec((1, BLOCK // LANES, LANES), lambda i, c: (i, 0, 0))],
            out_specs=[pl.BlockSpec((BLOCK, LANES), lambda i, c: (i, 0)), half, half, half],
        ),
        out_shape=[jax.ShapeDtypeStruct((NODES, LANES), bf16)]
        + [jax.ShapeDtypeStruct((HALF, LANES), f32)] * 3,
        compiler_params=params(60),
        name="turn",
        cost_estimate=FREE,
    )(core, own, other, potential.reshape(NODES // BLOCK, BLOCK // LANES, LANES))


def apply_kernel(
    second, core, cells, face, potential,
    index, field, start, matrix, ghosts, edge_mine, edge_other, back,
    kept, sent, edge_kept, edge_sent,
    x, g0, g1, p0, p1, stage, picked, *rest,
):
    accs = rest[:ACCS]
    ahead, behind, sems, slots = rest[ACCS : ACCS + 4], rest[ACCS + 4 : ACCS + 8], rest[-2], rest[-1]
    h = core[0]
    mine = pl.multiple_of(h * HALF, HALF)
    theirs = pl.multiple_of((1 - h) * HALF, HALF)
    load = pltpu.make_async_copy(start, accs[0].at[pl.ds(mine, HALF)], sems.at[0])
    copies = []
    for k in range(NODES // PIECE):
        ref, at = (field[0], k * PIECE) if len(field) == 1 else (field[k // 2], k % 2 * PIECE)
        copies.append(
            pltpu.make_async_copy(
                ref.at[pl.ds(at, PIECE)], stage.at[pl.ds(k * PIECE, PIECE)], sems.at[k + 1]
            )
        )
    for copy in copies:
        copy.start()
    load.start()

    def fetch(stage_number, cell):
        row = cell + 1
        a = pltpu.make_async_copy(index.at[row + 1], ahead[stage_number], slots.at[stage_number])
        b = pltpu.make_async_copy(index.at[row - 1], behind[stage_number], slots.at[4 + stage_number])
        return a, b

    for k in range(4):
        for copy in fetch(k, k):
            copy.start()

    zeros = jnp.zeros((256, LANES), f32)

    def clear(i, _):
        for a in accs[1:]:
            a[pl.ds(pl.multiple_of(i * 256, 256), 256), :] = zeros
        return 0

    lax.fori_loop(0, EXT // 256, clear, 0)

    def clear_first(i, _):
        accs[0][pl.ds(pl.multiple_of(theirs + i * 256, 256), 256), :] = zeros
        return 0

    lax.fori_loop(0, HALF // 256, clear_first, 0)
    accs[0][pl.ds(NODES, FACE), :] = jnp.zeros((FACE, LANES), f32)
    for ref in (x, *accs):
        ref[pl.ds(EXT, SPARE), :] = jnp.zeros((SPARE, LANES), f32)
    for ref in (g0, g1, p0, p1):
        ref[...] = jnp.zeros_like(ref)

    if second:
        for edge, part in ((edge_mine, h), (edge_other, 1 - h)):
            to = pl.multiple_of(NODES + part * HFACE, HFACE)
            x[pl.ds(to, HFACE), :] = edge[pl.ds(0, HFACE), :].astype(f32)
            picked[pl.ds(pl.multiple_of(part * HFACE, HFACE), HFACE), :] = edge[
                pl.ds(HFACE, HFACE), :
            ].astype(f32)
    else:
        first = core[0] == 0
        own, other = ghosts[0][...].astype(f32), ghosts[1][...].astype(f32)
        low, high = jnp.where(first, own, other), jnp.where(first, other, own)
        left = lax.broadcasted_iota(jnp.int32, (HFACE, LANES), 1) < 64
        x[pl.ds(NODES, HFACE), :] = jnp.where(left, low, pltpu.roll(high, 64, 1))
        x[pl.ds(NODES + HFACE, HFACE), :] = jnp.where(left, pltpu.roll(low, 64, 1), high)

    for k, copy in enumerate(copies):
        copy.wait()
        if second:
            base = (mine if k < 2 else theirs) + k % 2 * PIECE
        else:
            base = k * PIECE

        def widen(i, _, k=k, base=base):
            at = pl.multiple_of(k * PIECE + i * 256, 256)
            rows = pl.ds(pl.multiple_of(base + i * 256, 256), 256)
            x[rows, :] = stage[pl.ds(at, 256), :].astype(f32)
            return 0

        lax.fori_loop(0, PIECE // 256, widen, 0)
    load.wait()

    if second:

        def put(i, _):
            for k in range(16):
                at = i * 16 + k
                x[pl.ds(face[at], 1), :] = picked[pl.ds(at, 1), :]
            return 0

        lax.fori_loop(0, FACE // 16, put, 0)

        picked[pl.ds(0, HFACE), :] = back[...].astype(f32)

        def shift(i, _):
            for j in range(0, 16, ACCS):
                at = [i * 16 + j + k for k in range(ACCS)]
                node = [face[h * HFACE + a] for a in at]
                gain = [(potential[n] - 6.0) * 0.25 for n in node]
                sums = [
                    accs[k][pl.ds(node[k], 1), :] + picked[pl.ds(at[k], 1), :] * gain[k]
                    for k in range(ACCS)
                ]
                for k in range(ACCS):
                    accs[k][pl.ds(node[k], 1), :] = sums[k]
            return 0

        lax.fori_loop(0, HFACE // 16, shift, 0)

    def gather(g, nodes, lo, hi):
        for a in range(lo, min(hi, CELL_NODES)):
            g[pl.ds(a, 1), :] = x[pl.ds(nodes[a // LANES, a % LANES], 1), :]

    def scatter(p, nodes, lo, hi):
        for a in range(lo, min(hi, CELL_NODES), 2 * ACCS):
            count = min(2 * ACCS, CELL_NODES - a)
            at = [nodes[(a + k) // LANES, (a + k) % LANES] for k in range(count)]
            held = [accs[k % ACCS][pl.ds(at[k], 1), :] for k in range(count)]
            sums = []
            for k in range(count):
                if k >= ACCS:
                    held[k] = jnp.where(at[k] == at[k - ACCS], sums[k - ACCS], held[k])
                sums.append(held[k] + p[pl.ds(a + k, 1), :])
            for k in range(count):
                accs[k % ACCS][pl.ds(at[k], 1), :] = sums[k]

    def step(k, cell):
        g_now, g_next, p_now, p_last = (g0, g1, p0, p1) if k % 2 == 0 else (g1, g0, p1, p0)
        for copy in fetch(k, cell + k):
            copy.wait()
        p_now[...] = jnp.dot(matrix[...], g_now[...].astype(bf16), preferred_element_type=f32)
        for lo in range(0, CELL_NODES, 8):
            scatter(p_last, behind[k], lo, lo + 8)
            gather(g_next, ahead[k], lo, lo + 8)
        for copy in fetch(k, cell + 4 + k):
            copy.start()

    first = pltpu.make_async_copy(index.at[1], rest[ACCS + 8], slots.at[8])
    first.start()
    first.wait()
    gather(g0, rest[ACCS + 8], 0, CELL_NODES)

    def four(i, _):
        for k in range(4):
            step(k, 4 * i)
        return 0

    fours = (cells[0] + 3) // 4
    lax.fori_loop(0, fours, four, 0)
    for k in range(4):
        for copy in fetch(k, 4 * fours + k):
            copy.wait()
    scatter(p1, behind[0], 0, CELL_NODES)

    def total(begin, count):
        def add(i, _):
            rows = pl.ds(pl.multiple_of(begin + i * 256, 256), 256)
            accs[0][rows, :] = (accs[0][rows, :] + accs[1][rows, :]) + (
                accs[2][rows, :] + accs[3][rows, :]
            )
            return 0

        lax.fori_loop(0, count // 256, add, 0)

    writes = []

    def write(source, target):
        writes.append(pltpu.make_async_copy(source, target, sems.at[len(writes)]))
        writes[-1].start()

    for begin, target in ((theirs, sent), (mine, kept)):
        for at in range(0, HALF, PIECE):
            total(begin + at, PIECE)
            write(
                accs[0].at[pl.ds(pl.multiple_of(begin + at, PIECE), PIECE)],
                target.at[pl.ds(at, PIECE)],
            )
    total(NODES, FACE)

    def pick(i, _):
        for k in range(16):
            at = i * 16 + k
            picked[pl.ds(at, 1), :] = accs[0][pl.ds(face[at], 1), :]
        return 0

    lax.fori_loop(0, FACE // 16, pick, 0)
    for part, target in ((1 - h, edge_sent), (h, edge_kept)):
        ghost = pl.multiple_of(NODES + part * HFACE, HFACE)
        write(accs[0].at[pl.ds(ghost, HFACE)], target.at[pl.ds(0, HFACE)])
        own = pl.multiple_of(part * HFACE, HFACE)
        write(picked.at[pl.ds(own, HFACE)], target.at[pl.ds(HFACE, HFACE)])
    for w in writes:
        w.wait()


def first_kernel(core, cells, face, potential, index, field, start, matrix, own, other, *rest):
    apply_kernel(
        False, core, cells, face, potential, index,
        (field,), start, matrix, (own, other), None, None, None, *rest,
    )


def second_kernel(
    core, cells, face, potential, index, mine, theirs, start, matrix,
    edge_mine, edge_other, back, *rest,
):
    apply_kernel(
        True, core, cells, face, potential, index,
        (mine, theirs), start, matrix, None, edge_mine, edge_other, back, *rest,
    )


def apply(kernel, fields, edges, *operands):
    edge = jax.ShapeDtypeStruct((FACE, LANES), f32)
    half = jax.ShapeDtypeStruct((HALF, LANES), f32)
    return pl.pallas_call(
        kernel,
        in_specs=[SMEM] * 4 + [ANY] * (2 + fields) + [VMEM] * (1 + edges),
        out_specs=[ANY] * 4,
        scratch_shapes=[pltpu.VMEM((EXT + SPARE, LANES), f32)]
        + [pltpu.VMEM((MAT, LANES), f32)] * 4
        + [pltpu.VMEM((NODES, LANES), bf16), pltpu.VMEM((FACE, LANES), f32)]
        + [pltpu.VMEM((EXT + SPARE, LANES), f32)] * ACCS
        + [pltpu.SMEM((8, LANES), jnp.int32)] * 9
        + [pltpu.SemaphoreType.DMA((8,)), pltpu.SemaphoreType.DMA((9,))],
        out_shape=[half, half, edge, edge],
        compiler_params=params(61),
        name="apply",
    )(*operands)


def finish_kernel(core, face, kept, came, back_mine, back_other, mine, theirs, sums, wide):
    def add(i, _):
        rows = pl.ds(pl.multiple_of(i * 256, 256), 256)
        sums[rows, :] = (kept[rows, :] + came[rows, :]) * 0.5
        return 0

    lax.fori_loop(0, HALF // 256, add, 0)
    sums[pl.ds(HALF, SPARE), :] = jnp.zeros((SPARE, LANES), f32)
    base = core[0] * HALF
    for back, part in ((back_mine, core[0]), (back_other, 1 - core[0])):
        wide[...] = back[...].astype(f32)

        def put(i, _, part=part):
            for k in range(8):
                at = i * 8 + k
                node = face[part * HFACE + at] - base
                node = jnp.where((node >= 0) & (node < HALF), node, HALF)
                sums[pl.ds(node, 1), :] += wide[pl.ds(at, 1), :] * 0.5
            return 0

        lax.fori_loop(0, HFACE // 8, put, 0)

    def out(i, _):
        rows = pl.ds(pl.multiple_of(i * 256, 256), 256)
        block = sums[rows, :].T
        mine[:, rows] = jnp.where(core[0] == 0, block[:64], block[64:])
        theirs[:, rows] = jnp.where(core[0] == 0, block[64:], block[:64])
        return 0

    lax.fori_loop(0, HALF // 256, out, 0)


def finish(core, face, kept, came, back_mine, back_other):
    return pl.pallas_call(
        finish_kernel,
        in_specs=[SMEM] * 2 + [VMEM] * 4,
        out_specs=[VMEM] * 2,
        scratch_shapes=[pltpu.VMEM((HALF + SPARE, LANES), f32), pltpu.VMEM((HFACE, LANES), f32)],
        out_shape=[jax.ShapeDtypeStruct((64, HALF), f32)] * 2,
        compiler_params=params(60),
        name="finish",
        cost_estimate=FREE,
    )(core, face, kept, came, back_mine, back_other)


def place_kernel(core, mine, theirs, out):
    out[...] = jnp.where(pl.program_id(0) // (HALF // BLOCK) == core[0], mine[...], theirs[...])


def assemble(core, mine, theirs):
    last = HALF // BLOCK - 1
    return pl.pallas_call(
        place_kernel,
        grid_spec=pltpu.PrefetchScalarGridSpec(
            num_scalar_prefetch=1,
            grid=(NODES // BLOCK,),
            in_specs=[
                pl.BlockSpec((64, BLOCK), lambda i, c: (0, jnp.clip(i - (last + 1) * c[0], 0, last))),
                pl.BlockSpec((64, BLOCK), lambda i, c: (0, jnp.clip(i - (last + 1) * (1 - c[0]), 0, last))),
            ],
            out_specs=pl.BlockSpec((64, BLOCK), lambda i, c: (0, i)),
        ),
        out_shape=jax.ShapeDtypeStruct((64, NODES), f32),
        compiler_params=params(40),
        name="place",
        cost_estimate=FREE,
    )(core, mine, theirs)


def weigh_kernel(place, face, weights, own, out, rows):
    for j in range(SHARE // LANES):
        row = jnp.broadcast_to(own[pl.ds(j, 1), :], (LANES, LANES))
        rows[pl.ds(j * LANES, LANES), :] = row.T
    zero = jnp.zeros((1, LANES), f32)

    def drop(i, _):
        for k in range(8):
            node = face[i * 8 + k] - place[0]
            node = jnp.where((node >= 0) & (node < SHARE), node, SHARE)
            rows[pl.ds(node, 1), :] = zero
        return 0

    lax.fori_loop(0, FACE // 8, drop, 0)
    out[pl.ds(0, SHARE), :] = rows[pl.ds(0, SHARE), :]

    def add(i, _):
        for k in range(8):
            at = i * 8 + k
            out[pl.ds(SHARE + at, 1), :] = jnp.full((1, LANES), weights[face[place[1] + at]], f32)
        return 0

    lax.fori_loop(0, FSHARE // 8, add, 0)


def weigh(place, face, weights, own):
    return pl.pallas_call(
        weigh_kernel,
        in_specs=[SMEM] * 3 + [VMEM],
        out_specs=VMEM,
        scratch_shapes=[pltpu.VMEM((SHARE + SPARE, LANES), f32)],
        out_shape=jax.ShapeDtypeStruct((SHARE + FSHARE, LANES), f32),
        compiler_params=params(60),
        name="weigh",
        cost_estimate=FREE,
    )(place, face, weights, own.reshape(SHARE // LANES, LANES))


def outgoing_kernel(kept, came, edge, back, out):
    out[0, pl.ds(0, SHARE), :] = ((kept[...] + came[...]) * 0.5).astype(bf16)
    out[0, pl.ds(SHARE, FSHARE), :] = ((edge[...] + back[...].astype(f32)) * 0.5).astype(bf16)


def outgoing(kept, came, edge, back):
    nodes = pl.BlockSpec((SHARE, LANES), lambda i: (i, 0))
    faces = pl.BlockSpec((FSHARE, LANES), lambda i: (i, 0))
    return pl.pallas_call(
        outgoing_kernel,
        grid=(8,),
        in_specs=[nodes, nodes, faces, faces],
        out_specs=pl.BlockSpec((1, SHARE + FSHARE, LANES), lambda i: (i, 0, 0)),
        out_shape=jax.ShapeDtypeStruct((8, SHARE + FSHARE, LANES), bf16),
        compiler_params=params(40),
        name="outgoing",
        cost_estimate=FREE,
    )(kept, came, edge, back)


def gram_kernel(nodes, weights, out, everyone):
    for q in range(8):
        lanes = pl.ds(q * LANES, LANES)
        everyone[:, lanes] = nodes[q]

    def rows(q, _):
        at = pl.multiple_of(q * LANES, LANES)
        block = everyone[:, pl.ds(at, LANES)].astype(f32)
        scaled = (weights[...] * block).T.astype(bf16)
        product = jnp.dot(scaled, everyone[...], preferred_element_type=f32)
        out[pl.ds(at, LANES), :] = product.astype(bf16)
        return 0

    lax.fori_loop(0, 8, rows, 0)


def gram_rows(nodes, weights):
    return pl.pallas_call(
        gram_kernel,
        in_specs=[VMEM] * 2,
        out_specs=VMEM,
        scratch_shapes=[pltpu.VMEM((SHARE + FSHARE, 1024), bf16)],
        out_shape=jax.ShapeDtypeStruct((1024, 1024), bf16),
        compiler_params=params(40),
        name="gram",
    )(nodes, weights)


def across_chips(block):
    groups = [list(range(0, 16, 2)), list(range(1, 16, 2))]
    return lax.all_to_all(block, "band", 0, 0, axis_index_groups=groups, tiled=True)


def sum_everywhere(partial, filtered):
    parts = lax.all_to_all(partial.reshape(128, 8, 1024), ("band", "dom"), 0, 0, tiled=True)
    parts, filtered = lax.optimization_barrier((parts, filtered))
    part = jnp.sum(parts.astype(f32), axis=0)
    copies = jnp.broadcast_to(part[None], (8, 8, 1024))
    return filtered, lax.all_to_all(copies, "dom", 0, 0, tiled=True).reshape(64, 1024)


def body(states, cell_matrix, potential, weights, connectivity, face_nodes, cell_counts):
    band = lax.axis_index("band")
    chip = band // 2
    h = band % 2
    core = h.astype(jnp.int32).reshape(1)

    other = to_mate(states)
    own_cells = lax.dynamic_index_in_dim(
        connectivity.reshape(CELL_NODES, CELLS, 2), h, 2, keepdims=False
    )
    cells = (cell_counts - h + 1) // 2
    live = jnp.arange(CELLS) < cells[0]
    index = jnp.where(live[:, None], own_cells.T, EXT)
    index = jnp.pad(index, ((1, ROWS - 1 - CELLS), (0, 1024 - CELL_NODES)), constant_values=EXT)
    index = index.reshape(ROWS, 8, LANES)
    matrix = jnp.pad(cell_matrix, ((0, MAT - CELL_NODES),) * 2)
    faces = own_faces(face_nodes, states)
    ghosts = along_dom(faces, -1)
    ghosts_other = along_dom_crossed(faces, -1)
    field, half, raised, start = turn(core, states, other, potential)
    scalars = (core, cells, face_nodes, potential, index)
    kept, sent, edge_kept, edge_sent = apply(
        first_kernel, 1, 2, *scalars, field, start, matrix, ghosts, ghosts_other
    )
    edge = edge_kept + to_mate(edge_sent)
    sent, edge = lax.optimization_barrier((sent, edge))
    came = to_mate(sent)
    rounded = ((kept + came) * 0.25).astype(bf16)
    back = along_dom(edge[:HFACE].astype(bf16), 1)
    ahead = along_dom(edge[HFACE:].astype(bf16), -1)
    theirs = to_mate(rounded)
    kept, came, _ = lax.optimization_barrier((kept, came, rounded))
    start = raised * ((kept + came) * 0.25) - 2.0 * half
    back, ahead, start = lax.optimization_barrier((back, ahead, start))
    inner = (lax.axis_index("dom") < 7).astype(f32)
    edge_mine = jnp.concatenate(
        [(edge[:HFACE] + ahead.astype(f32)) * inner, edge[HFACE:] + back.astype(f32)]
    )
    edge_mine = (edge_mine * 0.25).astype(bf16)
    edge_other = to_mate(edge_mine)
    kept, sent, edge_kept, edge_sent = apply(
        second_kernel, 2, 3, *scalars, rounded, theirs, start, matrix, edge_mine, edge_other, back
    )
    edge = edge_kept + to_mate(edge_sent)
    sent, edge = lax.optimization_barrier((sent, edge))
    came = to_mate(sent)
    back = along_dom(edge[:HFACE].astype(bf16), 1)
    everyone = across_chips(outgoing(kept, came, edge[HFACE:], back))
    mine, theirs = finish(core, face_nodes, kept, came, back, to_mate(back))
    everyone, mine, theirs = lax.optimization_barrier((everyone, mine, theirs))

    begin = h * HALF + chip * SHARE
    place = jnp.stack([begin, h * HFACE + chip * FSHARE]).astype(jnp.int32)
    own = lax.dynamic_slice(weights, (begin,), (SHARE,))
    partial = gram_rows(everyone, weigh(place, face_nodes, weights, own))
    filtered = assemble(core, mine, to_mate(theirs))
    return sum_everywhere(partial, filtered)


def solution(mesh):
    in_specs = (P("band", "dom"), P(), P("dom"), P("dom"), P(None, "dom"), P("dom"), P("dom"))
    out_specs = (P("band", "dom"), P("band", None))
    return jax.shard_map(body, mesh=mesh, in_specs=in_specs, out_specs=out_specs, check_vma=False)
```

```python
import functools

import jax
import jax.numpy as jnp
from jax import lax
from jax.experimental import pallas as pl
from jax.experimental.pallas import tpu as pltpu
from jax.sharding import PartitionSpec as P

NODES = 18432
HALF = 9216
FACE = 1536
HFACE = 768
EXT = NODES + FACE
CELL_NODES = 343
CELLS = 64
ROWS = 70
MAT = 352
LANES = 128
ACCS = 4
SPARE = 8
SHARE = HALF // 8
FSHARE = HFACE // 8
BLOCK = 3072
PIECE = 4608
VMEM = pl.BlockSpec(memory_space=pltpu.VMEM)
SMEM = pl.BlockSpec(memory_space=pltpu.SMEM)
ANY = pl.BlockSpec(memory_space=pl.ANY)
f32 = jnp.float32
bf16 = jnp.bfloat16


def to_mate(block):
    return lax.ppermute(block, "band", [(i, i ^ 1) for i in range(16)])


def along_dom(block, shift):
    return lax.ppermute(block, "dom", [(i, i + shift) for i in range(8) if 0 <= i + shift < 8])


def along_dom_crossed(block, shift):
    pairs = [(i, i + shift, j) for i in range(8) for j in range(16) if 0 <= i + shift < 8]
    route = [(i * 16 + (j ^ 1), to * 16 + j) for i, to, j in pairs]
    return lax.ppermute(block, ("dom", "band"), route)


FREE = pl.CostEstimate(flops=0, bytes_accessed=0, transcendentals=0)


def params(mib):
    return pltpu.CompilerParams(vmem_limit_bytes=mib * 2**20)


def eye():
    rows = lax.broadcasted_iota(jnp.int32, (LANES, LANES), 0)
    return jnp.where(rows == lax.broadcasted_iota(jnp.int32, (LANES, LANES), 1), 1.0, 0.0).astype(bf16)


def turned_by(unit, block):
    return lax.dot_general(unit, block, (((1,), (1,)), ((), ())), preferred_element_type=f32)


def faces_kernel(face, own, out, whole, picked):
    step = pl.program_id(0)
    unit = eye()
    block = own[...].astype(bf16)
    for j in range(BLOCK // LANES):
        rows = pl.ds(pl.multiple_of(step * BLOCK + j * LANES, LANES), LANES)
        whole[rows, pl.ds(0, 64)] = turned_by(unit, block[:, j * LANES : (j + 1) * LANES])

    @pl.when(step == NODES // BLOCK - 1)
    def _():
        def pick(i, _):
            for k in range(16):
                at = i * 16 + k
                picked[pl.ds(at, 1), :] = whole[pl.ds(face[at], 1), :]
            return 0

        lax.fori_loop(0, FACE // 16, pick, 0)
        left = lax.broadcasted_iota(jnp.int32, (HFACE, LANES), 1) < 64
        right = pltpu.roll(picked[pl.ds(HFACE, HFACE), :], 64, 1)
        out[...] = jnp.where(left, picked[pl.ds(0, HFACE), :], right).astype(bf16)


def own_faces(face, own):
    return pl.pallas_call(
        faces_kernel,
        grid_spec=pltpu.PrefetchScalarGridSpec(
            num_scalar_prefetch=1,
            grid=(NODES // BLOCK,),
            in_specs=[pl.BlockSpec((64, BLOCK), lambda i, f: (0, i))],
            out_specs=pl.BlockSpec((HFACE, LANES), lambda i, f: (0, 0)),
            scratch_shapes=[pltpu.VMEM((NODES, LANES), f32), pltpu.VMEM((FACE, LANES), f32)],
        ),
        out_shape=jax.ShapeDtypeStruct((HFACE, LANES), bf16),
        compiler_params=params(48),
        name="faces",
        cost_estimate=FREE,
    )(face, own)


def turn_kernel(core, own, other, potential, field, half, raised, start):
    step = pl.program_id(0)
    first = core[0] == 0
    low = jnp.where(first, own[...], other[...])
    high = jnp.where(first, other[...], own[...])
    block = jnp.concatenate([low, high], axis=0)
    field[...] = block.astype(bf16).T

    @pl.when(step // (HALF // BLOCK) == core[0])
    def _():
        half[...] = block.T
        for j in range(BLOCK // LANES):
            rows = pl.ds(j * LANES, LANES)
            row = potential[0, pl.ds(j, 1), :] - 6.0
            column = jnp.broadcast_to(row, (LANES, LANES)).T
            raised[rows, :] = column
            start[rows, :] = column * half[rows, :]


def turn(core, own, other, potential):
    half = pl.BlockSpec((BLOCK, LANES), lambda i, c: (jnp.clip(i - HALF // BLOCK * c[0], 0, HALF // BLOCK - 1), 0))
    return pl.pallas_call(
        turn_kernel,
        grid_spec=pltpu.PrefetchScalarGridSpec(
            num_scalar_prefetch=1,
            grid=(NODES // BLOCK,),
            in_specs=[pl.BlockSpec((64, BLOCK), lambda i, c: (0, i))] * 2
            + [pl.BlockSpec((1, BLOCK // LANES, LANES), lambda i, c: (i, 0, 0))],
            out_specs=[pl.BlockSpec((BLOCK, LANES), lambda i, c: (i, 0)), half, half, half],
        ),
        out_shape=[jax.ShapeDtypeStruct((NODES, LANES), bf16)]
        + [jax.ShapeDtypeStruct((HALF, LANES), f32)] * 3,
        compiler_params=params(60),
        name="turn",
        cost_estimate=FREE,
    )(core, own, other, potential.reshape(NODES // BLOCK, BLOCK // LANES, LANES))


def apply_kernel(
    second, core, cells, face, potential,
    index, field, start, matrix, ghosts, edge_mine, edge_other, back,
    kept, sent, edge_kept, edge_sent,
    x, g0, g1, p0, p1, stage, picked, *rest,
):
    accs = rest[:ACCS]
    ahead, behind, sems, slots = rest[ACCS : ACCS + 4], rest[ACCS + 4 : ACCS + 8], rest[-2], rest[-1]
    h = core[0]
    mine = pl.multiple_of(h * HALF, HALF)
    theirs = pl.multiple_of((1 - h) * HALF, HALF)
    load = pltpu.make_async_copy(start, accs[0].at[pl.ds(mine, HALF)], sems.at[0])
    copies = []
    for k in range(NODES // PIECE):
        ref, at = (field[0], k * PIECE) if len(field) == 1 else (field[k // 2], k % 2 * PIECE)
        copies.append(
            pltpu.make_async_copy(
                ref.at[pl.ds(at, PIECE)], stage.at[pl.ds(k * PIECE, PIECE)], sems.at[k + 1]
            )
        )
    for copy in copies:
        copy.start()
    load.start()

    def fetch(stage_number, cell):
        row = cell + 1
        a = pltpu.make_async_copy(index.at[row + 1], ahead[stage_number], slots.at[stage_number])
        b = pltpu.make_async_copy(index.at[row - 1], behind[stage_number], slots.at[4 + stage_number])
        return a, b

    for k in range(4):
        for copy in fetch(k, k):
            copy.start()

    zeros = jnp.zeros((256, LANES), f32)

    def clear(i, _):
        for a in accs[1:]:
            a[pl.ds(pl.multiple_of(i * 256, 256), 256), :] = zeros
        return 0

    lax.fori_loop(0, EXT // 256, clear, 0)

    def clear_first(i, _):
        accs[0][pl.ds(pl.multiple_of(theirs + i * 256, 256), 256), :] = zeros
        return 0

    lax.fori_loop(0, HALF // 256, clear_first, 0)
    accs[0][pl.ds(NODES, FACE), :] = jnp.zeros((FACE, LANES), f32)
    for ref in (x, *accs):
        ref[pl.ds(EXT, SPARE), :] = jnp.zeros((SPARE, LANES), f32)
    for ref in (g0, g1, p0, p1):
        ref[...] = jnp.zeros_like(ref)

    if second:
        for edge, part in ((edge_mine, h), (edge_other, 1 - h)):
            to = pl.multiple_of(NODES + part * HFACE, HFACE)
            x[pl.ds(to, HFACE), :] = edge[pl.ds(0, HFACE), :].astype(f32)
            picked[pl.ds(pl.multiple_of(part * HFACE, HFACE), HFACE), :] = edge[
                pl.ds(HFACE, HFACE), :
            ].astype(f32)
    else:
        first = core[0] == 0
        own, other = ghosts[0][...].astype(f32), ghosts[1][...].astype(f32)
        low, high = jnp.where(first, own, other), jnp.where(first, other, own)
        left = lax.broadcasted_iota(jnp.int32, (HFACE, LANES), 1) < 64
        x[pl.ds(NODES, HFACE), :] = jnp.where(left, low, pltpu.roll(high, 64, 1))
        x[pl.ds(NODES + HFACE, HFACE), :] = jnp.where(left, pltpu.roll(low, 64, 1), high)

    for k, copy in enumerate(copies):
        copy.wait()
        if second:
            base = (mine if k < 2 else theirs) + k % 2 * PIECE
        else:
            base = k * PIECE

        def widen(i, _, k=k, base=base):
            at = pl.multiple_of(k * PIECE + i * 256, 256)
            rows = pl.ds(pl.multiple_of(base + i * 256, 256), 256)
            x[rows, :] = stage[pl.ds(at, 256), :].astype(f32)
            return 0

        lax.fori_loop(0, PIECE // 256, widen, 0)
    load.wait()

    if second:

        def put(i, _):
            for k in range(16):
                at = i * 16 + k
                x[pl.ds(face[at], 1), :] = picked[pl.ds(at, 1), :]
            return 0

        lax.fori_loop(0, FACE // 16, put, 0)

        picked[pl.ds(0, HFACE), :] = back[...].astype(f32)

        def shift(i, _):
            for j in range(0, 16, ACCS):
                at = [i * 16 + j + k for k in range(ACCS)]
                node = [face[h * HFACE + a] for a in at]
                gain = [(potential[n] - 6.0) * 0.25 for n in node]
                sums = [
                    accs[k][pl.ds(node[k], 1), :] + picked[pl.ds(at[k], 1), :] * gain[k]
                    for k in range(ACCS)
                ]
                for k in range(ACCS):
                    accs[k][pl.ds(node[k], 1), :] = sums[k]
            return 0

        lax.fori_loop(0, HFACE // 16, shift, 0)

    def gather(g, nodes, lo, hi):
        for a in range(lo, min(hi, CELL_NODES)):
            g[pl.ds(a, 1), :] = x[pl.ds(nodes[a // LANES, a % LANES], 1), :]

    def scatter(p, nodes, lo, hi):
        for a in range(lo, min(hi, CELL_NODES), 2 * ACCS):
            count = min(2 * ACCS, CELL_NODES - a)
            at = [nodes[(a + k) // LANES, (a + k) % LANES] for k in range(count)]
            held = [accs[k % ACCS][pl.ds(at[k], 1), :] for k in range(count)]
            sums = []
            for k in range(count):
                if k >= ACCS:
                    held[k] = jnp.where(at[k] == at[k - ACCS], sums[k - ACCS], held[k])
                sums.append(held[k] + p[pl.ds(a + k, 1), :])
            for k in range(count):
                accs[k % ACCS][pl.ds(at[k], 1), :] = sums[k]

    def step(k, cell):
        g_now, g_next, p_now, p_last = (g0, g1, p0, p1) if k % 2 == 0 else (g1, g0, p1, p0)
        for copy in fetch(k, cell + k):
            copy.wait()
        p_now[...] = jnp.dot(matrix[...], g_now[...].astype(bf16), preferred_element_type=f32)
        for lo in range(0, CELL_NODES, 8):
            scatter(p_last, behind[k], lo, lo + 8)
            gather(g_next, ahead[k], lo, lo + 8)
        for copy in fetch(k, cell + 4 + k):
            copy.start()

    first = pltpu.make_async_copy(index.at[1], rest[ACCS + 8], slots.at[8])
    first.start()
    first.wait()
    gather(g0, rest[ACCS + 8], 0, CELL_NODES)

    def four(i, _):
        for k in range(4):
            step(k, 4 * i)
        return 0

    fours = (cells[0] + 3) // 4
    lax.fori_loop(0, fours, four, 0)
    for k in range(4):
        for copy in fetch(k, 4 * fours + k):
            copy.wait()
    scatter(p1, behind[0], 0, CELL_NODES)

    def total(begin, count):
        def add(i, _):
            rows = pl.ds(pl.multiple_of(begin + i * 256, 256), 256)
            accs[0][rows, :] = (accs[0][rows, :] + accs[1][rows, :]) + (
                accs[2][rows, :] + accs[3][rows, :]
            )
            return 0

        lax.fori_loop(0, count // 256, add, 0)

    writes = []

    def write(source, target):
        writes.append(pltpu.make_async_copy(source, target, sems.at[len(writes)]))
        writes[-1].start()

    for begin, target in ((theirs, sent), (mine, kept)):
        for at in range(0, HALF, PIECE):
            total(begin + at, PIECE)
            write(
                accs[0].at[pl.ds(pl.multiple_of(begin + at, PIECE), PIECE)],
                target.at[pl.ds(at, PIECE)],
            )
    total(NODES, FACE)

    def pick(i, _):
        for k in range(16):
            at = i * 16 + k
            picked[pl.ds(at, 1), :] = accs[0][pl.ds(face[at], 1), :]
        return 0

    lax.fori_loop(0, FACE // 16, pick, 0)
    for part, target in ((1 - h, edge_sent), (h, edge_kept)):
        ghost = pl.multiple_of(NODES + part * HFACE, HFACE)
        write(accs[0].at[pl.ds(ghost, HFACE)], target.at[pl.ds(0, HFACE)])
        own = pl.multiple_of(part * HFACE, HFACE)
        write(picked.at[pl.ds(own, HFACE)], target.at[pl.ds(HFACE, HFACE)])
    for w in writes:
        w.wait()


def first_kernel(core, cells, face, potential, index, field, start, matrix, own, other, *rest):
    apply_kernel(
        False, core, cells, face, potential, index,
        (field,), start, matrix, (own, other), None, None, None, *rest,
    )


def second_kernel(
    core, cells, face, potential, index, mine, theirs, start, matrix,
    edge_mine, edge_other, back, *rest,
):
    apply_kernel(
        True, core, cells, face, potential, index,
        (mine, theirs), start, matrix, None, edge_mine, edge_other, back, *rest,
    )


def apply(kernel, fields, edges, *operands):
    edge = jax.ShapeDtypeStruct((FACE, LANES), f32)
    half = jax.ShapeDtypeStruct((HALF, LANES), f32)
    return pl.pallas_call(
        kernel,
        in_specs=[SMEM] * 4 + [ANY] * (2 + fields) + [VMEM] * (1 + edges),
        out_specs=[ANY] * 4,
        scratch_shapes=[pltpu.VMEM((EXT + SPARE, LANES), f32)]
        + [pltpu.VMEM((MAT, LANES), f32)] * 4
        + [pltpu.VMEM((NODES, LANES), bf16), pltpu.VMEM((FACE, LANES), f32)]
        + [pltpu.VMEM((EXT + SPARE, LANES), f32)] * ACCS
        + [pltpu.SMEM((8, LANES), jnp.int32)] * 9
        + [pltpu.SemaphoreType.DMA((8,)), pltpu.SemaphoreType.DMA((9,))],
        out_shape=[half, half, edge, edge],
        compiler_params=params(61),
        name="apply",
    )(*operands)


def finish_kernel(core, face, kept, came, back_mine, back_other, mine, theirs, sums, wide):
    def add(i, _):
        rows = pl.ds(pl.multiple_of(i * 256, 256), 256)
        sums[rows, :] = (kept[rows, :] + came[rows, :]) * 0.5
        return 0

    lax.fori_loop(0, HALF // 256, add, 0)
    sums[pl.ds(HALF, SPARE), :] = jnp.zeros((SPARE, LANES), f32)
    base = core[0] * HALF
    for back, part in ((back_mine, core[0]), (back_other, 1 - core[0])):
        wide[...] = back[...].astype(f32)

        def put(i, _, part=part):
            for k in range(8):
                at = i * 8 + k
                node = face[part * HFACE + at] - base
                node = jnp.where((node >= 0) & (node < HALF), node, HALF)
                sums[pl.ds(node, 1), :] += wide[pl.ds(at, 1), :] * 0.5
            return 0

        lax.fori_loop(0, HFACE // 8, put, 0)

    def out(i, _):
        rows = pl.ds(pl.multiple_of(i * 256, 256), 256)
        block = sums[rows, :].T
        mine[:, rows] = jnp.where(core[0] == 0, block[:64], block[64:])
        theirs[:, rows] = jnp.where(core[0] == 0, block[64:], block[:64])
        return 0

    lax.fori_loop(0, HALF // 256, out, 0)


def finish(core, face, kept, came, back_mine, back_other):
    return pl.pallas_call(
        finish_kernel,
        in_specs=[SMEM] * 2 + [VMEM] * 4,
        out_specs=[VMEM] * 2,
        scratch_shapes=[pltpu.VMEM((HALF + SPARE, LANES), f32), pltpu.VMEM((HFACE, LANES), f32)],
        out_shape=[jax.ShapeDtypeStruct((64, HALF), f32)] * 2,
        compiler_params=params(60),
        name="finish",
        cost_estimate=FREE,
    )(core, face, kept, came, back_mine, back_other)


def place_kernel(core, mine, theirs, out):
    out[...] = jnp.where(pl.program_id(0) // (HALF // BLOCK) == core[0], mine[...], theirs[...])


def assemble(core, mine, theirs):
    last = HALF // BLOCK - 1
    return pl.pallas_call(
        place_kernel,
        grid_spec=pltpu.PrefetchScalarGridSpec(
            num_scalar_prefetch=1,
            grid=(NODES // BLOCK,),
            in_specs=[
                pl.BlockSpec((64, BLOCK), lambda i, c: (0, jnp.clip(i - (last + 1) * c[0], 0, last))),
                pl.BlockSpec((64, BLOCK), lambda i, c: (0, jnp.clip(i - (last + 1) * (1 - c[0]), 0, last))),
            ],
            out_specs=pl.BlockSpec((64, BLOCK), lambda i, c: (0, i)),
        ),
        out_shape=jax.ShapeDtypeStruct((64, NODES), f32),
        compiler_params=params(40),
        name="place",
        cost_estimate=FREE,
    )(core, mine, theirs)


def weigh_kernel(place, face, weights, own, out, rows):
    for j in range(SHARE // LANES):
        row = jnp.broadcast_to(own[pl.ds(j, 1), :], (LANES, LANES))
        rows[pl.ds(j * LANES, LANES), :] = row.T
    zero = jnp.zeros((1, LANES), f32)

    def drop(i, _):
        for k in range(8):
            node = face[i * 8 + k] - place[0]
            node = jnp.where((node >= 0) & (node < SHARE), node, SHARE)
            rows[pl.ds(node, 1), :] = zero
        return 0

    lax.fori_loop(0, FACE // 8, drop, 0)
    out[pl.ds(0, SHARE), :] = rows[pl.ds(0, SHARE), :]

    def add(i, _):
        for k in range(8):
            at = i * 8 + k
            out[pl.ds(SHARE + at, 1), :] = jnp.full((1, LANES), weights[face[place[1] + at]], f32)
        return 0

    lax.fori_loop(0, FSHARE // 8, add, 0)


def weigh(place, face, weights, own):
    return pl.pallas_call(
        weigh_kernel,
        in_specs=[SMEM] * 3 + [VMEM],
        out_specs=VMEM,
        scratch_shapes=[pltpu.VMEM((SHARE + SPARE, LANES), f32)],
        out_shape=jax.ShapeDtypeStruct((SHARE + FSHARE, LANES), f32),
        compiler_params=params(60),
        name="weigh",
        cost_estimate=FREE,
    )(place, face, weights, own.reshape(SHARE // LANES, LANES))


def outgoing_kernel(kept, came, edge, back, out):
    out[0, pl.ds(0, SHARE), :] = ((kept[...] + came[...]) * 0.5).astype(bf16)
    out[0, pl.ds(SHARE, FSHARE), :] = ((edge[...] + back[...].astype(f32)) * 0.5).astype(bf16)


def outgoing(kept, came, edge, back):
    nodes = pl.BlockSpec((SHARE, LANES), lambda i: (i, 0))
    faces = pl.BlockSpec((FSHARE, LANES), lambda i: (i, 0))
    return pl.pallas_call(
        outgoing_kernel,
        grid=(8,),
        in_specs=[nodes, nodes, faces, faces],
        out_specs=pl.BlockSpec((1, SHARE + FSHARE, LANES), lambda i: (i, 0, 0)),
        out_shape=jax.ShapeDtypeStruct((8, SHARE + FSHARE, LANES), bf16),
        compiler_params=params(40),
        name="outgoing",
        cost_estimate=FREE,
    )(kept, came, edge, back)


def gram_kernel(nodes, weights, out, everyone):
    for q in range(8):
        lanes = pl.ds(q * LANES, LANES)
        everyone[:, lanes] = nodes[q]

    def rows(q, _):
        at = pl.multiple_of(q * LANES, LANES)
        block = everyone[:, pl.ds(at, LANES)].astype(f32)
        scaled = (weights[...] * block).T.astype(bf16)
        product = jnp.dot(scaled, everyone[...], preferred_element_type=f32)
        out[pl.ds(at, LANES), :] = product.astype(bf16)
        return 0

    lax.fori_loop(0, 8, rows, 0)


def gram_rows(nodes, weights):
    return pl.pallas_call(
        gram_kernel,
        in_specs=[VMEM] * 2,
        out_specs=VMEM,
        scratch_shapes=[pltpu.VMEM((SHARE + FSHARE, 1024), bf16)],
        out_shape=jax.ShapeDtypeStruct((1024, 1024), bf16),
        compiler_params=params(40),
        name="gram",
    )(nodes, weights)


def across_chips(block):
    groups = [list(range(0, 16, 2)), list(range(1, 16, 2))]
    return lax.all_to_all(block, "band", 0, 0, axis_index_groups=groups, tiled=True)


def sum_everywhere(partial, filtered):
    parts = lax.all_to_all(partial.reshape(128, 8, 1024), ("band", "dom"), 0, 0, tiled=True)
    parts, filtered = lax.optimization_barrier((parts, filtered))
    part = jnp.sum(parts.astype(f32), axis=0)
    copies = jnp.broadcast_to(part[None], (8, 8, 1024))
    return filtered, lax.all_to_all(copies, "dom", 0, 0, tiled=True).reshape(64, 1024)


def body(states, cell_matrix, potential, weights, connectivity, face_nodes, cell_counts):
    band = lax.axis_index("band")
    chip = band // 2
    h = band % 2
    core = h.astype(jnp.int32).reshape(1)

    other = to_mate(states)
    own_cells = lax.dynamic_index_in_dim(
        connectivity.reshape(CELL_NODES, CELLS, 2), h, 2, keepdims=False
    )
    cells = (cell_counts - h + 1) // 2
    live = jnp.arange(CELLS) < cells[0]
    index = jnp.where(live[:, None], own_cells.T, EXT)
    index = jnp.pad(index, ((1, ROWS - 1 - CELLS), (0, 1024 - CELL_NODES)), constant_values=EXT)
    index = index.reshape(ROWS, 8, LANES)
    matrix = jnp.pad(cell_matrix, ((0, MAT - CELL_NODES),) * 2)
    faces = own_faces(face_nodes, states)
    ghosts = along_dom(faces, -1)
    ghosts_other = along_dom_crossed(faces, -1)
    field, half, raised, start = turn(core, states, other, potential)
    scalars = (core, cells, face_nodes, potential, index)
    kept, sent, edge_kept, edge_sent = apply(
        first_kernel, 1, 2, *scalars, field, start, matrix, ghosts, ghosts_other
    )
    edge = edge_kept + to_mate(edge_sent)
    sent, edge = lax.optimization_barrier((sent, edge))
    came = to_mate(sent)
    rounded = ((kept + came) * 0.25).astype(bf16)
    back = along_dom(edge[:HFACE].astype(bf16), 1)
    ahead = along_dom(edge[HFACE:].astype(bf16), -1)
    theirs = to_mate(rounded)
    kept, came, _ = lax.optimization_barrier((kept, came, rounded))
    start = raised * ((kept + came) * 0.25) - 2.0 * half
    back, ahead, start = lax.optimization_barrier((back, ahead, start))
    inner = (lax.axis_index("dom") < 7).astype(f32)
    edge_mine = jnp.concatenate(
        [(edge[:HFACE] + ahead.astype(f32)) * inner, edge[HFACE:] + back.astype(f32)]
    )
    edge_mine = (edge_mine * 0.25).astype(bf16)
    edge_other = to_mate(edge_mine)
    kept, sent, edge_kept, edge_sent = apply(
        second_kernel, 2, 3, *scalars, rounded, theirs, start, matrix, edge_mine, edge_other, back
    )
    edge = edge_kept + to_mate(edge_sent)
    sent, edge = lax.optimization_barrier((sent, edge))
    came = to_mate(sent)
    back = along_dom(edge[:HFACE].astype(bf16), 1)
    everyone = across_chips(outgoing(kept, came, edge[HFACE:], back))
    mine, theirs = finish(core, face_nodes, kept, came, back, to_mate(back))
    begin = h * HALF + chip * SHARE
    place = jnp.stack([begin, h * HFACE + chip * FSHARE]).astype(jnp.int32)
    own = lax.dynamic_slice(weights, (begin,), (SHARE,))
    weight = weigh(place, face_nodes, weights, own)
    everyone, weight, mine, theirs = lax.optimization_barrier((everyone, weight, mine, theirs))
    partial = gram_rows(everyone, weight)
    filtered = assemble(core, mine, to_mate(theirs))
    return sum_everywhere(partial, filtered)


def solution(mesh):
    in_specs = (P("band", "dom"), P(), P("dom"), P("dom"), P(None, "dom"), P("dom"), P("dom"))
    out_specs = (P("band", "dom"), P("band", None))
    return jax.shard_map(body, mesh=mesh, in_specs=in_specs, out_specs=out_specs, check_vma=False)
```

```python
import functools

import jax
import jax.numpy as jnp
from jax import lax
from jax.experimental import pallas as pl
from jax.experimental.pallas import tpu as pltpu
from jax.sharding import PartitionSpec as P

NODES = 18432
HALF = 9216
FACE = 1536
HFACE = 768
EXT = NODES + FACE
CELL_NODES = 343
CELLS = 64
ROWS = 70
MAT = 352
LANES = 128
ACCS = 4
SPARE = 8
SHARE = HALF // 8
FSHARE = HFACE // 8
BLOCK = 3072
PIECE = 4608
VMEM = pl.BlockSpec(memory_space=pltpu.VMEM)
SMEM = pl.BlockSpec(memory_space=pltpu.SMEM)
ANY = pl.BlockSpec(memory_space=pl.ANY)
f32 = jnp.float32
bf16 = jnp.bfloat16


def to_mate(block):
    return lax.ppermute(block, "band", [(i, i ^ 1) for i in range(16)])


def along_dom(block, shift):
    return lax.ppermute(block, "dom", [(i, i + shift) for i in range(8) if 0 <= i + shift < 8])


def along_dom_crossed(block, shift):
    pairs = [(i, i + shift, j) for i in range(8) for j in range(16) if 0 <= i + shift < 8]
    route = [(i * 16 + (j ^ 1), to * 16 + j) for i, to, j in pairs]
    return lax.ppermute(block, ("dom", "band"), route)


FREE = pl.CostEstimate(flops=0, bytes_accessed=0, transcendentals=0)


def params(mib):
    return pltpu.CompilerParams(vmem_limit_bytes=mib * 2**20)


def eye():
    rows = lax.broadcasted_iota(jnp.int32, (LANES, LANES), 0)
    return jnp.where(rows == lax.broadcasted_iota(jnp.int32, (LANES, LANES), 1), 1.0, 0.0).astype(bf16)


def turned_by(unit, block):
    return lax.dot_general(unit, block, (((1,), (1,)), ((), ())), preferred_element_type=f32)


def faces_kernel(face, own, out, whole, picked):
    step = pl.program_id(0)
    unit = eye()
    block = own[...].astype(bf16)
    for j in range(BLOCK // LANES):
        rows = pl.ds(pl.multiple_of(step * BLOCK + j * LANES, LANES), LANES)
        whole[rows, pl.ds(0, 64)] = turned_by(unit, block[:, j * LANES : (j + 1) * LANES])

    @pl.when(step == NODES // BLOCK - 1)
    def _():
        def pick(i, _):
            for k in range(16):
                at = i * 16 + k
                picked[pl.ds(at, 1), :] = whole[pl.ds(face[at], 1), :]
            return 0

        lax.fori_loop(0, FACE // 16, pick, 0)
        left = lax.broadcasted_iota(jnp.int32, (HFACE, LANES), 1) < 64
        right = pltpu.roll(picked[pl.ds(HFACE, HFACE), :], 64, 1)
        out[...] = jnp.where(left, picked[pl.ds(0, HFACE), :], right).astype(bf16)


def own_faces(face, own):
    return pl.pallas_call(
        faces_kernel,
        grid_spec=pltpu.PrefetchScalarGridSpec(
            num_scalar_prefetch=1,
            grid=(NODES // BLOCK,),
            in_specs=[pl.BlockSpec((64, BLOCK), lambda i, f: (0, i))],
            out_specs=pl.BlockSpec((HFACE, LANES), lambda i, f: (0, 0)),
            scratch_shapes=[pltpu.VMEM((NODES, LANES), f32), pltpu.VMEM((FACE, LANES), f32)],
        ),
        out_shape=jax.ShapeDtypeStruct((HFACE, LANES), bf16),
        compiler_params=params(60),
        name="faces",
        cost_estimate=FREE,
    )(face, own)


def turn_kernel(core, own, other, potential, field, half, raised, start):
    step = pl.program_id(0)
    first = core[0] == 0
    low = jnp.where(first, own[...], other[...])
    high = jnp.where(first, other[...], own[...])
    block = jnp.concatenate([low, high], axis=0)
    field[...] = block.astype(bf16).T

    @pl.when(step // (HALF // BLOCK) == core[0])
    def _():
        half[...] = block.T
        for j in range(BLOCK // LANES):
            rows = pl.ds(j * LANES, LANES)
            row = potential[0, pl.ds(j, 1), :] - 6.0
            column = jnp.broadcast_to(row, (LANES, LANES)).T
            raised[rows, :] = column
            start[rows, :] = column * half[rows, :]


def turn(core, own, other, potential):
    half = pl.BlockSpec((BLOCK, LANES), lambda i, c: (jnp.clip(i - HALF // BLOCK * c[0], 0, HALF // BLOCK - 1), 0))
    return pl.pallas_call(
        turn_kernel,
        grid_spec=pltpu.PrefetchScalarGridSpec(
            num_scalar_prefetch=1,
            grid=(NODES // BLOCK,),
            in_specs=[pl.BlockSpec((64, BLOCK), lambda i, c: (0, i))] * 2
            + [pl.BlockSpec((1, BLOCK // LANES, LANES), lambda i, c: (i, 0, 0))],
            out_specs=[pl.BlockSpec((BLOCK, LANES), lambda i, c: (i, 0)), half, half, half],
        ),
        out_shape=[jax.ShapeDtypeStruct((NODES, LANES), bf16)]
        + [jax.ShapeDtypeStruct((HALF, LANES), f32)] * 3,
        compiler_params=params(60),
        name="turn",
        cost_estimate=FREE,
    )(core, own, other, potential.reshape(NODES // BLOCK, BLOCK // LANES, LANES))


def apply_kernel(
    second, core, cells, face, potential,
    index, field, start, matrix, ghosts, edge_mine, edge_other, back,
    kept, sent, edge_kept, edge_sent,
    x, g0, g1, p0, p1, stage, picked, *rest,
):
    accs = rest[:ACCS]
    ahead, behind, sems, slots = rest[ACCS : ACCS + 4], rest[ACCS + 4 : ACCS + 8], rest[-2], rest[-1]
    h = core[0]
    mine = pl.multiple_of(h * HALF, HALF)
    theirs = pl.multiple_of((1 - h) * HALF, HALF)
    load = pltpu.make_async_copy(start, accs[0].at[pl.ds(mine, HALF)], sems.at[0])
    copies = []
    for k in range(NODES // PIECE):
        ref, at = (field[0], k * PIECE) if len(field) == 1 else (field[k // 2], k % 2 * PIECE)
        copies.append(
            pltpu.make_async_copy(
                ref.at[pl.ds(at, PIECE)], stage.at[pl.ds(k * PIECE, PIECE)], sems.at[k + 1]
            )
        )
    for copy in copies:
        copy.start()
    load.start()

    def fetch(stage_number, cell):
        row = cell + 1
        a = pltpu.make_async_copy(index.at[row + 1], ahead[stage_number], slots.at[stage_number])
        b = pltpu.make_async_copy(index.at[row - 1], behind[stage_number], slots.at[4 + stage_number])
        return a, b

    for k in range(4):
        for copy in fetch(k, k):
            copy.start()

    zeros = jnp.zeros((256, LANES), f32)

    def clear(i, _):
        for a in accs[1:]:
            a[pl.ds(pl.multiple_of(i * 256, 256), 256), :] = zeros
        return 0

    lax.fori_loop(0, EXT // 256, clear, 0)

    def clear_first(i, _):
        accs[0][pl.ds(pl.multiple_of(theirs + i * 256, 256), 256), :] = zeros
        return 0

    lax.fori_loop(0, HALF // 256, clear_first, 0)
    accs[0][pl.ds(NODES, FACE), :] = jnp.zeros((FACE, LANES), f32)
    for ref in (x, *accs):
        ref[pl.ds(EXT, SPARE), :] = jnp.zeros((SPARE, LANES), f32)
    for ref in (g0, g1, p0, p1):
        ref[...] = jnp.zeros_like(ref)

    if second:
        for edge, part in ((edge_mine, h), (edge_other, 1 - h)):
            to = pl.multiple_of(NODES + part * HFACE, HFACE)
            x[pl.ds(to, HFACE), :] = edge[pl.ds(0, HFACE), :].astype(f32)
            picked[pl.ds(pl.multiple_of(part * HFACE, HFACE), HFACE), :] = edge[
                pl.ds(HFACE, HFACE), :
            ].astype(f32)
    else:
        first = core[0] == 0
        own, other = ghosts[0][...].astype(f32), ghosts[1][...].astype(f32)
        low, high = jnp.where(first, own, other), jnp.where(first, other, own)
        left = lax.broadcasted_iota(jnp.int32, (HFACE, LANES), 1) < 64
        x[pl.ds(NODES, HFACE), :] = jnp.where(left, low, pltpu.roll(high, 64, 1))
        x[pl.ds(NODES + HFACE, HFACE), :] = jnp.where(left, pltpu.roll(low, 64, 1), high)

    for k, copy in enumerate(copies):
        copy.wait()
        if second:
            base = (mine if k < 2 else theirs) + k % 2 * PIECE
        else:
            base = k * PIECE

        def widen(i, _, k=k, base=base):
            at = pl.multiple_of(k * PIECE + i * 256, 256)
            rows = pl.ds(pl.multiple_of(base + i * 256, 256), 256)
            x[rows, :] = stage[pl.ds(at, 256), :].astype(f32)
            return 0

        lax.fori_loop(0, PIECE // 256, widen, 0)
    load.wait()

    if second:

        def put(i, _):
            for k in range(16):
                at = i * 16 + k
                x[pl.ds(face[at], 1), :] = picked[pl.ds(at, 1), :]
            return 0

        lax.fori_loop(0, FACE // 16, put, 0)

        picked[pl.ds(0, HFACE), :] = back[...].astype(f32)

        def shift(i, _):
            for j in range(0, 16, ACCS):
                at = [i * 16 + j + k for k in range(ACCS)]
                node = [face[h * HFACE + a] for a in at]
                gain = [(potential[n] - 6.0) * 0.25 for n in node]
                sums = [
                    accs[k][pl.ds(node[k], 1), :] + picked[pl.ds(at[k], 1), :] * gain[k]
                    for k in range(ACCS)
                ]
                for k in range(ACCS):
                    accs[k][pl.ds(node[k], 1), :] = sums[k]
            return 0

        lax.fori_loop(0, HFACE // 16, shift, 0)

    def gather(g, nodes, lo, hi):
        for a in range(lo, min(hi, CELL_NODES)):
            g[pl.ds(a, 1), :] = x[pl.ds(nodes[a // LANES, a % LANES], 1), :]

    def scatter(p, nodes, lo, hi):
        for a in range(lo, min(hi, CELL_NODES), 2 * ACCS):
            count = min(2 * ACCS, CELL_NODES - a)
            at = [nodes[(a + k) // LANES, (a + k) % LANES] for k in range(count)]
            held = [accs[k % ACCS][pl.ds(at[k], 1), :] for k in range(count)]
            sums = []
            for k in range(count):
                if k >= ACCS:
                    held[k] = jnp.where(at[k] == at[k - ACCS], sums[k - ACCS], held[k])
                sums.append(held[k] + p[pl.ds(a + k, 1), :])
            for k in range(count):
                accs[k % ACCS][pl.ds(at[k], 1), :] = sums[k]

    def step(k, cell):
        g_now, g_next, p_now, p_last = (g0, g1, p0, p1) if k % 2 == 0 else (g1, g0, p1, p0)
        for copy in fetch(k, cell + k):
            copy.wait()
        p_now[...] = jnp.dot(matrix[...], g_now[...].astype(bf16), preferred_element_type=f32)
        for lo in range(0, CELL_NODES, 8):
            scatter(p_last, behind[k], lo, lo + 8)
            gather(g_next, ahead[k], lo, lo + 8)
        for copy in fetch(k, cell + 4 + k):
            copy.start()

    first = pltpu.make_async_copy(index.at[1], rest[ACCS + 8], slots.at[8])
    first.start()
    first.wait()
    gather(g0, rest[ACCS + 8], 0, CELL_NODES)

    def four(i, _):
        for k in range(4):
            step(k, 4 * i)
        return 0

    fours = (cells[0] + 3) // 4
    lax.fori_loop(0, fours, four, 0)
    for k in range(4):
        for copy in fetch(k, 4 * fours + k):
            copy.wait()
    scatter(p1, behind[0], 0, CELL_NODES)

    def total(begin, count):
        def add(i, _):
            rows = pl.ds(pl.multiple_of(begin + i * 256, 256), 256)
            accs[0][rows, :] = (accs[0][rows, :] + accs[1][rows, :]) + (
                accs[2][rows, :] + accs[3][rows, :]
            )
            return 0

        lax.fori_loop(0, count // 256, add, 0)

    writes = []

    def write(source, target):
        writes.append(pltpu.make_async_copy(source, target, sems.at[len(writes)]))
        writes[-1].start()

    for begin, target in ((theirs, sent), (mine, kept)):
        for at in range(0, HALF, PIECE):
            total(begin + at, PIECE)
            write(
                accs[0].at[pl.ds(pl.multiple_of(begin + at, PIECE), PIECE)],
                target.at[pl.ds(at, PIECE)],
            )
    total(NODES, FACE)

    def pick(i, _):
        for k in range(16):
            at = i * 16 + k
            picked[pl.ds(at, 1), :] = accs[0][pl.ds(face[at], 1), :]
        return 0

    lax.fori_loop(0, FACE // 16, pick, 0)
    for part, target in ((1 - h, edge_sent), (h, edge_kept)):
        ghost = pl.multiple_of(NODES + part * HFACE, HFACE)
        write(accs[0].at[pl.ds(ghost, HFACE)], target.at[pl.ds(0, HFACE)])
        own = pl.multiple_of(part * HFACE, HFACE)
        write(picked.at[pl.ds(own, HFACE)], target.at[pl.ds(HFACE, HFACE)])
    for w in writes:
        w.wait()


def first_kernel(core, cells, face, potential, index, field, start, matrix, own, other, *rest):
    apply_kernel(
        False, core, cells, face, potential, index,
        (field,), start, matrix, (own, other), None, None, None, *rest,
    )


def second_kernel(
    core, cells, face, potential, index, mine, theirs, start, matrix,
    edge_mine, edge_other, back, *rest,
):
    apply_kernel(
        True, core, cells, face, potential, index,
        (mine, theirs), start, matrix, None, edge_mine, edge_other, back, *rest,
    )


def apply(kernel, fields, edges, *operands):
    edge = jax.ShapeDtypeStruct((FACE, LANES), f32)
    half = jax.ShapeDtypeStruct((HALF, LANES), f32)
    return pl.pallas_call(
        kernel,
        in_specs=[SMEM] * 4 + [ANY] * (2 + fields) + [VMEM] * (1 + edges),
        out_specs=[ANY] * 4,
        scratch_shapes=[pltpu.VMEM((EXT + SPARE, LANES), f32)]
        + [pltpu.VMEM((MAT, LANES), f32)] * 4
        + [pltpu.VMEM((NODES, LANES), bf16), pltpu.VMEM((FACE, LANES), f32)]
        + [pltpu.VMEM((EXT + SPARE, LANES), f32)] * ACCS
        + [pltpu.SMEM((8, LANES), jnp.int32)] * 9
        + [pltpu.SemaphoreType.DMA((8,)), pltpu.SemaphoreType.DMA((9,))],
        out_shape=[half, half, edge, edge],
        compiler_params=params(61),
        name="apply",
    )(*operands)


def finish_kernel(core, face, kept, came, back_mine, back_other, mine, theirs, sums, wide):
    def add(i, _):
        rows = pl.ds(pl.multiple_of(i * 256, 256), 256)
        sums[rows, :] = (kept[rows, :] + came[rows, :]) * 0.5
        return 0

    lax.fori_loop(0, HALF // 256, add, 0)
    sums[pl.ds(HALF, SPARE), :] = jnp.zeros((SPARE, LANES), f32)
    base = core[0] * HALF
    for back, part in ((back_mine, core[0]), (back_other, 1 - core[0])):
        wide[...] = back[...].astype(f32)

        def put(i, _, part=part):
            for k in range(8):
                at = i * 8 + k
                node = face[part * HFACE + at] - base
                node = jnp.where((node >= 0) & (node < HALF), node, HALF)
                sums[pl.ds(node, 1), :] += wide[pl.ds(at, 1), :] * 0.5
            return 0

        lax.fori_loop(0, HFACE // 8, put, 0)

    def out(i, _):
        rows = pl.ds(pl.multiple_of(i * 256, 256), 256)
        block = sums[rows, :].T
        mine[:, rows] = jnp.where(core[0] == 0, block[:64], block[64:])
        theirs[:, rows] = jnp.where(core[0] == 0, block[64:], block[:64])
        return 0

    lax.fori_loop(0, HALF // 256, out, 0)


def finish(core, face, kept, came, back_mine, back_other):
    return pl.pallas_call(
        finish_kernel,
        in_specs=[SMEM] * 2 + [VMEM] * 4,
        out_specs=[VMEM] * 2,
        scratch_shapes=[pltpu.VMEM((HALF + SPARE, LANES), f32), pltpu.VMEM((HFACE, LANES), f32)],
        out_shape=[jax.ShapeDtypeStruct((64, HALF), f32)] * 2,
        compiler_params=params(60),
        name="finish",
        cost_estimate=FREE,
    )(core, face, kept, came, back_mine, back_other)


def place_kernel(core, mine, theirs, out):
    out[...] = jnp.where(pl.program_id(0) // (HALF // BLOCK) == core[0], mine[...], theirs[...])


def assemble(core, mine, theirs):
    last = HALF // BLOCK - 1
    return pl.pallas_call(
        place_kernel,
        grid_spec=pltpu.PrefetchScalarGridSpec(
            num_scalar_prefetch=1,
            grid=(NODES // BLOCK,),
            in_specs=[
                pl.BlockSpec((64, BLOCK), lambda i, c: (0, jnp.clip(i - (last + 1) * c[0], 0, last))),
                pl.BlockSpec((64, BLOCK), lambda i, c: (0, jnp.clip(i - (last + 1) * (1 - c[0]), 0, last))),
            ],
            out_specs=pl.BlockSpec((64, BLOCK), lambda i, c: (0, i)),
        ),
        out_shape=jax.ShapeDtypeStruct((64, NODES), f32),
        compiler_params=params(40),
        name="place",
        cost_estimate=FREE,
    )(core, mine, theirs)


def weigh_kernel(place, face, weights, own, out, rows):
    for j in range(SHARE // LANES):
        row = jnp.broadcast_to(own[pl.ds(j, 1), :], (LANES, LANES))
        rows[pl.ds(j * LANES, LANES), :] = row.T
    zero = jnp.zeros((1, LANES), f32)

    def drop(i, _):
        for k in range(8):
            node = face[i * 8 + k] - place[0]
            node = jnp.where((node >= 0) & (node < SHARE), node, SHARE)
            rows[pl.ds(node, 1), :] = zero
        return 0

    lax.fori_loop(0, FACE // 8, drop, 0)
    out[pl.ds(0, SHARE), :] = rows[pl.ds(0, SHARE), :]

    def add(i, _):
        for k in range(8):
            at = i * 8 + k
            out[pl.ds(SHARE + at, 1), :] = jnp.full((1, LANES), weights[face[place[1] + at]], f32)
        return 0

    lax.fori_loop(0, FSHARE // 8, add, 0)


def weigh(place, face, weights, own):
    return pl.pallas_call(
        weigh_kernel,
        in_specs=[SMEM] * 3 + [VMEM],
        out_specs=VMEM,
        scratch_shapes=[pltpu.VMEM((SHARE + SPARE, LANES), f32)],
        out_shape=jax.ShapeDtypeStruct((SHARE + FSHARE, LANES), f32),
        compiler_params=params(60),
        name="weigh",
        cost_estimate=FREE,
    )(place, face, weights, own.reshape(SHARE // LANES, LANES))


def outgoing_kernel(kept, came, edge, back, out):
    out[0, pl.ds(0, SHARE), :] = ((kept[...] + came[...]) * 0.5).astype(bf16)
    out[0, pl.ds(SHARE, FSHARE), :] = ((edge[...] + back[...].astype(f32)) * 0.5).astype(bf16)


def outgoing(kept, came, edge, back):
    nodes = pl.BlockSpec((SHARE, LANES), lambda i: (i, 0))
    faces = pl.BlockSpec((FSHARE, LANES), lambda i: (i, 0))
    return pl.pallas_call(
        outgoing_kernel,
        grid=(8,),
        in_specs=[nodes, nodes, faces, faces],
        out_specs=pl.BlockSpec((1, SHARE + FSHARE, LANES), lambda i: (i, 0, 0)),
        out_shape=jax.ShapeDtypeStruct((8, SHARE + FSHARE, LANES), bf16),
        compiler_params=params(60),
        name="outgoing",
        cost_estimate=FREE,
    )(kept, came, edge, back)


def gram_kernel(nodes, weights, out, everyone):
    for q in range(8):
        lanes = pl.ds(q * LANES, LANES)
        everyone[:, lanes] = nodes[q]

    def rows(q, _):
        at = pl.multiple_of(q * LANES, LANES)
        block = everyone[:, pl.ds(at, LANES)].astype(f32)
        scaled = (weights[...] * block).T.astype(bf16)
        product = jnp.dot(scaled, everyone[...], preferred_element_type=f32)
        out[pl.ds(at, LANES), :] = product.astype(bf16)
        return 0

    lax.fori_loop(0, 8, rows, 0)


def gram_rows(nodes, weights):
    return pl.pallas_call(
        gram_kernel,
        in_specs=[VMEM] * 2,
        out_specs=VMEM,
        scratch_shapes=[pltpu.VMEM((SHARE + FSHARE, 1024), bf16)],
        out_shape=jax.ShapeDtypeStruct((1024, 1024), bf16),
        compiler_params=params(40),
        name="gram",
    )(nodes, weights)


def across_chips(block):
    groups = [list(range(0, 16, 2)), list(range(1, 16, 2))]
    return lax.all_to_all(block, "band", 0, 0, axis_index_groups=groups, tiled=True)


def sum_everywhere(partial, filtered):
    parts = lax.all_to_all(partial.reshape(128, 8, 1024), ("band", "dom"), 0, 0, tiled=True)
    parts, filtered = lax.optimization_barrier((parts, filtered))
    part = jnp.sum(parts.astype(f32), axis=0)
    copies = jnp.broadcast_to(part[None], (8, 8, 1024))
    return filtered, lax.all_to_all(copies, "dom", 0, 0, tiled=True).reshape(64, 1024)


def body(states, cell_matrix, potential, weights, connectivity, face_nodes, cell_counts):
    band = lax.axis_index("band")
    chip = band // 2
    h = band % 2
    core = h.astype(jnp.int32).reshape(1)

    other = to_mate(states)
    own_cells = lax.dynamic_index_in_dim(
        connectivity.reshape(CELL_NODES, CELLS, 2), h, 2, keepdims=False
    )
    cells = (cell_counts - h + 1) // 2
    live = jnp.arange(CELLS) < cells[0]
    index = jnp.where(live[:, None], own_cells.T, EXT)
    index = jnp.pad(index, ((1, ROWS - 1 - CELLS), (0, 1024 - CELL_NODES)), constant_values=EXT)
    index = index.reshape(ROWS, 8, LANES)
    matrix = jnp.pad(cell_matrix, ((0, MAT - CELL_NODES),) * 2)
    faces = own_faces(face_nodes, states)
    ghosts = along_dom(faces, -1)
    ghosts_other = along_dom_crossed(faces, -1)
    field, half, raised, start = turn(core, states, other, potential)
    scalars = (core, cells, face_nodes, potential, index)
    kept, sent, edge_kept, edge_sent = apply(
        first_kernel, 1, 2, *scalars, field, start, matrix, ghosts, ghosts_other
    )
    edge = edge_kept + to_mate(edge_sent)
    sent, edge = lax.optimization_barrier((sent, edge))
    came = to_mate(sent)
    rounded = ((kept + came) * 0.25).astype(bf16)
    back = along_dom(edge[:HFACE].astype(bf16), 1)
    ahead = along_dom(edge[HFACE:].astype(bf16), -1)
    theirs = to_mate(rounded)
    kept, came, _ = lax.optimization_barrier((kept, came, rounded))
    start = raised * ((kept + came) * 0.25) - 2.0 * half
    back, ahead, start = lax.optimization_barrier((back, ahead, start))
    inner = (lax.axis_index("dom") < 7).astype(f32)
    edge_mine = jnp.concatenate(
        [(edge[:HFACE] + ahead.astype(f32)) * inner, edge[HFACE:] + back.astype(f32)]
    )
    edge_mine = (edge_mine * 0.25).astype(bf16)
    edge_other = to_mate(edge_mine)
    kept, sent, edge_kept, edge_sent = apply(
        second_kernel, 2, 3, *scalars, rounded, theirs, start, matrix, edge_mine, edge_other, back
    )
    edge = edge_kept + to_mate(edge_sent)
    sent, edge = lax.optimization_barrier((sent, edge))
    came = to_mate(sent)
    back = along_dom(edge[:HFACE].astype(bf16), 1)
    everyone = across_chips(outgoing(kept, came, edge[HFACE:], back))
    mine, theirs = finish(core, face_nodes, kept, came, back, to_mate(back))
    begin = h * HALF + chip * SHARE
    place = jnp.stack([begin, h * HFACE + chip * FSHARE]).astype(jnp.int32)
    own = lax.dynamic_slice(weights, (begin,), (SHARE,))
    weight = weigh(place, face_nodes, weights, own)
    everyone, weight, mine, theirs = lax.optimization_barrier((everyone, weight, mine, theirs))
    partial = gram_rows(everyone, weight)
    filtered = assemble(core, mine, to_mate(theirs))
    return sum_everywhere(partial, filtered)


def solution(mesh):
    in_specs = (P("band", "dom"), P(), P("dom"), P("dom"), P(None, "dom"), P("dom"), P("dom"))
    out_specs = (P("band", "dom"), P("band", None))
    return jax.shard_map(body, mesh=mesh, in_specs=in_specs, out_specs=out_specs, check_vma=False)
```

```python
import functools

import jax
import jax.numpy as jnp
from jax import lax
from jax.experimental import pallas as pl
from jax.experimental.pallas import tpu as pltpu
from jax.sharding import PartitionSpec as P

NODES = 18432
HALF = 9216
FACE = 1536
HFACE = 768
EXT = NODES + FACE
CELL_NODES = 343
CELLS = 64
ROWS = 70
MAT = 352
LANES = 128
ACCS = 4
SPARE = 8
SHARE = HALF // 8
FSHARE = HFACE // 8
BLOCK = 3072
PIECE = 4608
VMEM = pl.BlockSpec(memory_space=pltpu.VMEM)
SMEM = pl.BlockSpec(memory_space=pltpu.SMEM)
ANY = pl.BlockSpec(memory_space=pl.ANY)
f32 = jnp.float32
bf16 = jnp.bfloat16


def to_mate(block):
    return lax.ppermute(block, "band", [(i, i ^ 1) for i in range(16)])


def along_dom(block, shift):
    return lax.ppermute(block, "dom", [(i, i + shift) for i in range(8) if 0 <= i + shift < 8])


def along_dom_crossed(block, shift):
    pairs = [(i, i + shift, j) for i in range(8) for j in range(16) if 0 <= i + shift < 8]
    route = [(i * 16 + (j ^ 1), to * 16 + j) for i, to, j in pairs]
    return lax.ppermute(block, ("dom", "band"), route)


FREE = pl.CostEstimate(flops=0, bytes_accessed=0, transcendentals=0)


def params(mib):
    return pltpu.CompilerParams(vmem_limit_bytes=mib * 2**20)


def eye():
    rows = lax.broadcasted_iota(jnp.int32, (LANES, LANES), 0)
    return jnp.where(rows == lax.broadcasted_iota(jnp.int32, (LANES, LANES), 1), 1.0, 0.0).astype(bf16)


def turned_by(unit, block):
    return lax.dot_general(unit, block, (((1,), (1,)), ((), ())), preferred_element_type=f32)


def faces_kernel(face, own, out, whole, picked):
    step = pl.program_id(0)
    unit = eye()
    block = own[...].astype(bf16)
    for j in range(BLOCK // LANES):
        rows = pl.ds(pl.multiple_of(step * BLOCK + j * LANES, LANES), LANES)
        whole[rows, pl.ds(0, 64)] = turned_by(unit, block[:, j * LANES : (j + 1) * LANES])

    @pl.when(step == NODES // BLOCK - 1)
    def _():
        def pick(i, _):
            for k in range(16):
                at = i * 16 + k
                picked[pl.ds(at, 1), :] = whole[pl.ds(face[at], 1), :]
            return 0

        lax.fori_loop(0, FACE // 16, pick, 0)
        left = lax.broadcasted_iota(jnp.int32, (HFACE, LANES), 1) < 64
        right = pltpu.roll(picked[pl.ds(HFACE, HFACE), :], 64, 1)
        out[...] = jnp.where(left, picked[pl.ds(0, HFACE), :], right).astype(bf16)


def own_faces(face, own):
    return pl.pallas_call(
        faces_kernel,
        grid_spec=pltpu.PrefetchScalarGridSpec(
            num_scalar_prefetch=1,
            grid=(NODES // BLOCK,),
            in_specs=[pl.BlockSpec((64, BLOCK), lambda i, f: (0, i))],
            out_specs=pl.BlockSpec((HFACE, LANES), lambda i, f: (0, 0)),
            scratch_shapes=[pltpu.VMEM((NODES, LANES), f32), pltpu.VMEM((FACE, LANES), f32)],
        ),
        out_shape=jax.ShapeDtypeStruct((HFACE, LANES), bf16),
        compiler_params=params(60),
        name="faces",
        cost_estimate=FREE,
    )(face, own)


def turn_kernel(core, own, other, potential, field, half, raised, start):
    step = pl.program_id(0)
    first = core[0] == 0
    low = jnp.where(first, own[...], other[...])
    high = jnp.where(first, other[...], own[...])
    block = jnp.concatenate([low, high], axis=0)
    field[...] = block.astype(bf16).T

    @pl.when(step // (HALF // BLOCK) == core[0])
    def _():
        half[...] = block.T
        for j in range(BLOCK // LANES):
            rows = pl.ds(j * LANES, LANES)
            row = potential[0, pl.ds(j, 1), :] - 6.0
            column = jnp.broadcast_to(row, (LANES, LANES)).T
            raised[rows, :] = column
            start[rows, :] = column * half[rows, :]


def turn(core, own, other, potential):
    half = pl.BlockSpec((BLOCK, LANES), lambda i, c: (jnp.clip(i - HALF // BLOCK * c[0], 0, HALF // BLOCK - 1), 0))
    return pl.pallas_call(
        turn_kernel,
        grid_spec=pltpu.PrefetchScalarGridSpec(
            num_scalar_prefetch=1,
            grid=(NODES // BLOCK,),
            in_specs=[pl.BlockSpec((64, BLOCK), lambda i, c: (0, i))] * 2
            + [pl.BlockSpec((1, BLOCK // LANES, LANES), lambda i, c: (i, 0, 0))],
            out_specs=[pl.BlockSpec((BLOCK, LANES), lambda i, c: (i, 0)), half, half, half],
        ),
        out_shape=[jax.ShapeDtypeStruct((NODES, LANES), bf16)]
        + [jax.ShapeDtypeStruct((HALF, LANES), f32)] * 3,
        compiler_params=params(60),
        name="turn",
        cost_estimate=FREE,
    )(core, own, other, potential.reshape(NODES // BLOCK, BLOCK // LANES, LANES))


def apply_kernel(
    second, core, cells, face, potential,
    index, field, start, matrix, ghosts, edge_mine, edge_other, back,
    kept, sent, edge_kept, edge_sent,
    x, g0, g1, p0, p1, stage, picked, *rest,
):
    accs = rest[:ACCS]
    ahead, behind, sems, slots = rest[ACCS : ACCS + 4], rest[ACCS + 4 : ACCS + 8], rest[-2], rest[-1]
    h = core[0]
    mine = pl.multiple_of(h * HALF, HALF)
    theirs = pl.multiple_of((1 - h) * HALF, HALF)
    load = pltpu.make_async_copy(start, accs[0].at[pl.ds(mine, HALF)], sems.at[0])
    copies = []
    for k in range(NODES // PIECE):
        ref, at = (field[0], k * PIECE) if len(field) == 1 else (field[k // 2], k % 2 * PIECE)
        copies.append(
            pltpu.make_async_copy(
                ref.at[pl.ds(at, PIECE)], stage.at[pl.ds(k * PIECE, PIECE)], sems.at[k + 1]
            )
        )
    for copy in copies:
        copy.start()
    load.start()

    def fetch(stage_number, cell):
        row = cell + 1
        a = pltpu.make_async_copy(index.at[row + 1], ahead[stage_number], slots.at[stage_number])
        b = pltpu.make_async_copy(index.at[row - 1], behind[stage_number], slots.at[4 + stage_number])
        return a, b

    for k in range(4):
        for copy in fetch(k, k):
            copy.start()

    zeros = jnp.zeros((256, LANES), f32)

    def clear(i, _):
        for a in accs[1:]:
            a[pl.ds(pl.multiple_of(i * 256, 256), 256), :] = zeros
        return 0

    lax.fori_loop(0, EXT // 256, clear, 0)

    def clear_first(i, _):
        accs[0][pl.ds(pl.multiple_of(theirs + i * 256, 256), 256), :] = zeros
        return 0

    lax.fori_loop(0, HALF // 256, clear_first, 0)
    accs[0][pl.ds(NODES, FACE), :] = jnp.zeros((FACE, LANES), f32)
    for ref in (x, *accs):
        ref[pl.ds(EXT, SPARE), :] = jnp.zeros((SPARE, LANES), f32)
    for ref in (g0, g1, p0, p1):
        ref[...] = jnp.zeros_like(ref)

    if second:
        for edge, part in ((edge_mine, h), (edge_other, 1 - h)):
            to = pl.multiple_of(NODES + part * HFACE, HFACE)
            x[pl.ds(to, HFACE), :] = edge[pl.ds(0, HFACE), :].astype(f32)
            picked[pl.ds(pl.multiple_of(part * HFACE, HFACE), HFACE), :] = edge[
                pl.ds(HFACE, HFACE), :
            ].astype(f32)
    else:
        first = core[0] == 0
        own, other = ghosts[0][...].astype(f32), ghosts[1][...].astype(f32)
        low, high = jnp.where(first, own, other), jnp.where(first, other, own)
        left = lax.broadcasted_iota(jnp.int32, (HFACE, LANES), 1) < 64
        x[pl.ds(NODES, HFACE), :] = jnp.where(left, low, pltpu.roll(high, 64, 1))
        x[pl.ds(NODES + HFACE, HFACE), :] = jnp.where(left, pltpu.roll(low, 64, 1), high)

    for k, copy in enumerate(copies):
        copy.wait()
        if second:
            base = (mine if k < 2 else theirs) + k % 2 * PIECE
        else:
            base = k * PIECE

        def widen(i, _, k=k, base=base):
            at = pl.multiple_of(k * PIECE + i * 256, 256)
            rows = pl.ds(pl.multiple_of(base + i * 256, 256), 256)
            x[rows, :] = stage[pl.ds(at, 256), :].astype(f32)
            return 0

        lax.fori_loop(0, PIECE // 256, widen, 0)
    load.wait()

    if second:

        def put(i, _):
            for k in range(16):
                at = i * 16 + k
                x[pl.ds(face[at], 1), :] = picked[pl.ds(at, 1), :]
            return 0

        lax.fori_loop(0, FACE // 16, put, 0)

        picked[pl.ds(0, HFACE), :] = back[...].astype(f32)

        def shift(i, _):
            for j in range(0, 16, ACCS):
                at = [i * 16 + j + k for k in range(ACCS)]
                node = [face[h * HFACE + a] for a in at]
                gain = [(potential[n] - 6.0) * 0.25 for n in node]
                sums = [
                    accs[k][pl.ds(node[k], 1), :] + picked[pl.ds(at[k], 1), :] * gain[k]
                    for k in range(ACCS)
                ]
                for k in range(ACCS):
                    accs[k][pl.ds(node[k], 1), :] = sums[k]
            return 0

        lax.fori_loop(0, HFACE // 16, shift, 0)

    def gather(g, nodes, lo, hi):
        for a in range(lo, min(hi, CELL_NODES)):
            g[pl.ds(a, 1), :] = x[pl.ds(nodes[a // LANES, a % LANES], 1), :]

    def scatter(p, nodes, lo, hi):
        for a in range(lo, min(hi, CELL_NODES), 2 * ACCS):
            count = min(2 * ACCS, CELL_NODES - a)
            at = [nodes[(a + k) // LANES, (a + k) % LANES] for k in range(count)]
            held = [accs[k % ACCS][pl.ds(at[k], 1), :] for k in range(count)]
            sums = []
            for k in range(count):
                if k >= ACCS:
                    held[k] = jnp.where(at[k] == at[k - ACCS], sums[k - ACCS], held[k])
                sums.append(held[k] + p[pl.ds(a + k, 1), :])
            for k in range(count):
                accs[k % ACCS][pl.ds(at[k], 1), :] = sums[k]

    def step(k, cell):
        g_now, g_next, p_now, p_last = (g0, g1, p0, p1) if k % 2 == 0 else (g1, g0, p1, p0)
        for copy in fetch(k, cell + k):
            copy.wait()
        p_now[...] = jnp.dot(matrix[...], g_now[...].astype(bf16), preferred_element_type=f32)
        for lo in range(0, CELL_NODES, 8):
            scatter(p_last, behind[k], lo, lo + 8)
            gather(g_next, ahead[k], lo, lo + 8)
        for copy in fetch(k, cell + 4 + k):
            copy.start()

    first = pltpu.make_async_copy(index.at[1], rest[ACCS + 8], slots.at[8])
    first.start()
    first.wait()
    gather(g0, rest[ACCS + 8], 0, CELL_NODES)

    def four(i, _):
        for k in range(4):
            step(k, 4 * i)
        return 0

    fours = (cells[0] + 3) // 4
    lax.fori_loop(0, fours, four, 0)
    for k in range(4):
        for copy in fetch(k, 4 * fours + k):
            copy.wait()
    scatter(p1, behind[0], 0, CELL_NODES)

    def total(begin, count):
        def add(i, _):
            rows = pl.ds(pl.multiple_of(begin + i * 256, 256), 256)
            accs[0][rows, :] = (accs[0][rows, :] + accs[1][rows, :]) + (
                accs[2][rows, :] + accs[3][rows, :]
            )
            return 0

        lax.fori_loop(0, count // 256, add, 0)

    writes = []

    def write(source, target):
        writes.append(pltpu.make_async_copy(source, target, sems.at[len(writes)]))
        writes[-1].start()

    for begin, target in ((theirs, sent), (mine, kept)):
        for at in range(0, HALF, PIECE):
            total(begin + at, PIECE)
            write(
                accs[0].at[pl.ds(pl.multiple_of(begin + at, PIECE), PIECE)],
                target.at[pl.ds(at, PIECE)],
            )
    total(NODES, FACE)

    def pick(i, _):
        for k in range(16):
            at = i * 16 + k
            picked[pl.ds(at, 1), :] = accs[0][pl.ds(face[at], 1), :]
        return 0

    lax.fori_loop(0, FACE // 16, pick, 0)
    for part, target in ((1 - h, edge_sent), (h, edge_kept)):
        ghost = pl.multiple_of(NODES + part * HFACE, HFACE)
        write(accs[0].at[pl.ds(ghost, HFACE)], target.at[pl.ds(0, HFACE)])
        own = pl.multiple_of(part * HFACE, HFACE)
        write(picked.at[pl.ds(own, HFACE)], target.at[pl.ds(HFACE, HFACE)])
    for w in writes:
        w.wait()


def first_kernel(core, cells, face, potential, index, field, start, matrix, own, other, *rest):
    apply_kernel(
        False, core, cells, face, potential, index,
        (field,), start, matrix, (own, other), None, None, None, *rest,
    )


def second_kernel(
    core, cells, face, potential, index, mine, theirs, start, matrix,
    edge_mine, edge_other, back, *rest,
):
    apply_kernel(
        True, core, cells, face, potential, index,
        (mine, theirs), start, matrix, None, edge_mine, edge_other, back, *rest,
    )


def apply(kernel, fields, edges, *operands):
    edge = jax.ShapeDtypeStruct((FACE, LANES), f32)
    half = jax.ShapeDtypeStruct((HALF, LANES), f32)
    return pl.pallas_call(
        kernel,
        in_specs=[SMEM] * 4 + [ANY] * (2 + fields) + [VMEM] * (1 + edges),
        out_specs=[ANY] * 4,
        scratch_shapes=[pltpu.VMEM((EXT + SPARE, LANES), f32)]
        + [pltpu.VMEM((MAT, LANES), f32)] * 4
        + [pltpu.VMEM((NODES, LANES), bf16), pltpu.VMEM((FACE, LANES), f32)]
        + [pltpu.VMEM((EXT + SPARE, LANES), f32)] * ACCS
        + [pltpu.SMEM((8, LANES), jnp.int32)] * 9
        + [pltpu.SemaphoreType.DMA((8,)), pltpu.SemaphoreType.DMA((9,))],
        out_shape=[half, half, edge, edge],
        compiler_params=params(61),
        name="apply",
    )(*operands)


def finish_kernel(core, face, kept, came, back_mine, back_other, mine, theirs, sums, wide):
    def add(i, _):
        rows = pl.ds(pl.multiple_of(i * 256, 256), 256)
        sums[rows, :] = (kept[rows, :] + came[rows, :]) * 0.5
        return 0

    lax.fori_loop(0, HALF // 256, add, 0)
    sums[pl.ds(HALF, SPARE), :] = jnp.zeros((SPARE, LANES), f32)
    base = core[0] * HALF
    for back, part in ((back_mine, core[0]), (back_other, 1 - core[0])):
        wide[...] = back[...].astype(f32)

        def put(i, _, part=part):
            for k in range(8):
                at = i * 8 + k
                node = face[part * HFACE + at] - base
                node = jnp.where((node >= 0) & (node < HALF), node, HALF)
                sums[pl.ds(node, 1), :] += wide[pl.ds(at, 1), :] * 0.5
            return 0

        lax.fori_loop(0, HFACE // 8, put, 0)

    def out(i, _):
        rows = pl.ds(pl.multiple_of(i * 256, 256), 256)
        block = sums[rows, :].T
        mine[:, rows] = jnp.where(core[0] == 0, block[:64], block[64:])
        theirs[:, rows] = jnp.where(core[0] == 0, block[64:], block[:64])
        return 0

    lax.fori_loop(0, HALF // 256, out, 0)


def finish(core, face, kept, came, back_mine, back_other):
    return pl.pallas_call(
        finish_kernel,
        in_specs=[SMEM] * 2 + [VMEM] * 4,
        out_specs=[VMEM] * 2,
        scratch_shapes=[pltpu.VMEM((HALF + SPARE, LANES), f32), pltpu.VMEM((HFACE, LANES), f32)],
        out_shape=[jax.ShapeDtypeStruct((64, HALF), f32)] * 2,
        compiler_params=params(60),
        name="finish",
        cost_estimate=FREE,
    )(core, face, kept, came, back_mine, back_other)


def place_kernel(core, mine, theirs, out):
    out[...] = jnp.where(pl.program_id(0) // (HALF // BLOCK) == core[0], mine[...], theirs[...])


def assemble(core, mine, theirs):
    last = HALF // BLOCK - 1
    return pl.pallas_call(
        place_kernel,
        grid_spec=pltpu.PrefetchScalarGridSpec(
            num_scalar_prefetch=1,
            grid=(NODES // BLOCK,),
            in_specs=[
                pl.BlockSpec((64, BLOCK), lambda i, c: (0, jnp.clip(i - (last + 1) * c[0], 0, last))),
                pl.BlockSpec((64, BLOCK), lambda i, c: (0, jnp.clip(i - (last + 1) * (1 - c[0]), 0, last))),
            ],
            out_specs=pl.BlockSpec((64, BLOCK), lambda i, c: (0, i)),
        ),
        out_shape=jax.ShapeDtypeStruct((64, NODES), f32),
        compiler_params=params(40),
        name="place",
        cost_estimate=FREE,
    )(core, mine, theirs)


def weigh_kernel(place, face, weights, own, out, rows):
    for j in range(SHARE // LANES):
        row = jnp.broadcast_to(own[pl.ds(j, 1), :], (LANES, LANES))
        rows[pl.ds(j * LANES, LANES), :] = row.T
    zero = jnp.zeros((1, LANES), f32)

    def drop(i, _):
        for k in range(8):
            node = face[i * 8 + k] - place[0]
            node = jnp.where((node >= 0) & (node < SHARE), node, SHARE)
            rows[pl.ds(node, 1), :] = zero
        return 0

    lax.fori_loop(0, FACE // 8, drop, 0)
    out[pl.ds(0, SHARE), :] = rows[pl.ds(0, SHARE), :]

    def add(i, _):
        for k in range(8):
            at = i * 8 + k
            out[pl.ds(SHARE + at, 1), :] = jnp.full((1, LANES), weights[face[place[1] + at]], f32)
        return 0

    lax.fori_loop(0, FSHARE // 8, add, 0)


def weigh(place, face, weights, own):
    return pl.pallas_call(
        weigh_kernel,
        in_specs=[SMEM] * 3 + [VMEM],
        out_specs=VMEM,
        scratch_shapes=[pltpu.VMEM((SHARE + SPARE, LANES), f32)],
        out_shape=jax.ShapeDtypeStruct((SHARE + FSHARE, LANES), f32),
        compiler_params=params(60),
        name="weigh",
        cost_estimate=FREE,
    )(place, face, weights, own.reshape(SHARE // LANES, LANES))


def outgoing_kernel(kept, came, edge, back, out):
    out[0, pl.ds(0, SHARE), :] = ((kept[...] + came[...]) * 0.5).astype(bf16)
    out[0, pl.ds(SHARE, FSHARE), :] = ((edge[...] + back[...].astype(f32)) * 0.5).astype(bf16)


def outgoing(kept, came, edge, back):
    nodes = pl.BlockSpec((SHARE, LANES), lambda i: (i, 0))
    faces = pl.BlockSpec((FSHARE, LANES), lambda i: (i, 0))
    return pl.pallas_call(
        outgoing_kernel,
        grid=(8,),
        in_specs=[nodes, nodes, faces, faces],
        out_specs=pl.BlockSpec((1, SHARE + FSHARE, LANES), lambda i: (i, 0, 0)),
        out_shape=jax.ShapeDtypeStruct((8, SHARE + FSHARE, LANES), bf16),
        compiler_params=params(60),
        name="outgoing",
        cost_estimate=FREE,
    )(kept, came, edge, back)


def gram_kernel(nodes, weights, out, everyone):
    for q in range(8):
        lanes = pl.ds(q * LANES, LANES)
        everyone[:, lanes] = nodes[q]

    def rows(q, _):
        at = pl.multiple_of(q * LANES, LANES)
        block = everyone[:, pl.ds(at, LANES)].astype(f32)
        scaled = (weights[...] * block).T.astype(bf16)
        product = jnp.dot(scaled, everyone[...], preferred_element_type=f32)
        out[pl.ds(at, LANES), :] = product.astype(bf16)
        return 0

    lax.fori_loop(0, 8, rows, 0)


def gram_rows(nodes, weights):
    return pl.pallas_call(
        gram_kernel,
        in_specs=[VMEM] * 2,
        out_specs=VMEM,
        scratch_shapes=[pltpu.VMEM((SHARE + FSHARE, 1024), bf16)],
        out_shape=jax.ShapeDtypeStruct((1024, 1024), bf16),
        compiler_params=params(40),
        name="gram",
    )(nodes, weights)


def across_chips(block):
    groups = [list(range(0, 16, 2)), list(range(1, 16, 2))]
    return lax.all_to_all(block, "band", 0, 0, axis_index_groups=groups, tiled=True)


def sum_everywhere(partial, filtered):
    parts = lax.all_to_all(partial.reshape(128, 8, 1024), ("band", "dom"), 0, 0, tiled=True)
    parts, filtered = lax.optimization_barrier((parts, filtered))
    part = jnp.sum(parts.astype(f32), axis=0)
    copies = jnp.broadcast_to(part[None], (8, 8, 1024))
    return filtered, lax.all_to_all(copies, "dom", 0, 0, tiled=True).reshape(64, 1024)


def body(states, cell_matrix, potential, weights, connectivity, face_nodes, cell_counts):
    band = lax.axis_index("band")
    chip = band // 2
    h = band % 2
    core = h.astype(jnp.int32).reshape(1)

    other = to_mate(states)
    own_cells = lax.dynamic_index_in_dim(
        connectivity.reshape(CELL_NODES, CELLS, 2), h, 2, keepdims=False
    )
    cells = (cell_counts - h + 1) // 2
    live = jnp.arange(CELLS) < cells[0]
    index = jnp.where(live[:, None], own_cells.T, EXT)
    index = jnp.pad(index, ((1, ROWS - 1 - CELLS), (0, 1024 - CELL_NODES)), constant_values=EXT)
    index = index.reshape(ROWS, 8, LANES)
    matrix = jnp.pad(cell_matrix, ((0, MAT - CELL_NODES),) * 2)
    faces = own_faces(face_nodes, states)
    ghosts = along_dom(faces, -1)
    ghosts_other = along_dom_crossed(faces, -1)
    field, half, raised, start = turn(core, states, other, potential)
    scalars = (core, cells, face_nodes, potential, index)
    kept, sent, edge_kept, edge_sent = apply(
        first_kernel, 1, 2, *scalars, field, start, matrix, ghosts, ghosts_other
    )
    sent, arrived = lax.optimization_barrier((sent, to_mate(edge_sent)))
    came = to_mate(sent)
    edge = edge_kept + arrived
    rounded = ((kept + came) * 0.25).astype(bf16)
    back = along_dom(edge[:HFACE].astype(bf16), 1)
    ahead = along_dom(edge[HFACE:].astype(bf16), -1)
    theirs = to_mate(rounded)
    kept, came, _ = lax.optimization_barrier((kept, came, rounded))
    start = raised * ((kept + came) * 0.25) - 2.0 * half
    back, ahead, start = lax.optimization_barrier((back, ahead, start))
    inner = (lax.axis_index("dom") < 7).astype(f32)
    edge_mine = jnp.concatenate(
        [(edge[:HFACE] + ahead.astype(f32)) * inner, edge[HFACE:] + back.astype(f32)]
    )
    edge_mine = (edge_mine * 0.25).astype(bf16)
    edge_other = to_mate(edge_mine)
    kept, sent, edge_kept, edge_sent = apply(
        second_kernel, 2, 3, *scalars, rounded, theirs, start, matrix, edge_mine, edge_other, back
    )
    sent, arrived = lax.optimization_barrier((sent, to_mate(edge_sent)))
    came = to_mate(sent)
    edge = edge_kept + arrived
    back = along_dom(edge[:HFACE].astype(bf16), 1)
    everyone = across_chips(outgoing(kept, came, edge[HFACE:], back))
    mine, theirs = finish(core, face_nodes, kept, came, back, to_mate(back))
    begin = h * HALF + chip * SHARE
    place = jnp.stack([begin, h * HFACE + chip * FSHARE]).astype(jnp.int32)
    own = lax.dynamic_slice(weights, (begin,), (SHARE,))
    weight = weigh(place, face_nodes, weights, own)
    everyone, weight, mine, theirs = lax.optimization_barrier((everyone, weight, mine, theirs))
    partial = gram_rows(everyone, weight)
    filtered = assemble(core, mine, to_mate(theirs))
    return sum_everywhere(partial, filtered)


def solution(mesh):
    in_specs = (P("band", "dom"), P(), P("dom"), P("dom"), P(None, "dom"), P("dom"), P("dom"))
    out_specs = (P("band", "dom"), P("band", None))
    return jax.shard_map(body, mesh=mesh, in_specs=in_specs, out_specs=out_specs, check_vma=False)
```

```python
import functools

import jax
import jax.numpy as jnp
from jax import lax
from jax.experimental import pallas as pl
from jax.experimental.pallas import tpu as pltpu
from jax.sharding import PartitionSpec as P

NODES = 18432
HALF = 9216
FACE = 1536
HFACE = 768
EXT = NODES + FACE
CELL_NODES = 343
CELLS = 64
ROWS = 70
MAT = 352
LANES = 128
ACCS = 4
SPARE = 8
SHARE = HALF // 8
FSHARE = HFACE // 8
BLOCK = 3072
PIECE = 4608
VMEM = pl.BlockSpec(memory_space=pltpu.VMEM)
SMEM = pl.BlockSpec(memory_space=pltpu.SMEM)
ANY = pl.BlockSpec(memory_space=pl.ANY)
f32 = jnp.float32
bf16 = jnp.bfloat16


def to_mate(block):
    return lax.ppermute(block, "band", [(i, i ^ 1) for i in range(16)])


def along_dom(block, shift):
    return lax.ppermute(block, "dom", [(i, i + shift) for i in range(8) if 0 <= i + shift < 8])


def along_dom_crossed(block, shift):
    pairs = [(i, i + shift, j) for i in range(8) for j in range(16) if 0 <= i + shift < 8]
    route = [(i * 16 + (j ^ 1), to * 16 + j) for i, to, j in pairs]
    return lax.ppermute(block, ("dom", "band"), route)


FREE = pl.CostEstimate(flops=0, bytes_accessed=0, transcendentals=0)


def params(mib):
    return pltpu.CompilerParams(vmem_limit_bytes=mib * 2**20)


def eye():
    rows = lax.broadcasted_iota(jnp.int32, (LANES, LANES), 0)
    return jnp.where(rows == lax.broadcasted_iota(jnp.int32, (LANES, LANES), 1), 1.0, 0.0).astype(bf16)


def turned_by(unit, block):
    return lax.dot_general(unit, block, (((1,), (1,)), ((), ())), preferred_element_type=f32)


def faces_kernel(face, own, out, whole, picked):
    step = pl.program_id(0)
    unit = eye()
    block = own[...].astype(bf16)
    for j in range(BLOCK // LANES):
        rows = pl.ds(pl.multiple_of(step * BLOCK + j * LANES, LANES), LANES)
        whole[rows, pl.ds(0, 64)] = turned_by(unit, block[:, j * LANES : (j + 1) * LANES])

    @pl.when(step == NODES // BLOCK - 1)
    def _():
        def pick(i, _):
            for k in range(16):
                at = i * 16 + k
                picked[pl.ds(at, 1), :] = whole[pl.ds(face[at], 1), :]
            return 0

        lax.fori_loop(0, FACE // 16, pick, 0)
        left = lax.broadcasted_iota(jnp.int32, (HFACE, LANES), 1) < 64
        right = pltpu.roll(picked[pl.ds(HFACE, HFACE), :], 64, 1)
        out[...] = jnp.where(left, picked[pl.ds(0, HFACE), :], right).astype(bf16)


def own_faces(face, own):
    return pl.pallas_call(
        faces_kernel,
        grid_spec=pltpu.PrefetchScalarGridSpec(
            num_scalar_prefetch=1,
            grid=(NODES // BLOCK,),
            in_specs=[pl.BlockSpec((64, BLOCK), lambda i, f: (0, i))],
            out_specs=pl.BlockSpec((HFACE, LANES), lambda i, f: (0, 0)),
            scratch_shapes=[pltpu.VMEM((NODES, LANES), f32), pltpu.VMEM((FACE, LANES), f32)],
        ),
        out_shape=jax.ShapeDtypeStruct((HFACE, LANES), bf16),
        compiler_params=params(60),
        name="faces",
        cost_estimate=FREE,
    )(face, own)


def turn_kernel(core, own, other, potential, field, half, raised, start):
    step = pl.program_id(0)
    first = core[0] == 0
    low = jnp.where(first, own[...], other[...])
    high = jnp.where(first, other[...], own[...])
    block = jnp.concatenate([low, high], axis=0)
    field[...] = block.astype(bf16).T

    @pl.when(step // (HALF // BLOCK) == core[0])
    def _():
        half[...] = block.T
        for j in range(BLOCK // LANES):
            rows = pl.ds(j * LANES, LANES)
            row = potential[0, pl.ds(j, 1), :] - 6.0
            column = jnp.broadcast_to(row, (LANES, LANES)).T
            raised[rows, :] = column
            start[rows, :] = column * half[rows, :]


def turn(core, own, other, potential):
    half = pl.BlockSpec((BLOCK, LANES), lambda i, c: (jnp.clip(i - HALF // BLOCK * c[0], 0, HALF // BLOCK - 1), 0))
    return pl.pallas_call(
        turn_kernel,
        grid_spec=pltpu.PrefetchScalarGridSpec(
            num_scalar_prefetch=1,
            grid=(NODES // BLOCK,),
            in_specs=[pl.BlockSpec((64, BLOCK), lambda i, c: (0, i))] * 2
            + [pl.BlockSpec((1, BLOCK // LANES, LANES), lambda i, c: (i, 0, 0))],
            out_specs=[pl.BlockSpec((BLOCK, LANES), lambda i, c: (i, 0)), half, half, half],
        ),
        out_shape=[jax.ShapeDtypeStruct((NODES, LANES), bf16)]
        + [jax.ShapeDtypeStruct((HALF, LANES), f32)] * 3,
        compiler_params=params(60),
        name="turn",
        cost_estimate=FREE,
    )(core, own, other, potential.reshape(NODES // BLOCK, BLOCK // LANES, LANES))


def apply_kernel(
    second, core, cells, face, potential,
    index, field, start, matrix, ghosts, edge_mine, edge_other, back,
    kept, sent, edge_kept, edge_sent,
    x, g0, g1, p0, p1, stage, picked, *rest,
):
    accs = rest[:ACCS]
    ahead, behind, sems, slots = rest[ACCS : ACCS + 4], rest[ACCS + 4 : ACCS + 8], rest[-2], rest[-1]
    h = core[0]
    mine = pl.multiple_of(h * HALF, HALF)
    theirs = pl.multiple_of((1 - h) * HALF, HALF)
    load = pltpu.make_async_copy(start, accs[0].at[pl.ds(mine, HALF)], sems.at[0])
    copies = []
    for k in range(NODES // PIECE):
        ref, at = (field[0], k * PIECE) if len(field) == 1 else (field[k // 2], k % 2 * PIECE)
        copies.append(
            pltpu.make_async_copy(
                ref.at[pl.ds(at, PIECE)], stage.at[pl.ds(k * PIECE, PIECE)], sems.at[k + 1]
            )
        )
    for copy in copies:
        copy.start()
    load.start()

    def fetch(stage_number, cell):
        row = cell + 1
        a = pltpu.make_async_copy(index.at[row + 1], ahead[stage_number], slots.at[stage_number])
        b = pltpu.make_async_copy(index.at[row - 1], behind[stage_number], slots.at[4 + stage_number])
        return a, b

    for k in range(4):
        for copy in fetch(k, k):
            copy.start()

    zeros = jnp.zeros((256, LANES), f32)

    def clear(i, _):
        for a in accs[1:]:
            a[pl.ds(pl.multiple_of(i * 256, 256), 256), :] = zeros
        return 0

    lax.fori_loop(0, EXT // 256, clear, 0)

    def clear_first(i, _):
        accs[0][pl.ds(pl.multiple_of(theirs + i * 256, 256), 256), :] = zeros
        return 0

    lax.fori_loop(0, HALF // 256, clear_first, 0)
    accs[0][pl.ds(NODES, FACE), :] = jnp.zeros((FACE, LANES), f32)
    for ref in (x, *accs):
        ref[pl.ds(EXT, SPARE), :] = jnp.zeros((SPARE, LANES), f32)
    for ref in (g0, g1, p0, p1):
        ref[...] = jnp.zeros_like(ref)

    if second:
        for edge, part in ((edge_mine, h), (edge_other, 1 - h)):
            to = pl.multiple_of(NODES + part * HFACE, HFACE)
            x[pl.ds(to, HFACE), :] = edge[pl.ds(0, HFACE), :].astype(f32)
            picked[pl.ds(pl.multiple_of(part * HFACE, HFACE), HFACE), :] = edge[
                pl.ds(HFACE, HFACE), :
            ].astype(f32)
    else:
        first = core[0] == 0
        own, other = ghosts[0][...].astype(f32), ghosts[1][...].astype(f32)
        low, high = jnp.where(first, own, other), jnp.where(first, other, own)
        left = lax.broadcasted_iota(jnp.int32, (HFACE, LANES), 1) < 64
        x[pl.ds(NODES, HFACE), :] = jnp.where(left, low, pltpu.roll(high, 64, 1))
        x[pl.ds(NODES + HFACE, HFACE), :] = jnp.where(left, pltpu.roll(low, 64, 1), high)

    for k, copy in enumerate(copies):
        copy.wait()
        if second:
            base = (mine if k < 2 else theirs) + k % 2 * PIECE
        else:
            base = k * PIECE

        def widen(i, _, k=k, base=base):
            at = pl.multiple_of(k * PIECE + i * 256, 256)
            rows = pl.ds(pl.multiple_of(base + i * 256, 256), 256)
            x[rows, :] = stage[pl.ds(at, 256), :].astype(f32)
            return 0

        lax.fori_loop(0, PIECE // 256, widen, 0)
    load.wait()

    if second:

        def put(i, _):
            for k in range(16):
                at = i * 16 + k
                x[pl.ds(face[at], 1), :] = picked[pl.ds(at, 1), :]
            return 0

        lax.fori_loop(0, FACE // 16, put, 0)

        picked[pl.ds(0, HFACE), :] = back[...].astype(f32)

        def shift(i, _):
            for j in range(0, 16, ACCS):
                at = [i * 16 + j + k for k in range(ACCS)]
                node = [face[h * HFACE + a] for a in at]
                gain = [(potential[n] - 6.0) * 0.25 for n in node]
                sums = [
                    accs[k][pl.ds(node[k], 1), :] + picked[pl.ds(at[k], 1), :] * gain[k]
                    for k in range(ACCS)
                ]
                for k in range(ACCS):
                    accs[k][pl.ds(node[k], 1), :] = sums[k]
            return 0

        lax.fori_loop(0, HFACE // 16, shift, 0)

    def gather(g, nodes, lo, hi):
        for a in range(lo, min(hi, CELL_NODES)):
            g[pl.ds(a, 1), :] = x[pl.ds(nodes[a // LANES, a % LANES], 1), :]

    def scatter(p, nodes, lo, hi):
        for a in range(lo, min(hi, CELL_NODES), 2 * ACCS):
            count = min(2 * ACCS, CELL_NODES - a)
            at = [nodes[(a + k) // LANES, (a + k) % LANES] for k in range(count)]
            held = [accs[k % ACCS][pl.ds(at[k], 1), :] for k in range(count)]
            sums = []
            for k in range(count):
                if k >= ACCS:
                    held[k] = jnp.where(at[k] == at[k - ACCS], sums[k - ACCS], held[k])
                sums.append(held[k] + p[pl.ds(a + k, 1), :])
            for k in range(count):
                accs[k % ACCS][pl.ds(at[k], 1), :] = sums[k]

    def step(k, cell):
        g_now, g_next, p_now, p_last = (g0, g1, p0, p1) if k % 2 == 0 else (g1, g0, p1, p0)
        for copy in fetch(k, cell + k):
            copy.wait()
        p_now[...] = jnp.dot(matrix[...], g_now[...].astype(bf16), preferred_element_type=f32)
        for lo in range(0, CELL_NODES, 8):
            gather(g_next, ahead[k], lo, lo + 8)
            scatter(p_last, behind[k], lo, lo + 8)
        for copy in fetch(k, cell + 4 + k):
            copy.start()

    first = pltpu.make_async_copy(index.at[1], rest[ACCS + 8], slots.at[8])
    first.start()
    first.wait()
    gather(g0, rest[ACCS + 8], 0, CELL_NODES)

    def four(i, _):
        for k in range(4):
            step(k, 4 * i)
        return 0

    fours = (cells[0] + 3) // 4
    lax.fori_loop(0, fours, four, 0)
    for k in range(4):
        for copy in fetch(k, 4 * fours + k):
            copy.wait()
    scatter(p1, behind[0], 0, CELL_NODES)

    def total(begin, count):
        def add(i, _):
            rows = pl.ds(pl.multiple_of(begin + i * 256, 256), 256)
            accs[0][rows, :] = (accs[0][rows, :] + accs[1][rows, :]) + (
                accs[2][rows, :] + accs[3][rows, :]
            )
            return 0

        lax.fori_loop(0, count // 256, add, 0)

    writes = []

    def write(source, target):
        writes.append(pltpu.make_async_copy(source, target, sems.at[len(writes)]))
        writes[-1].start()

    for begin, target in ((theirs, sent), (mine, kept)):
        for at in range(0, HALF, PIECE):
            total(begin + at, PIECE)
            write(
                accs[0].at[pl.ds(pl.multiple_of(begin + at, PIECE), PIECE)],
                target.at[pl.ds(at, PIECE)],
            )
    total(NODES, FACE)

    def pick(i, _):
        for k in range(16):
            at = i * 16 + k
            picked[pl.ds(at, 1), :] = accs[0][pl.ds(face[at], 1), :]
        return 0

    lax.fori_loop(0, FACE // 16, pick, 0)
    for part, target in ((1 - h, edge_sent), (h, edge_kept)):
        ghost = pl.multiple_of(NODES + part * HFACE, HFACE)
        write(accs[0].at[pl.ds(ghost, HFACE)], target.at[pl.ds(0, HFACE)])
        own = pl.multiple_of(part * HFACE, HFACE)
        write(picked.at[pl.ds(own, HFACE)], target.at[pl.ds(HFACE, HFACE)])
    for w in writes:
        w.wait()


def first_kernel(core, cells, face, potential, index, field, start, matrix, own, other, *rest):
    apply_kernel(
        False, core, cells, face, potential, index,
        (field,), start, matrix, (own, other), None, None, None, *rest,
    )


def second_kernel(
    core, cells, face, potential, index, mine, theirs, start, matrix,
    edge_mine, edge_other, back, *rest,
):
    apply_kernel(
        True, core, cells, face, potential, index,
        (mine, theirs), start, matrix, None, edge_mine, edge_other, back, *rest,
    )


def apply(kernel, fields, edges, *operands):
    edge = jax.ShapeDtypeStruct((FACE, LANES), f32)
    half = jax.ShapeDtypeStruct((HALF, LANES), f32)
    return pl.pallas_call(
        kernel,
        in_specs=[SMEM] * 4 + [ANY] * (2 + fields) + [VMEM] * (1 + edges),
        out_specs=[ANY] * 4,
        scratch_shapes=[pltpu.VMEM((EXT + SPARE, LANES), f32)]
        + [pltpu.VMEM((MAT, LANES), f32)] * 4
        + [pltpu.VMEM((NODES, LANES), bf16), pltpu.VMEM((FACE, LANES), f32)]
        + [pltpu.VMEM((EXT + SPARE, LANES), f32)] * ACCS
        + [pltpu.SMEM((8, LANES), jnp.int32)] * 9
        + [pltpu.SemaphoreType.DMA((8,)), pltpu.SemaphoreType.DMA((9,))],
        out_shape=[half, half, edge, edge],
        compiler_params=params(61),
        name="apply",
    )(*operands)


def finish_kernel(core, face, kept, came, back_mine, back_other, mine, theirs, sums, wide):
    def add(i, _):
        rows = pl.ds(pl.multiple_of(i * 256, 256), 256)
        sums[rows, :] = (kept[rows, :] + came[rows, :]) * 0.5
        return 0

    lax.fori_loop(0, HALF // 256, add, 0)
    sums[pl.ds(HALF, SPARE), :] = jnp.zeros((SPARE, LANES), f32)
    base = core[0] * HALF
    for back, part in ((back_mine, core[0]), (back_other, 1 - core[0])):
        wide[...] = back[...].astype(f32)

        def put(i, _, part=part):
            for k in range(8):
                at = i * 8 + k
                node = face[part * HFACE + at] - base
                node = jnp.where((node >= 0) & (node < HALF), node, HALF)
                sums[pl.ds(node, 1), :] += wide[pl.ds(at, 1), :] * 0.5
            return 0

        lax.fori_loop(0, HFACE // 8, put, 0)

    def out(i, _):
        rows = pl.ds(pl.multiple_of(i * 256, 256), 256)
        block = sums[rows, :].T
        mine[:, rows] = jnp.where(core[0] == 0, block[:64], block[64:])
        theirs[:, rows] = jnp.where(core[0] == 0, block[64:], block[:64])
        return 0

    lax.fori_loop(0, HALF // 256, out, 0)


def finish(core, face, kept, came, back_mine, back_other):
    return pl.pallas_call(
        finish_kernel,
        in_specs=[SMEM] * 2 + [VMEM] * 4,
        out_specs=[VMEM] * 2,
        scratch_shapes=[pltpu.VMEM((HALF + SPARE, LANES), f32), pltpu.VMEM((HFACE, LANES), f32)],
        out_shape=[jax.ShapeDtypeStruct((64, HALF), f32)] * 2,
        compiler_params=params(60),
        name="finish",
        cost_estimate=FREE,
    )(core, face, kept, came, back_mine, back_other)


def place_kernel(core, mine, theirs, out):
    out[...] = jnp.where(pl.program_id(0) // (HALF // BLOCK) == core[0], mine[...], theirs[...])


def assemble(core, mine, theirs):
    last = HALF // BLOCK - 1
    return pl.pallas_call(
        place_kernel,
        grid_spec=pltpu.PrefetchScalarGridSpec(
            num_scalar_prefetch=1,
            grid=(NODES // BLOCK,),
            in_specs=[
                pl.BlockSpec((64, BLOCK), lambda i, c: (0, jnp.clip(i - (last + 1) * c[0], 0, last))),
                pl.BlockSpec((64, BLOCK), lambda i, c: (0, jnp.clip(i - (last + 1) * (1 - c[0]), 0, last))),
            ],
            out_specs=pl.BlockSpec((64, BLOCK), lambda i, c: (0, i)),
        ),
        out_shape=jax.ShapeDtypeStruct((64, NODES), f32),
        compiler_params=params(40),
        name="place",
        cost_estimate=FREE,
    )(core, mine, theirs)


def weigh_kernel(place, face, weights, own, out, rows):
    for j in range(SHARE // LANES):
        row = jnp.broadcast_to(own[pl.ds(j, 1), :], (LANES, LANES))
        rows[pl.ds(j * LANES, LANES), :] = row.T
    zero = jnp.zeros((1, LANES), f32)

    def drop(i, _):
        for k in range(8):
            node = face[i * 8 + k] - place[0]
            node = jnp.where((node >= 0) & (node < SHARE), node, SHARE)
            rows[pl.ds(node, 1), :] = zero
        return 0

    lax.fori_loop(0, FACE // 8, drop, 0)
    out[pl.ds(0, SHARE), :] = rows[pl.ds(0, SHARE), :]

    def add(i, _):
        for k in range(8):
            at = i * 8 + k
            out[pl.ds(SHARE + at, 1), :] = jnp.full((1, LANES), weights[face[place[1] + at]], f32)
        return 0

    lax.fori_loop(0, FSHARE // 8, add, 0)


def weigh(place, face, weights, own):
    return pl.pallas_call(
        weigh_kernel,
        in_specs=[SMEM] * 3 + [VMEM],
        out_specs=VMEM,
        scratch_shapes=[pltpu.VMEM((SHARE + SPARE, LANES), f32)],
        out_shape=jax.ShapeDtypeStruct((SHARE + FSHARE, LANES), f32),
        compiler_params=params(60),
        name="weigh",
        cost_estimate=FREE,
    )(place, face, weights, own.reshape(SHARE // LANES, LANES))


def outgoing_kernel(kept, came, edge, back, out):
    out[0, pl.ds(0, SHARE), :] = ((kept[...] + came[...]) * 0.5).astype(bf16)
    out[0, pl.ds(SHARE, FSHARE), :] = ((edge[...] + back[...].astype(f32)) * 0.5).astype(bf16)


def outgoing(kept, came, edge, back):
    nodes = pl.BlockSpec((SHARE, LANES), lambda i: (i, 0))
    faces = pl.BlockSpec((FSHARE, LANES), lambda i: (i, 0))
    return pl.pallas_call(
        outgoing_kernel,
        grid=(8,),
        in_specs=[nodes, nodes, faces, faces],
        out_specs=pl.BlockSpec((1, SHARE + FSHARE, LANES), lambda i: (i, 0, 0)),
        out_shape=jax.ShapeDtypeStruct((8, SHARE + FSHARE, LANES), bf16),
        compiler_params=params(60),
        name="outgoing",
        cost_estimate=FREE,
    )(kept, came, edge, back)


def gram_kernel(nodes, weights, out, everyone):
    for q in range(8):
        lanes = pl.ds(q * LANES, LANES)
        everyone[:, lanes] = nodes[q]

    def rows(q, _):
        at = pl.multiple_of(q * LANES, LANES)
        block = everyone[:, pl.ds(at, LANES)].astype(f32)
        scaled = (weights[...] * block).T.astype(bf16)
        product = jnp.dot(scaled, everyone[...], preferred_element_type=f32)
        out[pl.ds(at, LANES), :] = product.astype(bf16)
        return 0

    lax.fori_loop(0, 8, rows, 0)


def gram_rows(nodes, weights):
    return pl.pallas_call(
        gram_kernel,
        in_specs=[VMEM] * 2,
        out_specs=VMEM,
        scratch_shapes=[pltpu.VMEM((SHARE + FSHARE, 1024), bf16)],
        out_shape=jax.ShapeDtypeStruct((1024, 1024), bf16),
        compiler_params=params(40),
        name="gram",
    )(nodes, weights)


def across_chips(block):
    groups = [list(range(0, 16, 2)), list(range(1, 16, 2))]
    return lax.all_to_all(block, "band", 0, 0, axis_index_groups=groups, tiled=True)


def sum_everywhere(partial, filtered):
    parts = lax.all_to_all(partial.reshape(128, 8, 1024), ("band", "dom"), 0, 0, tiled=True)
    parts, filtered = lax.optimization_barrier((parts, filtered))
    part = jnp.sum(parts.astype(f32), axis=0)
    copies = jnp.broadcast_to(part[None], (8, 8, 1024))
    return filtered, lax.all_to_all(copies, "dom", 0, 0, tiled=True).reshape(64, 1024)


def body(states, cell_matrix, potential, weights, connectivity, face_nodes, cell_counts):
    band = lax.axis_index("band")
    chip = band // 2
    h = band % 2
    core = h.astype(jnp.int32).reshape(1)

    other = to_mate(states)
    own_cells = lax.dynamic_index_in_dim(
        connectivity.reshape(CELL_NODES, CELLS, 2), h, 2, keepdims=False
    )
    cells = (cell_counts - h + 1) // 2
    live = jnp.arange(CELLS) < cells[0]
    index = jnp.where(live[:, None], own_cells.T, EXT)
    index = jnp.pad(index, ((1, ROWS - 1 - CELLS), (0, 1024 - CELL_NODES)), constant_values=EXT)
    index = index.reshape(ROWS, 8, LANES)
    matrix = jnp.pad(cell_matrix, ((0, MAT - CELL_NODES),) * 2)
    faces = own_faces(face_nodes, states)
    ghosts = along_dom(faces, -1)
    ghosts_other = along_dom_crossed(faces, -1)
    field, half, raised, start = turn(core, states, other, potential)
    scalars = (core, cells, face_nodes, potential, index)
    kept, sent, edge_kept, edge_sent = apply(
        first_kernel, 1, 2, *scalars, field, start, matrix, ghosts, ghosts_other
    )
    sent, arrived = lax.optimization_barrier((sent, to_mate(edge_sent)))
    came = to_mate(sent)
    edge = edge_kept + arrived
    rounded = ((kept + came) * 0.25).astype(bf16)
    back = along_dom(edge[:HFACE].astype(bf16), 1)
    ahead = along_dom(edge[HFACE:].astype(bf16), -1)
    theirs = to_mate(rounded)
    kept, came, _ = lax.optimization_barrier((kept, came, rounded))
    start = raised * ((kept + came) * 0.25) - 2.0 * half
    back, ahead, start = lax.optimization_barrier((back, ahead, start))
    inner = (lax.axis_index("dom") < 7).astype(f32)
    edge_mine = jnp.concatenate(
        [(edge[:HFACE] + ahead.astype(f32)) * inner, edge[HFACE:] + back.astype(f32)]
    )
    edge_mine = (edge_mine * 0.25).astype(bf16)
    edge_other = to_mate(edge_mine)
    kept, sent, edge_kept, edge_sent = apply(
        second_kernel, 2, 3, *scalars, rounded, theirs, start, matrix, edge_mine, edge_other, back
    )
    sent, arrived = lax.optimization_barrier((sent, to_mate(edge_sent)))
    came = to_mate(sent)
    edge = edge_kept + arrived
    back = along_dom(edge[:HFACE].astype(bf16), 1)
    everyone = across_chips(outgoing(kept, came, edge[HFACE:], back))
    mine, theirs = finish(core, face_nodes, kept, came, back, to_mate(back))
    begin = h * HALF + chip * SHARE
    place = jnp.stack([begin, h * HFACE + chip * FSHARE]).astype(jnp.int32)
    own = lax.dynamic_slice(weights, (begin,), (SHARE,))
    weight = weigh(place, face_nodes, weights, own)
    everyone, weight, mine, theirs = lax.optimization_barrier((everyone, weight, mine, theirs))
    partial = gram_rows(everyone, weight)
    filtered = assemble(core, mine, to_mate(theirs))
    return sum_everywhere(partial, filtered)


def solution(mesh):
    in_specs = (P("band", "dom"), P(), P("dom"), P("dom"), P(None, "dom"), P("dom"), P("dom"))
    out_specs = (P("band", "dom"), P("band", None))
    return jax.shard_map(body, mesh=mesh, in_specs=in_specs, out_specs=out_specs, check_vma=False)
```
